32 devices in a mesh: group: 4 (over y, x), rep: 8 (over z, core).
Axes of the slice: x: 2, y: 2, z: 4, core: 2. Of those that a mesh axis runs over, the one named last changes fastest.
Arguments:
- hidden_in: bfloat16 [32, 1024, 768], P(('group', 'rep')), may hold values from -6 to 6
- out_grad: bfloat16 [32, 1024, 768], P(('group', 'rep')), may hold values from -6 to 6
- segment_ids: int32 [32, 1024], P(('group', 'rep')), may hold values from 0 to 3, never falling along the last dimension, each value on 1 to 800 neighbouring positions
- rand_blocks: int32 [32, 16, 3], P(('group', 'rep')), may hold values from 0 to 15
- w_qkv: float32 [768, 2304], P('group'), may hold values from -0.21875 to 0.21875
- w_out: float32 [768, 768], P('group'), may hold values from -0.875 to 0.875
- w_in: float32 [768, 3072], P('group'), may hold values from -0.21875 to 0.21875
- w_down: float32 [3072, 768], P('group'), may hold values from -0.109375 to 0.109375
- vec_params: float32 [768, 8], P('group'), may hold values from -0.6 to 1.6, as said below
- bias_hidden: float32 [3072], P('group'), may hold values from -1.5 to 1.5
- moments_qkv: float32 [2, 768, 2304], P(None, 'group'), may hold values from -4 to 4, as said below
- moments_out: float32 [2, 768, 768], P(None, 'group'), may hold values from -4 to 4, as said below
- moments_in: float32 [2, 768, 3072], P(None, 'group'), may hold values from -4 to 4, as said below
- moments_down: float32 [2, 3072, 768], P(None, 'group'), may hold values from -4 to 4, as said below
- moments_vec: float32 [2, 768, 8], P(None, 'group'), may hold values from -4 to 4, as said below
- moments_bias: float32 [2, 3072], P(None, 'group'), may hold values from -4 to 4, as said below
Outputs:
- layer_out: float32 [32, 1024, 768], P(('group', 'rep'))
- grad_in: float32 [32, 1024, 768], P(('group', 'rep'))
- grad_w_qkv: float32 [768, 2304], P('group')
- grad_w_out: float32 [768, 768], P('group')
- grad_w_in: float32 [768, 3072], P('group')
- grad_w_down: float32 [3072, 768], P('group')
- grad_vec: float32 [768, 8], P('group')
- grad_bias: float32 [3072], P('group')
- new_w_qkv: float32 [768, 2304], P('group')
- new_w_out: float32 [768, 768], P('group')
- new_w_in: float32 [768, 3072], P('group')
- new_w_down: float32 [3072, 768], P('group')
- new_vec: float32 [768, 8], P('group')
- new_bias: float32 [3072], P('group')
- new_mom_qkv: float32 [2, 768, 2304], P(None, 'group')
- new_mom_out: float32 [2, 768, 768], P(None, 'group')
- new_mom_in: float32 [2, 768, 3072], P(None, 'group')
- new_mom_down: float32 [2, 3072, 768], P(None, 'group')
- new_mom_vec: float32 [2, 768, 8], P(None, 'group')
- new_mom_bias: float32 [2, 3072], P(None, 'group')
The draws below stay inside these ranges and needn't reach their ends.
Inputs may be any that keep to these rules, and one draw needn't show every extreme that they name: `moments_qkv`: index 0 along the first dimension holds first moments, index 1 second moments, which are 0.5 or more. `moments_out`: like moments_qkv. `moments_in`: like moments_qkv. `moments_down`: like moments_qkv. `moments_vec`: like moments_qkv. `moments_bias`: like moments_qkv. `vec_params`: the two gain columns 3 and 6 lie in 0.4 to 1.6, the others in -0.6 to 0.6.
All inputs are finite; a program needn't handle non-finite values.
Results may differ from the reference program's by a relative error of at most 0.017.
The reference program's roundings to bfloat16 on the way count: a program that leaves them out, or rounds other values in their place, can miss the bound.
Values may be sent and summed in bfloat16 or wider, within the bound.
No kernel may reach another device: no remote copies, remote signals or barrier semaphores. Data moves between devices by JAX's collectives and lax.ppermute only.
A program may use at most 320 MiB of HBM per device.

```python
import math
import jax
import jax.numpy as jnp
import numpy as np
from jax import lax

D = 768
HEAD_DIM = 64
FF = 3072
RAND = 3
STEP = 4
LEN = 1024
SEQS = 32
NB = 16


def moment_pair(key, shape):
    first_m = jnp.clip(jax.random.normal(jax.random.fold_in(key, 1), shape, jnp.float32), -4.0, 4.0)
    second_m = jax.random.uniform(jax.random.fold_in(key, 2), shape, jnp.float32, 0.5, 4.0)
    return jnp.stack([first_m, second_m])


def draw_moments_qkv(key, part):
    key = jax.random.fold_in(key, 11)
    return moment_pair(key, (D, 3 * D))


def draw_moments_out(key, part):
    key = jax.random.fold_in(key, 12)
    return moment_pair(key, (D, D))


def draw_moments_in(key, part):
    key = jax.random.fold_in(key, 13)
    return moment_pair(key, (D, FF))


def draw_moments_down(key, part):
    key = jax.random.fold_in(key, 14)
    return moment_pair(key, (FF, D))


def draw_moments_vec(key, part):
    key = jax.random.fold_in(key, 15)
    return moment_pair(key, (D, 8))


def draw_moments_bias(key, part):
    key = jax.random.fold_in(key, 16)
    return moment_pair(key, (FF,))


def draw_vec_params(key, part):
    key = jax.random.fold_in(key, 17)
    base_vals = jax.random.uniform(key, (D, 8), jnp.float32, -0.6, 0.6)
    column = jnp.arange(8)[None, :]
    gain_lift = ((column == 3) | (column == 6)).astype(jnp.float32)
    return base_vals + gain_lift


def with_ends(values, key, least, top_value):
    place = [jax.random.randint(jax.random.fold_in(key, axis), (), 0, length) for axis, length in enumerate(values.shape)]
    widest = values.shape.index(max(values.shape))
    beside = place[:widest] + [(place[widest] + 1) % values.shape[widest]] + place[widest + 1:]
    return values.at[tuple(place)].set(least).at[tuple(beside)].set(top_value)


def shard_levels(rng, extent, shards, least, top_value):
    gain = 1.0
    for dim, blocks in shards:
        draws = jax.random.uniform(jax.random.fold_in(jax.random.fold_in(rng, 6), dim), (blocks,), jnp.float32, least / len(shards), top_value / len(shards))
        gain = gain * jnp.repeat(jnp.exp(draws), extent[dim] // blocks).reshape((-1,) + (1,) * (len(extent) - 1 - dim))
    return gain


def split_up(count, total, most, lean):
    weights = [(1 << 20) // math.isqrt(standing ** lean) + 1 for standing in range(2, count + 1)]
    surplus, counts = total - most - (count - 1), [1] * (count - 1)
    while surplus > 0:
        free = [i for i in range(count - 1) if counts[i] < most]
        mass, left = sum([weights[i] for i in free]), surplus
        for i in free:
            extra = min(most - counts[i], max(1, left * weights[i] // mass), surplus)
            counts[i] = counts[i] + extra
            surplus = surplus - extra
    return np.array([most] + counts)


def uneven_parts(key, count, total, bound, slope):
    if count == 2:
        one = jax.random.randint(key, (), max(1, total - bound), min(bound, total - 1) + 1)
        return jnp.stack([one, total - one])
    tallies = jnp.asarray(split_up(count, total, bound, slope), jnp.int32)
    pairs = (count - 1) // 2
    donor, sink = tallies[1:1 + 2 * pairs:2], tallies[2:2 + 2 * pairs:2]
    room = jnp.minimum(donor - 1, bound - sink)
    shifted = jax.random.randint(jax.random.fold_in(key, 1), (pairs,), 0, 1 << 20) % (room + 1)
    tallies = tallies.at[1:1 + 2 * pairs:2].set(donor - shifted).at[2:2 + 2 * pairs:2].set(sink + shifted)
    return tallies[jax.random.permutation(jax.random.fold_in(key, 2), count)]


def normal_values(own_key, extent, scale, most, pieces=(), kind=jnp.bfloat16):
    entries = jax.random.normal(own_key, extent, jnp.float32) * scale
    if len(pieces) > 0:
        entries = shard_levels(own_key, extent, pieces, -0.22, 0.18) * entries
    return jnp.clip(entries, min=-most, max=most).astype(kind)


def setup_inputs(seed: int = 0) -> dict:
    streams_of = jax.random.split(jax.random.key(seed), 17)
    hidden_in = normal_values(streams_of[0], (SEQS, LEN, D), 1.0, 6.0, ((0, 32),))
    out_grad = normal_values(streams_of[1], (SEQS, LEN, D), 1.0, 6.0, ((0, 32),))
    segment_ids = jax.vmap(lambda own: jnp.searchsorted(jnp.cumsum(uneven_parts(own, 4, LEN, LEN * 25 // 32, 1)), jnp.arange(LEN), side="right"))(jax.random.split(streams_of[2], SEQS)).reshape((SEQS, LEN)).astype(jnp.int32)
    rand_blocks = with_ends(jax.random.randint(streams_of[3], (SEQS, NB, RAND), 0, NB), jax.random.fold_in(streams_of[3], 1), 0, NB - 1).astype(jnp.int32)
    w_qkv = normal_values(streams_of[4], (D, 3 * D), D ** -0.5, 0.21875, ((0, 4),), jnp.float32)
    w_out = normal_values(streams_of[5], (D, D), (D // 16) ** -0.5, 0.875, ((0, 4),), jnp.float32)
    w_in = normal_values(streams_of[6], (D, FF), D ** -0.5, 0.21875, ((0, 4),), jnp.float32)
    w_down = normal_values(streams_of[7], (FF, D), FF ** -0.5, 0.109375, ((0, 4),), jnp.float32)
    vec_params = draw_vec_params(jax.random.fold_in(streams_of[16], 71), 0)
    bias_hidden = normal_values(streams_of[9], (FF,), 0.3, 1.5, ((0, 4),), jnp.float32)
    moments_qkv = draw_moments_qkv(jax.random.fold_in(streams_of[16], 71), 0)
    moments_out = draw_moments_out(jax.random.fold_in(streams_of[16], 71), 0)
    moments_in = draw_moments_in(jax.random.fold_in(streams_of[16], 71), 0)
    moments_down = draw_moments_down(jax.random.fold_in(streams_of[16], 71), 0)
    moments_vec = draw_moments_vec(jax.random.fold_in(streams_of[16], 71), 0)
    moments_bias = draw_moments_bias(jax.random.fold_in(streams_of[16], 71), 0)
    return {"hidden_in": hidden_in, "out_grad": out_grad, "segment_ids": segment_ids, "rand_blocks": rand_blocks, "w_qkv": w_qkv, "w_out": w_out, "w_in": w_in, "w_down": w_down, "vec_params": vec_params, "bias_hidden": bias_hidden, "moments_qkv": moments_qkv, "moments_out": moments_out, "moments_in": moments_in, "moments_down": moments_down, "moments_vec": moments_vec, "moments_bias": moments_bias}


@jax.custom_vjp
def low(v):
    return lax.optimization_barrier(v.astype(jnp.bfloat16)).astype(jnp.float32)

@jax.custom_vjp
def low_back(v):
    return v

def low_keep(v):
    return (low(v), None)

def low_pass(kept, grad):
    return (grad,)

def back_keep(v):
    return (v, None)

def back_low(kept, grad):
    return (low(grad),)
low.defvjp(low_keep, low_pass)
low_back.defvjp(back_keep, back_low)
highest = lax.Precision.HIGHEST
norm_eps = 1e-05
adam_eps = 1e-08
matrix_decay = 0.1
step_rate = 0.1
masked_score = -1e+30

def both_ways(tensor):
    return low(low_back(tensor))

def attend_mask(segments, randoms):
    blocks = randoms.shape[0]
    block_len = segments.shape[0] // blocks
    block_ids = jnp.arange(blocks)
    nearby = jnp.abs(block_ids[:, None] - block_ids[None, :]) <= 1
    edge_row = (block_ids == 0) | (block_ids == blocks - 1)
    picked = jnp.any(randoms[:, :, None] == block_ids[None, None, :], axis=1)
    allowed = nearby | edge_row[:, None] | edge_row[None, :] | picked
    tokens = jnp.repeat(jnp.repeat(allowed, block_len, axis=0), block_len, axis=1)
    return tokens & (segments[:, None] == segments[None, :])

def layer_norm(residual, gain_vec, shift_vec):
    center = residual - lax.optimization_barrier(jnp.mean(residual, axis=-1, keepdims=True))
    spread = lax.optimization_barrier(jnp.mean(center * center, axis=-1, keepdims=True))
    return center * lax.rsqrt(spread + norm_eps) * gain_vec + shift_vec

def forward(inputs, mask_all, params):
    w_qkv, w_out, w_in, w_down, vec_params, bias_hidden = [low(tensor) for tensor in params]
    bias_q, bias_v, bias_o, gain_one, shift_one, bias_d, gain_two, shift_two = [vec_params[:, column] for column in range(8)]
    seq_count, seq_len, feat_width = inputs.shape
    head_count = feat_width // HEAD_DIM
    split = (seq_count, seq_len, head_count, HEAD_DIM)
    qkv_rows = jnp.einsum('bld,de->ble', inputs, w_qkv, precision=highest)
    query_vectors = both_ways(qkv_rows[..., :feat_width] + bias_q).reshape(split)
    key_matrix_rows = both_ways(qkv_rows[..., feat_width:2 * feat_width]).reshape(split)
    value_vectors = both_ways(qkv_rows[..., 2 * feat_width:] + bias_v).reshape(split)
    scores = low_back(jnp.einsum('blhd,bmhd->bhlm', query_vectors, key_matrix_rows, precision=highest) * HEAD_DIM ** (-0.5))
    scores = jnp.where(mask_all[:, None], scores, masked_score)
    attention_weights_soft = low(jax.nn.softmax(scores, axis=-1))
    attended = jnp.einsum('bhlm,bmhd->blhd', attention_weights_soft, value_vectors, precision=highest)
    attended = both_ways(attended.reshape(seq_count, seq_len, feat_width))
    branch = low_back(jnp.einsum('bld,de->ble', attended, w_out, precision=highest)) + bias_o
    norm_one = layer_norm(inputs + branch, gain_one, shift_one)
    hidden = low_back(jnp.einsum('bld,df->blf', low(norm_one), w_in, precision=highest) + bias_hidden)
    active = low(jax.nn.gelu(hidden, approximate=False))
    output = low_back(jnp.einsum('blf,fd->bld', active, w_down, precision=highest)) + bias_d
    return layer_norm(norm_one + output, gain_two, shift_two)

def adam_step(weight, moment, gradient, decay, correct, rate):
    first_m = 0.5 * moment[0] + 0.5 * gradient
    second_m = 0.5 * moment[1] + 0.5 * gradient * gradient
    update = first_m / correct / (jnp.sqrt(second_m / correct) + adam_eps) + decay * weight
    return (weight - rate * update, jnp.stack([first_m, second_m]))

def reference(hidden_in, out_grad, segment_ids, rand_blocks, w_qkv, w_out, w_in, w_down, vec_params, bias_hidden, moments_qkv, moments_out, moments_in, moments_down, moments_vec, moments_bias):
    params = (w_qkv, w_out, w_in, w_down, vec_params, bias_hidden)
    group_len = 4
    inputs = hidden_in.astype(jnp.float32).reshape(SEQS // group_len, group_len, LEN, D)
    cotangent = out_grad.astype(jnp.float32).reshape(SEQS // group_len, group_len, LEN, D)
    segments = segment_ids.reshape(SEQS // group_len, group_len, LEN)
    randoms = rand_blocks.reshape(SEQS // group_len, group_len, NB, RAND)

    def one_group(totals, item_in):
        inputs_grp, cot_grp, seg_grp, rand_grp = item_in
        mask_all = jax.vmap(attend_mask)(seg_grp, rand_grp)
        result, pullback = jax.vjp(lambda inner_x, weights: forward(inner_x, mask_all, weights), inputs_grp, params)
        grad_inputs, grad_params = pullback(cot_grp)
        totals = tuple((running + addend for running, addend in zip(totals, grad_params)))
        return (totals, (result, grad_inputs))
    zero_grads = tuple((jnp.zeros(tensor.shape, jnp.float32) for tensor in params))
    summed, (outs_y, outs_dx) = lax.scan(one_group, zero_grads, (inputs, cotangent, segments, randoms))
    inverse_count = 1.0 / SEQS
    grads = tuple((total * inverse_count for total in summed))
    layer_out = outs_y.reshape(SEQS, LEN, D)
    grad_in = outs_dx.reshape(SEQS, LEN, D)
    correct = 1.0 - 0.5 ** STEP
    rate = step_rate
    moments = (moments_qkv, moments_out, moments_in, moments_down, moments_vec, moments_bias)
    decays = (matrix_decay, matrix_decay, matrix_decay, matrix_decay, 0.0, 0.0)
    updated = [adam_step(tensor, moment, gradient, decay, correct, rate) for tensor, moment, gradient, decay in zip(params, moments, grads, decays)]
    return (layer_out, grad_in, grads[0], grads[1], grads[2], grads[3], grads[4], grads[5], updated[0][0], updated[1][0], updated[2][0], updated[3][0], updated[4][0], updated[5][0], updated[0][1], updated[1][1], updated[2][1], updated[3][1], updated[4][1], updated[5][1])
```

```python
import jax
import jax.numpy as jnp
from jax import lax
from jax.experimental import pallas as pl
from jax.experimental.pallas import tpu as pltpu
from jax.sharding import PartitionSpec as P

HEAD_DIM = 64
STEP = 4
norm_eps = 1e-05
adam_eps = 1e-08
matrix_decay = 0.1
step_rate = 0.1
BF = jnp.bfloat16
F32 = jnp.float32
I32 = jnp.int32
VM = 56 * 1024 * 1024
NEG = -1e30
PAIR = 2 * HEAD_DIM
SQH = 0.7071067811865476
PHI0 = 0.3989422804014327
AX = ("group", "rep")
ANY = pl.BlockSpec(memory_space=pl.ANY)
SMEM = pl.BlockSpec(memory_space=pltpu.SMEM)
VMEM = pl.BlockSpec(memory_space=pltpu.VMEM)
sds = jax.ShapeDtypeStruct


def cost(flops, nbytes, trans=0):
    return pl.CostEstimate(flops=int(flops), bytes_accessed=int(nbytes), transcendentals=int(trans))


def params(**kw):
    return pltpu.CompilerParams(vmem_limit_bytes=VM, **kw)

def nt(a, b):
    return lax.dot_general(a, b, (((1,), (1,)), ((), ())), preferred_element_type=F32)


def nn(a, b):
    return lax.dot_general(a, b, (((1,), (0,)), ((), ())), preferred_element_type=F32)


def tn(a, b):
    return lax.dot_general(a, b, (((0,), (0,)), ((), ())), preferred_element_type=F32)


def split3(v):
    hi = v.astype(BF).astype(F32)
    mid = (v - hi).astype(BF).astype(F32)
    return hi, mid, v - hi - mid


def attn_feats(seg_ref, rand_ref, fq_s, fk_s, nb):
    n = fq_s.shape[0]
    bl = n // nb
    lane = lax.broadcasted_iota(jnp.int32, (n, PAIR), 1) % HEAD_DIM
    blk = lax.broadcasted_iota(jnp.int32, (n, PAIR), 0) // bl
    seg = seg_ref[...]
    fq = (lane == blk) | ((lane >= nb) & (lane - nb == seg))
    fq_s[...] = jnp.where(fq, 1.0, 0.0).astype(BF)
    allow = (jnp.abs(lane - blk) <= 1) | (lane == 0) | (lane == nb - 1) | (blk == 0) | (blk == nb - 1)
    for j in range(rand_ref.shape[0]):
        allow = allow | (rand_ref[j : j + 1, :] == blk)
    bad = ((lane < nb) & jnp.logical_not(allow)) | ((lane >= nb) & (lane < nb + 4) & (lane - nb != seg))
    off = (lane >= nb + 4) & (lane < nb + 7)
    fk_s[...] = jnp.where(bad, NEG, jnp.where(off, -1.0, 0.0)).astype(BF)


def attn_fwd_kernel(nb, seg_ref, rand_ref, q_ref, k_ref, v_ref, o_ref, f_ref, fq_s, fk_s):
    @pl.when(pl.program_id(0) == 0)
    def _():
        attn_feats(seg_ref, rand_ref, fq_s, fk_s, nb)

    n = q_ref.shape[0]
    t = 256
    low1 = lax.broadcasted_iota(jnp.int32, (n, PAIR), 1) < HEAD_DIM
    k = k_ref[...]
    v = v_ref[...]
    fk = fk_s[...]
    one = jnp.ones((n, PAIR), BF)
    ks = (jnp.where(low1, k, fk), jnp.where(low1, fk, k))
    vs = (jnp.where(low1, v, one), jnp.where(low1, one, v))
    lowt = lax.broadcasted_iota(jnp.int32, (t, PAIR), 1) < HEAD_DIM
    lane = lax.broadcasted_iota(jnp.int32, (t, PAIR), 1) % HEAD_DIM
    for i in range(n // t):
        rows = pl.ds(i * t, t)
        q = q_ref[rows, :] * jnp.asarray(HEAD_DIM**-0.5, BF)
        fq = fq_s[rows, :]
        acc, top = [], []
        for h in range(2):
            qh = jnp.where(lowt, q, fq) if h == 0 else jnp.where(lowt, fq, q)
            s = nt(qh, ks[h])
            m = jnp.max(s, axis=-1, keepdims=True)
            p = jnp.exp(s - m).astype(BF)
            acc.append(nn(p, vs[h]))
            top.append(m)
        lsw = jnp.where(lowt, acc[1], acc[0])
        o = jnp.where(lowt, acc[0], acc[1]) / pltpu.roll(lsw, HEAD_DIM, 1)
        o_ref[rows, :] = o.astype(BF)
        hi, mid, lo = split3(jnp.where(lowt, top[1], top[0]) + jnp.log(lsw))
        f = jnp.where(lane == nb + 4, hi, jnp.where(lane == nb + 5, mid, lo))
        f_ref[rows, :] = jnp.where((lane >= nb + 4) & (lane < nb + 7), f.astype(BF), fq)


def attn_fwd(qkv, seg_col, rand_rows, nb):
    n, w3 = qkv.shape
    w = w3 // 3
    pairs = w // PAIR
    blk = lambda off: pl.BlockSpec((n, PAIR), lambda p, off=off: (0, p + off))
    full = lambda a: pl.BlockSpec(a.shape, lambda p: (0, 0))
    return pl.pallas_call(
        lambda *refs: attn_fwd_kernel(nb, *refs),
        grid=(pairs,),
        in_specs=[full(seg_col), full(rand_rows), blk(0), blk(pairs), blk(2 * pairs)],
        out_specs=[blk(0), blk(0)],
        out_shape=[jax.ShapeDtypeStruct((n, w), BF)] * 2,
        scratch_shapes=[pltpu.VMEM((n, PAIR), BF)] * 2,
        compiler_params=pltpu.CompilerParams(vmem_limit_bytes=VM),
        name="attn_fwd",
    )(seg_col, rand_rows, qkv, qkv, qkv)


def attn_bwd_kernel(nb, seg_ref, rand_ref, q_ref, k_ref, v_ref, f_ref, o_ref, do_ref, dq_ref, dk_ref, dv_ref, bias_ref, fq_s, fk_s):
    @pl.when(pl.program_id(0) == 0)
    def _():
        attn_feats(seg_ref, rand_ref, fq_s, fk_s, nb)

    n = q_ref.shape[0]
    t = 256
    low1 = lax.broadcasted_iota(jnp.int32, (n, PAIR), 1) < HEAD_DIM
    lane = lax.broadcasted_iota(jnp.int32, (n, PAIR), 1) % HEAD_DIM
    scale = jnp.asarray(HEAD_DIM**-0.5, BF)
    q = q_ref[...] * scale
    f = f_ref[...]
    do = do_ref[...]
    prod = do.astype(F32) * o_ref[...].astype(F32)
    d0 = jnp.sum(jnp.where(low1, prod, 0.0), axis=-1, keepdims=True)
    d1 = jnp.sum(jnp.where(low1, 0.0, prod), axis=-1, keepdims=True)
    hi, mid, lo = split3(jnp.where(low1, d1, d0))
    fd = jnp.where(lane == nb + 4, hi, jnp.where(lane == nb + 5, mid, jnp.where(lane == nb + 6, lo, 0.0))).astype(BF)
    qs = (jnp.where(low1, q, f), jnp.where(low1, f, q))
    dos = (jnp.where(low1, do, fd), jnp.where(low1, fd, do))
    kT = jnp.transpose(k_ref[...] * scale)
    lowt = lax.broadcasted_iota(jnp.int32, (t, PAIR), 1) < HEAD_DIM
    dqT = [None, None]
    dv_sum = jnp.zeros((1, PAIR), F32)
    for i in range(n // t):
        rows = pl.ds(i * t, t)
        k = k_ref[rows, :]
        v = v_ref[rows, :]
        fk = fk_s[rows, :]
        fv = jnp.where(fk == -1.0, fk, jnp.zeros_like(fk))
        dvh, dkh = [], []
        for h in range(2):
            kh = jnp.where(lowt, k, fk) if h == 0 else jnp.where(lowt, fk, k)
            vh = jnp.where(lowt, v, fv) if h == 0 else jnp.where(lowt, fv, v)
            p = jnp.exp(nt(kh, qs[h]))
            ds = (p * nt(vh, dos[h])).astype(BF)
            dvh.append(nn(p.astype(BF), do))
            dkh.append(nn(ds, q))
            part = nn(kT[h * HEAD_DIM : (h + 1) * HEAD_DIM, i * t : (i + 1) * t], ds)
            dqT[h] = part if dqT[h] is None else dqT[h] + part
        dk_ref[rows, :] = jnp.where(lowt, dkh[0], dkh[1]).astype(BF)
        dv = jnp.where(lowt, dvh[0], dvh[1]).astype(BF)
        dv_ref[rows, :] = dv
        dv_sum = dv_sum + jnp.sum(dv.astype(F32), axis=0, keepdims=True)
    dq = jnp.transpose(jnp.concatenate(dqT, axis=0)).astype(BF)
    dq_ref[...] = dq
    bias_ref[...] = jnp.concatenate([jnp.sum(dq.astype(F32), axis=0, keepdims=True), dv_sum, jnp.zeros((6, PAIR), F32)], axis=0)


def attn_bwd(qkv, f, o, do, seg_col, rand_rows, nb):
    n, w3 = qkv.shape
    w = w3 // 3
    pairs = w // PAIR
    blk = lambda off: pl.BlockSpec((n, PAIR), lambda p, off=off: (0, p + off))
    full = lambda a: pl.BlockSpec(a.shape, lambda p: (0, 0))
    return pl.pallas_call(
        lambda *refs: attn_bwd_kernel(nb, *refs),
        grid=(pairs,),
        in_specs=[full(seg_col), full(rand_rows), blk(0), blk(pairs), blk(2 * pairs), blk(0), blk(0), blk(0)],
        out_specs=[blk(0), blk(0), blk(0), pl.BlockSpec((8, PAIR), lambda p: (0, p))],
        out_shape=[jax.ShapeDtypeStruct((n, w), BF)] * 3 + [jax.ShapeDtypeStruct((8, w), F32)],
        scratch_shapes=[pltpu.VMEM((n, PAIR), BF)] * 2,
        compiler_params=pltpu.CompilerParams(vmem_limit_bytes=VM),
        name="attn_bwd",
    )(seg_col, rand_rows, qkv, qkv, qkv, f, o, do)


def norm(r, g, c):
    w = r.shape[-1]
    center = r - jnp.sum(r, axis=-1, keepdims=True) * (1.0 / w)
    inv = lax.rsqrt(jnp.sum(center * center, axis=-1, keepdims=True) * (1.0 / w) + norm_eps)
    n = center * inv
    return n * g + c, n, inv


def norm_back(dy, g, n, inv):
    w = dy.shape[-1]
    e = dy * g
    a = jnp.sum(e, axis=-1, keepdims=True) * (1.0 / w)
    b = jnp.sum(e * n, axis=-1, keepdims=True) * (1.0 / w)
    return inv * (e - a - n * b)


def colsum(a):
    return jnp.sum(a, axis=0, keepdims=True)


def pack_a(where, w, vec_t, bias):
    rows, cols = w.shape
    half = rows // 2

    def kern(where_ref, w_ref, vec_ref, bias_ref, out_ref):
        for h in range(2):
            pos = h ^ where_ref[1]
            out_ref[pos, 0:half, :] = w_ref[h * half : (h + 1) * half, :].astype(BF)
            small = vec_ref[...] if h == 0 else bias_ref[...]
            small = jnp.concatenate([small, jnp.zeros((small.shape[0], cols - small.shape[1]), F32)], axis=1)
            out_ref[pos, half : half + 16, :] = jnp.concatenate([small, small], axis=0).astype(BF)

    return pl.pallas_call(
        kern,
        in_specs=[SMEM, VMEM, VMEM, VMEM],
        out_specs=VMEM,
        out_shape=sds((2, half + 16, cols), BF),
        compiler_params=params(),
        cost_estimate=cost(0, 3 * w.size * 2),
        name="pack_a",
    )(where, w, vec_t, bias)


def pack_b(where, wo, wi, wd):
    rows, w = wo.shape
    half = rows // 2
    nf = wi.shape[1] // w
    nd = wd.shape[0] // rows

    def kern(where_ref, wo_ref, wi_ref, wd_ref, out_ref):
        for h in range(2):
            pos = h ^ where_ref[1]
            hs = slice(h * half, (h + 1) * half)
            out_ref[pos, 0] = wo_ref[hs, :].astype(BF)
            for j in range(nf):
                out_ref[pos, 1 + j] = wi_ref[hs, j * w : (j + 1) * w].astype(BF)
            for j in range(nd):
                at = (h * nd + j) * half
                out_ref[pos, 1 + nf + j] = wd_ref[at : at + half, :].astype(BF)

    return pl.pallas_call(
        kern,
        in_specs=[SMEM, VMEM, VMEM, VMEM],
        out_specs=VMEM,
        out_shape=sds((2, 1 + nf + nd, half, w), BF),
        compiler_params=params(),
        cost_estimate=cost(0, 6 * (wo.size + wi.size + wd.size)),
        name="pack_b",
    )(where, wo, wi, wd)


def pperm(a, pairs):
    return lax.ppermute(a, AX, pairs)


def gather(pack, perms):
    near = pperm(pack, perms["s1"])
    side = pperm(near, perms["core"])
    far = pperm(near[0:1], perms["s2"])
    back = pperm(far, perms["core"])
    return pack, near, side, far, back


def piece_refs(refs):
    own, near, side, far, back = refs
    return [own.at[0], own.at[1], near.at[0], near.at[1], side.at[0], side.at[1], far.at[0], back.at[0]]


def project(x, table, parts, groups, t=256):
    n, d = x.shape
    _, hp, cols = parts[0].shape
    half = hp - 16
    share = 2 * half

    def kern(tab_ref, x_ref, *refs):
        pieces = piece_refs(refs[:5])
        qkv_ref, w_out, vec_ref, bias_ref, w_s, e_s, sems, osem = refs[5:]
        first = pl.program_id(0) == 0
        last = pl.program_id(0) == pl.num_programs(0) - 1

        def copies():
            out = []
            for i, p in enumerate(pieces):
                u = tab_ref[i]
                out.append(pltpu.make_async_copy(p.at[pl.ds(0, half)], w_s.at[pl.ds(pl.multiple_of(u * half, 16), half)], sems.at[2 * i]))
                out.append(pltpu.make_async_copy(p.at[pl.ds(half, 16)], e_s.at[u], sems.at[2 * i + 1]))
            return out

        def whole():
            return pltpu.make_async_copy(w_s, w_out, osem)

        @pl.when(first)
        def _():
            for cp in copies():
                cp.start()
            for cp in copies():
                cp.wait()
            whole().start()
            vec_ref[...] = jnp.concatenate([e_s[2 * g, 0:8, 0:share].astype(F32) for g in range(groups)], axis=1)
            for g in range(groups):
                bias_ref[g] = e_s[2 * g + 1, 0:8, 0:d].astype(F32)

        qb = jnp.concatenate([vec_ref[0:1, :], jnp.zeros((1, d), F32), vec_ref[1:2, :]], axis=1)
        qkv_ref[...] = (nn(x_ref[...], w_s[...]) + qb).astype(BF)

        @pl.when(last)
        def _():
            whole().wait()

    return pl.pallas_call(
        kern,
        grid=(n // t,),
        in_specs=[SMEM, pl.BlockSpec((t, d), lambda i: (i, 0))] + [ANY] * 5,
        out_specs=[pl.BlockSpec((t, cols), lambda i: (i, 0)), ANY, pl.BlockSpec((8, d), lambda i: (0, 0)), pl.BlockSpec((groups, 8, d), lambda i: (0, 0, 0))],
        out_shape=[sds((n, cols), BF), sds((d, cols), BF), sds((8, d), F32), sds((groups, 8, d), F32)],
        scratch_shapes=[pltpu.VMEM((d, cols), BF), pltpu.VMEM((2 * groups, 16, cols), BF), pltpu.SemaphoreType.DMA((16,)), pltpu.SemaphoreType.DMA],
        compiler_params=params(),
        cost_estimate=cost(2 * n * d * cols, 2 * (n * d + 2 * d * cols + n * cols)),
        name="project",
    )(table, x, *parts)


def token(x, dy, o, vec, bias, table, parts, t=256):
    n, w = x.shape
    _, k9, half, _ = parts[0].shape
    nf = bias.shape[0]
    nd = k9 - 1 - nf
    ff = nf * w

    def kern(tab_ref, x_ref, dy_ref, o_ref, vec_ref, bias_ref, *refs):
        pieces = piece_refs(refs[:5])
        (y_ref, dr1_ref, hb_ref, dh_ref, x1b_ref, dfb_ref, dab_ref, do_ref, vs_ref, bs_ref, wo_s, wi_s, wd_s, sems) = refs[5:]
        first = pl.program_id(0) == 0

        def copies(kind):
            out = []
            for i, p in enumerate(pieces):
                u = tab_ref[i]
                rows = pl.ds(pl.multiple_of(u * half, 16), half)
                if kind == 0:
                    out.append(pltpu.make_async_copy(p.at[0], wo_s.at[rows], sems.at[0, i]))
                elif kind == 1:
                    out.append(pltpu.make_async_copy(p.at[pl.ds(1, nf)], wi_s.at[:, rows], sems.at[1, i]))
                else:
                    out.append(pltpu.make_async_copy(p.at[pl.ds(1 + nf, nd)], wd_s.at[pl.ds(u * nd, nd)], sems.at[2, i]))
            return out

        @pl.when(first)
        def _():
            for kind in range(3):
                for cp in copies(kind):
                    cp.start()
            for kind in range(3):
                for cp in copies(kind):
                    cp.wait()

        row = lambda j: vec_ref[j : j + 1, :]
        bo, g1, c1, bd, g2, c2 = [row(j) for j in range(2, 8)]
        per = wd_s.shape[0] // nf
        down = lambda j: wd_s[j * per : (j + 1) * per].reshape(w, w)
        xf = x_ref[...].astype(F32)
        x1, n1, inv1 = norm(xf + (nn(o_ref[...], wo_s[...]) + bo), g1, c1)
        x1b = x1.astype(BF)
        x1b_ref[...] = x1b
        back = None
        slopes = []
        for j in range(nf):
            cols = slice(j * w, (j + 1) * w)
            h = nn(x1b, wi_s[j]) + bias_ref[j, 0:1, :]
            cdf = 0.5 * (1.0 + lax.erf(h * SQH))
            hb = (h * cdf).astype(BF)
            slopes.append(cdf + h * (jnp.exp(-0.5 * (h * h)) * PHI0))
            hb_ref[:, cols] = hb
            part = nn(hb, down(j))
            back = part if back is None else back + part
        y, n2, inv2 = norm(x1 + (back + bd), g2, c2)
        y_ref[...] = y
        dyf = dy_ref[...].astype(F32)
        dr2 = norm_back(dyf, g2, n2, inv2)
        dfb = dr2.astype(BF)
        dfb_ref[...] = dfb
        dx1 = dr2
        bsum = []
        for j in range(nf):
            cols = slice(j * w, (j + 1) * w)
            dh = (nt(dfb, down(j)) * slopes[j]).astype(BF)
            dh_ref[:, cols] = dh
            bsum.append(colsum(dh.astype(F32)))
            dx1 = dx1 + nt(dh, wi_s[j])
        dr1 = norm_back(dx1, g1, n1, inv1)
        dr1_ref[...] = dr1
        dab = dr1.astype(BF)
        dab_ref[...] = dab
        do_ref[...] = nt(dab, wo_s[...]).astype(BF)
        zero = jnp.zeros((2, w), F32)
        vsum = jnp.concatenate([zero, colsum(dr1), colsum(dx1 * n1), colsum(dx1), colsum(dr2), colsum(dyf * n2), colsum(dyf)], axis=0)
        bsum = jnp.concatenate(bsum + [jnp.zeros((8 - nf, w), F32)], axis=0)
        vs_ref[...] = vsum + jnp.where(first, 0.0, vs_ref[...])
        bs_ref[...] = bsum + jnp.where(first, 0.0, bs_ref[...])

    rows = lambda c: pl.BlockSpec((t, c), lambda i: (i, 0))
    full = lambda s: pl.BlockSpec(s, lambda i: (0,) * len(s))
    return pl.pallas_call(
        kern,
        grid=(n // t,),
        in_specs=[SMEM, rows(w), rows(w), rows(w), full(vec.shape), full(bias.shape)] + [ANY] * 5,
        out_specs=[rows(w), rows(w), rows(ff), rows(ff), rows(w), rows(w), rows(w), rows(w), full((8, w)), full((8, w))],
        out_shape=[sds((n, w), F32), sds((n, w), F32), sds((n, ff), BF), sds((n, ff), BF)] + [sds((n, w), BF)] * 4 + [sds((8, w), F32), sds((8, w), F32)],
        scratch_shapes=[pltpu.VMEM((w, w), BF), pltpu.VMEM((nf, w, w), BF), pltpu.VMEM((ff // half, half, w), BF), pltpu.SemaphoreType.DMA((3, 8))],
        compiler_params=params(),
        cost_estimate=cost(2 * n * w * (2 * w + 4 * ff), 2 * (n * (9 * w + 2 * ff) + w * (w + 2 * ff)), 2 * n * ff),
        name="token",
    )(table, x, dy, o, vec, bias, *parts)


def grad_down(order, half, hb, dfb, groups, quarters):
    n, ff = hb.shape
    w = dfb.shape[1]
    share = ff // groups
    hr = share // 2
    rb = hr // quarters

    def kern(order_ref, half_ref, hb_ref, dfb_ref, out_ref):
        g = pl.program_id(0)
        r = tn(hb_ref[...], dfb_ref[...])
        for q in range(quarters):
            out_ref[order_ref[g * quarters + q]] = r[q * rb : (q + 1) * rb].astype(BF)

    return pl.pallas_call(
        kern,
        grid_spec=pltpu.PrefetchScalarGridSpec(
            num_scalar_prefetch=2,
            grid=(groups,),
            in_specs=[pl.BlockSpec((n, hr), lambda g, o, h: (0, 2 * g + h[0])), pl.BlockSpec((n, w), lambda g, o, h: (0, 0))],
            out_specs=pl.BlockSpec((groups * quarters, rb, w), lambda g, o, h: (0, 0, 0)),
        ),
        out_shape=sds((groups * quarters, rb, w), BF),
        compiler_params=params(),
        cost_estimate=cost(n * ff * w, 2 * (n * ff // 2 + n * w + ff * w // 2)),
        name="grad_down",
    )(order, half, hb, dfb)


def grad_cols(order, half, pairs, blocks, small, name):
    n, d = pairs[0][0].shape
    rb = d // blocks
    widths = [b.shape[1] // 2 for _, b in pairs]
    unit = min(widths)
    pieces = sum(widths) // unit
    rows = pieces * rb + (0 if small is None else 16)
    lefts = []
    for a, _ in pairs:
        if not any(a is b for b in lefts):
            lefts.append(a)
    where = [next(i for i, l in enumerate(lefts) if l is a) for a, _ in pairs]

    def kern(order_ref, half_ref, *refs):
        a_refs, b_refs, rest = refs[: len(lefts)], refs[len(lefts) : len(lefts) + len(pairs)], refs[len(lefts) + len(pairs) :]
        out_ref = rest[-1]
        at = 0
        for i in range(len(pairs)):
            r = tn(a_refs[where[i]][...], b_refs[i][...]).astype(BF)
            for j in range(widths[i] // unit):
                for k in range(blocks):
                    out_ref[order_ref[k], at : at + rb, :] = r[k * rb : (k + 1) * rb, j * unit : (j + 1) * unit]
                at += rb
        if small is not None:
            for k in range(blocks):
                row = rest[0][k, pl.ds(half_ref[0], 1), :]
                out_ref[order_ref[k], at : at + 16, :] = jnp.broadcast_to(row, (16, unit)).astype(BF)

    full = lambda s: pl.BlockSpec(s, lambda i, o, h: (0,) * len(s))
    out = (blocks, rows, unit)
    extra = [] if small is None else [small]
    return pl.pallas_call(
        kern,
        grid_spec=pltpu.PrefetchScalarGridSpec(
            num_scalar_prefetch=2,
            grid=(1,),
            in_specs=[full(a.shape) for a in lefts]
            + [pl.BlockSpec((n, wd), lambda i, o, h: (0, h[0])) for wd in widths]
            + [full(s.shape) for s in extra],
            out_specs=full(out),
        ),
        out_shape=sds(out, BF),
        compiler_params=params(),
        cost_estimate=cost(2 * n * d * sum(widths), 2 * (n * d + n * sum(widths) + d * sum(widths))),
        name=name,
    )(order, half, *lefts, *[b for _, b in pairs], *extra)


def grad_input(dr1, dq, dk, dv, w, t=256):
    n, d = dr1.shape

    def kern(r_ref, q_ref, k_ref, v_ref, w_ref, out_ref):
        out_ref[...] = r_ref[...] + nt(q_ref[...], w_ref[:, 0:d]) + nt(k_ref[...], w_ref[:, d : 2 * d]) + nt(v_ref[...], w_ref[:, 2 * d : 3 * d])

    rows = pl.BlockSpec((t, d), lambda i: (i, 0))
    return pl.pallas_call(
        kern,
        grid=(n // t,),
        in_specs=[rows] * 4 + [pl.BlockSpec(w.shape, lambda i: (0, 0))],
        out_specs=rows,
        out_shape=sds((n, d), F32),
        compiler_params=params(),
        cost_estimate=cost(6 * n * d * d, n * d * 14 + 2 * w.size),
        name="grad_input",
    )(dr1, dq, dk, dv, w)


def total(*terms):
    out = terms[0].astype(F32)
    for a in terms[1:]:
        out = out + a.astype(F32)
    return out.astype(BF)


def reduce_all(send, keep, perms):
    nb = keep.shape[0]
    a, b = nb // 2, nb // 4
    got = pperm(send, perms["core"])
    x1 = pperm(total(keep[a:], got[a:]), perms["s1"])
    x2 = pperm(total(keep[b:a], got[b:a], x1[b:]), perms["s2"])
    k, g, x = keep[:b], got[:b], x1[:b]
    m, e = b // 2, b // 4
    z1 = pperm(total(k[m:], g[m:], x[m:], x2[m:]), perms["z1"])
    z2 = pperm(total(k[e:m], g[e:m], x[e:m], x2[e:m], z1[e:]), perms["z2"])
    t0 = total(k[:e], g[:e], x[:e], x2[:e], z1[:e], z2)
    for extra in perms["far"]:
        t0 = total(t0, pperm(t0, extra))
    t1 = pperm(t0, perms["z2"])
    t01 = jnp.concatenate([t0, t1], axis=0)
    t23 = pperm(t01, perms["z1"])
    return t01, t23, pperm(t01, perms["core"]), pperm(t23, perms["core"])


def adam(w, m, u, g, decay):
    correct = 1.0 - 0.5**STEP
    m = 0.5 * m + 0.5 * g
    u = 0.5 * u + 0.5 * g * g
    return w - step_rate * (m / correct / (jnp.sqrt(u / correct) + adam_eps) + decay * w), m, u


def pick(lo_ref, hi_ref, t, rows=slice(None)):
    lo = lo_ref[t % 2, rows, :].astype(F32)
    hi = hi_ref[t % 2, rows, :].astype(F32)
    return jnp.where(t < 2, lo, hi)


def adam_down(where, tabs, sums, w, mom, count):
    rows, cols = w.shape
    rb = rows // 8

    def kern(where_ref, tab_ref, a0, a1, b0, b1, w_ref, m_ref, g_out, w_out, m_out):
        i = pl.program_id(0)
        mine = i // 4 == where_ref[1]
        q = i % 4
        g = jnp.where(mine, pick(a0, a1, tab_ref[q]), pick(b0, b1, tab_ref[4 + q])) * count
        g_out[...] = g
        w_out[...], m_out[0], m_out[1] = adam(w_ref[...], m_ref[0], m_ref[1], g, matrix_decay)

    full = lambda s: pl.BlockSpec(s, lambda i: (0,) * len(s))
    blk = pl.BlockSpec((rb, cols), lambda i: (i, 0))
    blk2 = pl.BlockSpec((2, rb, cols), lambda i: (0, i, 0))
    return pl.pallas_call(
        kern,
        grid=(8,),
        in_specs=[SMEM, SMEM] + [full(s.shape) for s in sums] + [blk, blk2],
        out_specs=[blk, blk, blk2],
        out_shape=[sds(w.shape, F32), sds(w.shape, F32), sds(mom.shape, F32)],
        compiler_params=params(),
        cost_estimate=cost(20 * w.size, 28 * w.size, 2 * w.size),
        name="adam_down",
    )(where, tabs, *sums, w, mom)


def adam_cols(where, tabs, sums, mats, at, count, name):
    unit = sums[0].shape[2]
    k = len(mats)

    def kern(where_ref, tab_ref, a0, a1, b0, b1, *refs):
        q = pl.program_id(0)
        flip = where_ref[1] == 1
        ta, tb = tab_ref[q], tab_ref[4 + q]
        p = at
        for i, (w, _, parts, per) in enumerate(mats):
            w_ref, m_ref = refs[2 * i], refs[2 * i + 1]
            g_out, w_out, m_out = refs[2 * k + 3 * i : 2 * k + 3 * i + 3]
            rb = w.shape[0] // 4
            for part in range(parts):
                for j in range(per):
                    rows = slice(p, p + rb)
                    a, b = pick(a0, a1, ta, rows) * count, pick(b0, b1, tb, rows) * count
                    p += rb
                    for h in range(2):
                        g = jnp.where(flip, b, a) if h == 0 else jnp.where(flip, a, b)
                        c0 = ((part * 2 + h) * per + j) * unit
                        cs = slice(c0, c0 + unit)
                        g_out[:, cs] = g
                        w_out[:, cs], m_out[0, :, cs], m_out[1, :, cs] = adam(w_ref[:, cs], m_ref[0, :, cs], m_ref[1, :, cs], g, matrix_decay)

    full = lambda s: pl.BlockSpec(s, lambda i: (0,) * len(s))
    ins, outs, shapes, args = [], [], [], []
    for w, mom, _, _ in mats:
        blk = pl.BlockSpec((w.shape[0] // 4, w.shape[1]), lambda i: (i, 0))
        blk2 = pl.BlockSpec((2, w.shape[0] // 4, w.shape[1]), lambda i: (0, i, 0))
        ins += [blk, blk2]
        outs += [blk, blk, blk2]
        shapes += [sds(w.shape, F32), sds(w.shape, F32), sds(mom.shape, F32)]
        args += [w, mom]
    size = sum(w.size for w, _, _, _ in mats)
    return pl.pallas_call(
        kern,
        grid=(4,),
        in_specs=[SMEM, SMEM] + [full(s.shape) for s in sums] + ins,
        out_specs=outs,
        out_shape=shapes,
        compiler_params=params(),
        cost_estimate=cost(20 * size, 28 * size, 2 * size),
        name=name,
    )(where, tabs, *sums, *args)


def permutations(groups, reps):
    flat = lambda f: [(g * reps + r, f(g, r)) for g in range(groups) for r in range(reps)]
    at = lambda g, r: g * reps + r
    far = []
    bit = 8
    while bit < reps:
        far.append(flat(lambda g, r, bit=bit: at(g, r ^ bit)))
        bit *= 2
    return {
        "core": flat(lambda g, r: at(g, r ^ 1)),
        "s1": flat(lambda g, r: at(g ^ (1 + r % 2), r)),
        "s2": flat(lambda g, r: at(g ^ (2 - r % 2), r)),
        "z1": flat(lambda g, r: at(g, r ^ (2 + 2 * (r % 2)))),
        "z2": flat(lambda g, r: at(g, r ^ (4 - 2 * (r % 2)))),
        "far": far,
    }


def local(groups, reps, hidden_in, out_grad, segment_ids, rand_blocks, w_qkv, w_out, w_in, w_down, vec_params, bias_hidden,
          moments_qkv, moments_out, moments_in, moments_down, moments_vec, moments_bias):
    perms = permutations(groups, reps)
    seqs, n, d = hidden_in.shape
    nb = rand_blocks.shape[1]
    g = lax.axis_index("group").astype(I32)
    r = lax.axis_index("rep").astype(I32)
    c, z = r % 2, (r // 2) % 4
    where = jnp.stack([g, c, z])
    one, two = 1 + c, 2 - c
    table = jnp.stack([2 * g + c, 2 * g + 1 - c, 2 * (g ^ one) + c, 2 * (g ^ one) + 1 - c,
                       2 * (g ^ two) + 1 - c, 2 * (g ^ two) + c, 2 * (g ^ 3) + c, 2 * (g ^ 3) + 1 - c])
    four = jnp.arange(4, dtype=I32)

    def turn(core, v):
        return jnp.where(core == 0, (v % 2) * 2 + v // 2, v)

    def order(core):
        return (turn(core, four ^ g)[:, None] * 4 + turn(core, four ^ z)[None, :]).reshape(16)

    tabs = jnp.concatenate([turn(c, four ^ z), turn(1 - c, four ^ z)])
    mine, other = order(c), order(1 - c)
    hm, ho = c[None], (1 - c)[None]

    pa = pack_a(where, w_qkv, vec_params.T, jnp.broadcast_to(bias_hidden[None], (8, bias_hidden.shape[0])))
    ga = gather(pa, perms)
    pb = pack_b(where, w_out, w_in, w_down)
    gb = gather(pb, perms)

    x = hidden_in.reshape(n, d)
    dy = out_grad.reshape(n, d)
    seg_col = jnp.broadcast_to(segment_ids.reshape(n, 1), (n, PAIR))
    rr = jnp.pad(rand_blocks[0].T, ((0, 0), (0, HEAD_DIM - nb)), constant_values=-1)
    rand_rows = jnp.concatenate([rr, rr], axis=1)

    qkv, wq_full, vec, bias = project(x, table, ga, groups)
    o, f = attn_fwd(qkv, seg_col, rand_rows, nb)
    y, dr1, hb, dh, x1b, dfb, dab, do, vs, bs = token(x, dy, o, vec, bias, table, gb)

    sums1 = reduce_all(grad_down(other, ho, hb, dfb, groups, 4), grad_down(mine, hm, hb, dfb, groups, 4), perms)
    sums2 = reduce_all(*[grad_cols(od, h, [(x1b, dh), (o, dab)], 16, None, "grad_in_out") for od, h in ((other, ho), (mine, hm))], perms)

    dq, dk, dv, qs = attn_bwd(qkv, f, o, do, seg_col, rand_rows, nb)
    vgrad = jnp.concatenate([qs[0:2], vs[2:8]], axis=0)
    small = jnp.concatenate([
        vgrad.reshape(4, 2, groups, d // groups).transpose(2, 0, 1, 3).reshape(groups, 4, 384),
        bs[:groups].reshape(groups, 2, 384),
        jnp.zeros((groups, 2, 384), F32),
    ], axis=1)
    small = small.reshape(groups, 2, 4, 384).transpose(0, 2, 1, 3).reshape(16, 2, 384)
    sums3 = reduce_all(*[grad_cols(od, h, [(x, dq), (x, dk), (x, dv)], 16, small, "grad_qkv") for od, h in ((other, ho), (mine, hm))], perms)
    gin = grad_input(dr1, dq, dk, dv, wq_full)

    count = 1.0 / (seqs * groups * reps)
    g_down, n_down, m_down = adam_down(where, tabs, sums1, w_down, moments_down, count)
    g_in, n_in, m_in, g_out, n_out, m_out = adam_cols(where, tabs, sums2, [(w_in, moments_in, 1, 4), (w_out, moments_out, 1, 1)], 0, count, "adam_in_out")
    g_qkv, n_qkv, m_qkv = adam_cols(where, tabs, sums3, [(w_qkv, moments_qkv, 3, 1)], 0, count, "adam_qkv")

    last = [jnp.concatenate([a[:, -1, :], b[:, -1, :]], axis=0) for a, b in ((sums3[0], sums3[1]), (sums3[2], sums3[3]))]
    own, sib = jnp.take(last[0], tabs[:4], axis=0), jnp.take(last[1], tabs[4:], axis=0)
    rows8 = jnp.where(c == 0, jnp.concatenate([own, sib]), jnp.concatenate([sib, own])).astype(F32) * count
    g_vec = rows8[:4].reshape(8, d // groups).T
    g_bias = rows8[4:6].reshape(-1)
    n_vec, m1, u1 = adam(vec_params, moments_vec[0], moments_vec[1], g_vec, 0.0)
    n_bias, m2, u2 = adam(bias_hidden, moments_bias[0], moments_bias[1], g_bias, 0.0)
    return (y.reshape(hidden_in.shape), gin.reshape(hidden_in.shape), g_qkv, g_out, g_in, g_down, g_vec, g_bias,
            n_qkv, n_out, n_in, n_down, n_vec, n_bias, m_qkv, m_out, m_in, m_down, jnp.stack([m1, u1]), jnp.stack([m2, u2]))


def solution(mesh):
    groups, reps = mesh.shape["group"], mesh.shape["rep"]
    tok = P(AX, None, None)
    row, mom = P("group", None), P(None, "group", None)

    def run(*args):
        return local(groups, reps, *args)

    return jax.shard_map(
        run,
        mesh=mesh,
        in_specs=(tok, tok, P(AX, None), tok, row, row, row, row, row, P("group"), mom, mom, mom, mom, mom, P(None, "group")),
        out_specs=(tok, tok, row, row, row, row, row, P("group"), row, row, row, row, row, P("group"), mom, mom, mom, mom, mom, P(None, "group")),
        check_vma=False,
    )
```

```python
import jax
import jax.numpy as jnp
from jax import lax
from jax.experimental import pallas as pl
from jax.experimental.pallas import tpu as pltpu
from jax.sharding import PartitionSpec as P

HEAD_DIM = 64
STEP = 4
norm_eps = 1e-05
adam_eps = 1e-08
matrix_decay = 0.1
step_rate = 0.1
BF = jnp.bfloat16
F32 = jnp.float32
I32 = jnp.int32
VM = 56 * 1024 * 1024
NEG = -1e30
PAIR = 2 * HEAD_DIM
SQH = 0.7071067811865476
PHI0 = 0.3989422804014327
AX = ("group", "rep")
ANY = pl.BlockSpec(memory_space=pl.ANY)
SMEM = pl.BlockSpec(memory_space=pltpu.SMEM)
VMEM = pl.BlockSpec(memory_space=pltpu.VMEM)
sds = jax.ShapeDtypeStruct


def cost(flops, nbytes, trans=0):
    return pl.CostEstimate(flops=int(flops), bytes_accessed=int(nbytes), transcendentals=int(trans))


def params(**kw):
    return pltpu.CompilerParams(vmem_limit_bytes=VM, **kw)

def nt(a, b):
    return lax.dot_general(a, b, (((1,), (1,)), ((), ())), preferred_element_type=F32)


def nn(a, b):
    return lax.dot_general(a, b, (((1,), (0,)), ((), ())), preferred_element_type=F32)


def tn(a, b):
    return lax.dot_general(a, b, (((0,), (0,)), ((), ())), preferred_element_type=F32)


def split3(v):
    hi = v.astype(BF).astype(F32)
    mid = (v - hi).astype(BF).astype(F32)
    return hi, mid, v - hi - mid


def attn_feats(seg_ref, rand_ref, fq_s, fk_s, nb):
    n = fq_s.shape[0]
    bl = n // nb
    lane = lax.broadcasted_iota(jnp.int32, (n, PAIR), 1) % HEAD_DIM
    blk = lax.broadcasted_iota(jnp.int32, (n, PAIR), 0) // bl
    seg = seg_ref[...]
    fq = (lane == blk) | ((lane >= nb) & (lane - nb == seg))
    fq_s[...] = jnp.where(fq, 1.0, 0.0).astype(BF)
    allow = (jnp.abs(lane - blk) <= 1) | (lane == 0) | (lane == nb - 1) | (blk == 0) | (blk == nb - 1)
    for j in range(rand_ref.shape[0]):
        allow = allow | (rand_ref[j : j + 1, :] == blk)
    bad = ((lane < nb) & jnp.logical_not(allow)) | ((lane >= nb) & (lane < nb + 4) & (lane - nb != seg))
    off = (lane >= nb + 4) & (lane < nb + 7)
    fk_s[...] = jnp.where(bad, NEG, jnp.where(off, -1.0, 0.0)).astype(BF)


def attn_fwd_kernel(nb, seg_ref, rand_ref, q_ref, k_ref, v_ref, o_ref, f_ref, fq_s, fk_s):
    @pl.when(pl.program_id(0) == 0)
    def _():
        attn_feats(seg_ref, rand_ref, fq_s, fk_s, nb)

    n = q_ref.shape[0]
    t = 256
    low1 = lax.broadcasted_iota(jnp.int32, (n, PAIR), 1) < HEAD_DIM
    k = k_ref[...]
    v = v_ref[...]
    fk = fk_s[...]
    one = jnp.ones((n, PAIR), BF)
    ks = (jnp.where(low1, k, fk), jnp.where(low1, fk, k))
    vs = (jnp.where(low1, v, one), jnp.where(low1, one, v))
    lowt = lax.broadcasted_iota(jnp.int32, (t, PAIR), 1) < HEAD_DIM
    lane = lax.broadcasted_iota(jnp.int32, (t, PAIR), 1) % HEAD_DIM
    for i in range(n // t):
        rows = pl.ds(i * t, t)
        q = q_ref[rows, :] * jnp.asarray(HEAD_DIM**-0.5, BF)
        fq = fq_s[rows, :]
        acc, top = [], []
        for h in range(2):
            qh = jnp.where(lowt, q, fq) if h == 0 else jnp.where(lowt, fq, q)
            s = nt(qh, ks[h])
            m = jnp.max(s, axis=-1, keepdims=True)
            p = jnp.exp(s - m).astype(BF)
            acc.append(nn(p, vs[h]))
            top.append(m)
        lsw = jnp.where(lowt, acc[1], acc[0])
        o = jnp.where(lowt, acc[0], acc[1]) / pltpu.roll(lsw, HEAD_DIM, 1)
        o_ref[rows, :] = o.astype(BF)
        hi, mid, lo = split3(jnp.where(lowt, top[1], top[0]) + jnp.log(lsw))
        f = jnp.where(lane == nb + 4, hi, jnp.where(lane == nb + 5, mid, lo))
        f_ref[rows, :] = jnp.where((lane >= nb + 4) & (lane < nb + 7), f.astype(BF), fq)


def attn_fwd(qkv, seg_col, rand_rows, nb, p0, p1):
    n, w3 = qkv.shape
    pairs = w3 // 3 // PAIR
    cols = (p1 - p0) * PAIR
    blk = lambda off: pl.BlockSpec((n, PAIR), lambda p, off=off: (0, p + off))
    full = lambda a: pl.BlockSpec(a.shape, lambda p: (0, 0))
    return pl.pallas_call(
        lambda *refs: attn_fwd_kernel(nb, *refs),
        grid=(p1 - p0,),
        in_specs=[full(seg_col), full(rand_rows), blk(p0), blk(pairs + p0), blk(2 * pairs + p0)],
        out_specs=[blk(0), blk(0)],
        out_shape=[sds((n, cols), BF)] * 2,
        scratch_shapes=[pltpu.VMEM((n, PAIR), BF)] * 2,
        compiler_params=params(),
        cost_estimate=cost(16 * n * n * cols, 12 * n * cols, n * n * cols // HEAD_DIM),
        name="attn_fwd",
    )(seg_col, rand_rows, qkv, qkv, qkv)


def attn_bwd_kernel(nb, seg_ref, rand_ref, q_ref, k_ref, v_ref, f_ref, o_ref, do_ref, dq_ref, dk_ref, dv_ref, b_ref, fq_s, fk_s):
    @pl.when(pl.program_id(0) == 0)
    def _():
        attn_feats(seg_ref, rand_ref, fq_s, fk_s, nb)

    n = q_ref.shape[0]
    t = 256
    low1 = lax.broadcasted_iota(jnp.int32, (n, PAIR), 1) < HEAD_DIM
    lane = lax.broadcasted_iota(jnp.int32, (n, PAIR), 1) % HEAD_DIM
    scale = jnp.asarray(HEAD_DIM**-0.5, BF)
    q = q_ref[...] * scale
    f = f_ref[...]
    do = do_ref[...]
    prod = do.astype(F32) * o_ref[...].astype(F32)
    d0 = jnp.sum(jnp.where(low1, prod, 0.0), axis=-1, keepdims=True)
    d1 = jnp.sum(jnp.where(low1, 0.0, prod), axis=-1, keepdims=True)
    hi, mid, lo = split3(jnp.where(low1, d1, d0))
    fd = jnp.where(lane == nb + 4, hi, jnp.where(lane == nb + 5, mid, jnp.where(lane == nb + 6, lo, 0.0))).astype(BF)
    qs = (jnp.where(low1, q, f), jnp.where(low1, f, q))
    dos = (jnp.where(low1, do, fd), jnp.where(low1, fd, do))
    kT = jnp.transpose(k_ref[...] * scale)
    lowt = lax.broadcasted_iota(jnp.int32, (t, PAIR), 1) < HEAD_DIM
    dqT = [None, None]
    dv_sum = jnp.zeros((1, PAIR), F32)
    for i in range(n // t):
        rows = pl.ds(i * t, t)
        k = k_ref[rows, :]
        v = v_ref[rows, :]
        fk = fk_s[rows, :]
        fv = jnp.where(fk == -1.0, fk, jnp.zeros_like(fk))
        dvh, dkh = [], []
        for h in range(2):
            kh = jnp.where(lowt, k, fk) if h == 0 else jnp.where(lowt, fk, k)
            vh = jnp.where(lowt, v, fv) if h == 0 else jnp.where(lowt, fv, v)
            p = jnp.exp(nt(kh, qs[h]))
            ds = (p * nt(vh, dos[h])).astype(BF)
            dvh.append(nn(p.astype(BF), do))
            dkh.append(nn(ds, q))
            part = nn(kT[h * HEAD_DIM : (h + 1) * HEAD_DIM, i * t : (i + 1) * t], ds)
            dqT[h] = part if dqT[h] is None else dqT[h] + part
        dk = jnp.where(lowt, dkh[0], dkh[1]).astype(BF)
        dv = jnp.where(lowt, dvh[0], dvh[1]).astype(BF)
        dk_ref[rows, :] = dk
        dv_ref[rows, :] = dv
        dv_sum = dv_sum + colsum(dv.astype(F32))
    dq = jnp.transpose(jnp.concatenate(dqT, axis=0)).astype(BF)
    dq_ref[...] = dq
    b_ref[...] = jnp.concatenate([colsum(dq.astype(F32)), dv_sum, jnp.zeros((6, PAIR), F32)], axis=0)


def attn_bwd(qkv, f, o, do, seg_col, rand_rows, nb, p0, p1, off):
    n, w3 = qkv.shape
    pairs = w3 // 3 // PAIR
    cols = (p1 - p0) * PAIR
    blk = lambda off: pl.BlockSpec((n, PAIR), lambda p, off=off: (0, p + off))
    full = lambda a: pl.BlockSpec(a.shape, lambda p: (0,) * a.ndim)
    return pl.pallas_call(
        lambda *refs: attn_bwd_kernel(nb, *refs),
        grid=(p1 - p0,),
        in_specs=[full(seg_col), full(rand_rows), blk(p0), blk(pairs + p0), blk(2 * pairs + p0), blk(p0 - off), blk(p0 - off), blk(p0)],
        out_specs=[blk(0), blk(0), blk(0), pl.BlockSpec((8, PAIR), lambda p: (0, p))],
        out_shape=[sds((n, cols), BF)] * 3 + [sds((8, cols), F32)],
        scratch_shapes=[pltpu.VMEM((n, PAIR), BF)] * 2,
        compiler_params=params(),
        cost_estimate=cost(40 * n * n * cols, 20 * n * cols, n * n * cols // HEAD_DIM),
        name="attn_bwd",
    )(seg_col, rand_rows, qkv, qkv, qkv, f, o, do)


def grad_qkv(x, parts, vs, bs, core, orders):
    n, d = x.shape
    blocks = orders.shape[1]
    np_ = len(parts)
    unit, rb = d // 2, d // blocks
    g = (blocks, 3 * rb + 16, unit)

    def kern(core_ref, ord_ref, x_ref, vs_ref, bs_ref, *refs):
        ds = [[refs[4 * p + part] for p in range(np_)] for part in range(4)]
        send_ref, keep_ref, g_s, osem = refs[4 * np_ :]
        groups = bs_ref.shape[0]
        quarters = blocks // groups
        x = x_ref[...]
        sels = [1 - (core_ref[0] ^ h) for h in range(2)]
        cat = lambda rs: jnp.concatenate([r[...] for r in rs], axis=1)
        for part in range(3):
            r = tn(x, cat(ds[part])).astype(BF)
            for h in range(2):
                for a in range(blocks):
                    g_s[sels[h], ord_ref[h, a], part * rb : (part + 1) * rb, :] = r[a * rb : (a + 1) * rb, h * unit : (h + 1) * unit]
        vec = jnp.concatenate([cat(ds[3])[0:2], vs_ref[2:8, :]], axis=0)
        share = d // groups
        for gr in range(groups):
            gs = slice(gr * share, (gr + 1) * share)
            lines = [jnp.concatenate([vec[2 * i : 2 * i + 1, gs], vec[2 * i + 1 : 2 * i + 2, gs]], axis=1) for i in range(4)]
            lines += [bs_ref[gr, 0:1, i * unit : (i + 1) * unit] for i in range(2)]
            for h in range(2):
                for q in range(quarters):
                    i = h * quarters + q
                    line = lines[i] if i < len(lines) else jnp.zeros((1, unit), F32)
                    g_s[sels[h], ord_ref[h, gr * quarters + q], 3 * rb : 3 * rb + 16, :] = jnp.broadcast_to(line, (16, unit)).astype(BF)
        out = [pltpu.make_async_copy(g_s.at[0], send_ref, osem.at[0]), pltpu.make_async_copy(g_s.at[1], keep_ref, osem.at[1])]
        for cp in out:
            cp.start()
        for cp in out:
            cp.wait()

    flat = [a for p in parts for a in p]
    return pl.pallas_call(
        kern,
        in_specs=[SMEM, SMEM] + [VMEM] * (3 + len(flat)),
        out_specs=[ANY, ANY],
        out_shape=[sds(g, BF)] * 2,
        scratch_shapes=[pltpu.VMEM((2,) + g, BF), pltpu.SemaphoreType.DMA((2,))],
        compiler_params=params(),
        cost_estimate=cost(6 * n * d * d, 14 * n * d),
        name="grad_qkv",
    )(core, orders, x, vs, bs, *flat)


def norm(r, g, c):
    w = r.shape[-1]
    center = r - jnp.sum(r, axis=-1, keepdims=True) * (1.0 / w)
    inv = lax.rsqrt(jnp.sum(center * center, axis=-1, keepdims=True) * (1.0 / w) + norm_eps)
    n = center * inv
    return n * g + c, n, inv


def norm_back(dy, g, n, inv):
    w = dy.shape[-1]
    e = dy * g
    a = jnp.sum(e, axis=-1, keepdims=True) * (1.0 / w)
    b = jnp.sum(e * n, axis=-1, keepdims=True) * (1.0 / w)
    return inv * (e - a - n * b)


def colsum(a):
    return jnp.sum(a, axis=0, keepdims=True)


def pack_a(where, w, vec_t, bias):
    rows, cols = w.shape
    half = rows // 2

    def kern(where_ref, w_ref, vec_ref, bias_ref, out_ref):
        for h in range(2):
            pos = h ^ where_ref[1]
            out_ref[pos, 0:half, :] = w_ref[h * half : (h + 1) * half, :].astype(BF)
            small = vec_ref[...] if h == 0 else bias_ref[...]
            small = jnp.concatenate([small, jnp.zeros((small.shape[0], cols - small.shape[1]), F32)], axis=1)
            out_ref[pos, half : half + 16, :] = jnp.concatenate([small, small], axis=0).astype(BF)

    return pl.pallas_call(
        kern,
        in_specs=[SMEM, VMEM, VMEM, VMEM],
        out_specs=VMEM,
        out_shape=sds((2, half + 16, cols), BF),
        compiler_params=params(),
        cost_estimate=cost(0, 3 * w.size * 2),
        name="pack_a",
    )(where, w, vec_t, bias)


def pack_b(where, wo, wi, wd):
    rows, w = wo.shape
    half = rows // 2
    nf = wi.shape[1] // w
    nd = wd.shape[0] // rows

    def kern(where_ref, wo_ref, wi_ref, wd_ref, out_ref):
        for h in range(2):
            pos = h ^ where_ref[1]
            hs = slice(h * half, (h + 1) * half)
            out_ref[pos, 0] = wo_ref[hs, :].astype(BF)
            for j in range(nf):
                out_ref[pos, 1 + j] = wi_ref[hs, j * w : (j + 1) * w].astype(BF)
            for j in range(nd):
                at = (h * nd + j) * half
                out_ref[pos, 1 + nf + j] = wd_ref[at : at + half, :].astype(BF)

    return pl.pallas_call(
        kern,
        in_specs=[SMEM, VMEM, VMEM, VMEM],
        out_specs=VMEM,
        out_shape=sds((2, 1 + nf + nd, half, w), BF),
        compiler_params=params(),
        cost_estimate=cost(0, 6 * (wo.size + wi.size + wd.size)),
        name="pack_b",
    )(where, wo, wi, wd)


def pperm(a, pairs):
    return lax.ppermute(a, AX, pairs)


def after(late, *early):
    out = lax.optimization_barrier(tuple(late) + early)
    return out[: len(late) + 1] if len(early) == 1 else out


def piece_refs(refs):
    own, near, side, far, back = refs
    return [own.at[0], own.at[1], near.at[0], near.at[1], side.at[0], side.at[1], far.at[0], back.at[0]]


def project(x, table, parts, groups, t=256):
    n, d = x.shape
    _, hp, cols = parts[0].shape
    half = hp - 16
    share = 2 * half

    def kern(tab_ref, x_ref, *refs):
        pieces = piece_refs(refs[:5])
        qkv_ref, w_out, vec_ref, bias_ref, w_s, e_s, sems, osem = refs[5:]
        first = pl.program_id(0) == 0
        last = pl.program_id(0) == pl.num_programs(0) - 1

        def copies():
            out = []
            for i, p in enumerate(pieces):
                u = tab_ref[i]
                out.append(pltpu.make_async_copy(p.at[pl.ds(0, half)], w_s.at[pl.ds(pl.multiple_of(u * half, 16), half)], sems.at[2 * i]))
                out.append(pltpu.make_async_copy(p.at[pl.ds(half, 16)], e_s.at[u], sems.at[2 * i + 1]))
            return out

        def whole():
            return pltpu.make_async_copy(w_s, w_out, osem)

        @pl.when(first)
        def _():
            for cp in copies():
                cp.start()
            for cp in copies():
                cp.wait()
            whole().start()
            vec_ref[...] = jnp.concatenate([e_s[2 * g, 0:8, 0:share].astype(F32) for g in range(groups)], axis=1)
            for g in range(groups):
                bias_ref[g] = e_s[2 * g + 1, 0:8, 0:d].astype(F32)

        qb = jnp.concatenate([vec_ref[0:1, :], jnp.zeros((1, d), F32), vec_ref[1:2, :]], axis=1)
        qkv_ref[...] = (nn(x_ref[...], w_s[...]) + qb).astype(BF)

        @pl.when(last)
        def _():
            whole().wait()

    return pl.pallas_call(
        kern,
        grid=(n // t,),
        in_specs=[SMEM, pl.BlockSpec((t, d), lambda i: (i, 0))] + [ANY] * 5,
        out_specs=[pl.BlockSpec((t, cols), lambda i: (i, 0)), ANY, pl.BlockSpec((8, d), lambda i: (0, 0)), pl.BlockSpec((groups, 8, d), lambda i: (0, 0, 0))],
        out_shape=[sds((n, cols), BF), sds((d, cols), BF), sds((8, d), F32), sds((groups, 8, d), F32)],
        scratch_shapes=[pltpu.VMEM((d, cols), BF), pltpu.VMEM((2 * groups, 16, cols), BF), pltpu.SemaphoreType.DMA((16,)), pltpu.SemaphoreType.DMA],
        compiler_params=params(),
        cost_estimate=cost(2 * n * d * cols, 2 * (n * d + 2 * d * cols + n * cols)),
        name="project",
    )(table, x, *parts)


def token(x, dy, os, vec, bias, table, core, orders, parts):
    n, w = x.shape
    _, k9, half, _ = parts[0].shape
    nf = bias.shape[0]
    nd = k9 - 1 - nf
    ff = nf * w
    nblk = orders.shape[1]
    nq = nblk // nf
    unit = w // 2
    rb = w // nblk
    db = w // (2 * nq)
    t = n // 2

    def kern(tab_ref, core_ref, ord_ref, vec_ref, bias_ref, x_ref, dy_ref, o0_ref, o1_ref, *refs):
        pieces = piece_refs(refs[:5])
        (y_ref, dr1_ref, do_ref, s1_ref, k1_ref, vs_ref, bs_ref,
         wo_s, wi_s, wd_s, x_s, dy_s, o_s, n1_s, inv_s, x1b_s, hb_s, sl_s, acc_s, dfb_s, y_s, g_s, sems, isem, osem) = refs[5:]
        ow = o0_ref.shape[1]

        def copies(kind):
            out = []
            for i, p in enumerate(pieces):
                u = tab_ref[i]
                rows = pl.ds(pl.multiple_of(u * half, 16), half)
                if kind == 0:
                    out.append(pltpu.make_async_copy(p.at[0], wo_s.at[rows], sems.at[0, i]))
                elif kind == 1:
                    out.append(pltpu.make_async_copy(p.at[pl.ds(1, nf)], wi_s.at[:, rows], sems.at[1, i]))
                else:
                    out.append(pltpu.make_async_copy(p.at[pl.ds(1 + nf, nd)], wd_s.at[pl.ds(u * nd, nd)], sems.at[2, i]))
            return out

        c_o0 = pltpu.make_async_copy(o0_ref, o_s.at[:, 0:ow], isem.at[0])
        c_o1 = pltpu.make_async_copy(o1_ref, o_s.at[:, ow:w], isem.at[3])
        c_x = pltpu.make_async_copy(x_ref, x_s, isem.at[1])
        c_dy = pltpu.make_async_copy(dy_ref, dy_s, isem.at[2])
        for cp in copies(0) + [c_o0, c_o1, c_x] + copies(1) + copies(2) + [c_dy]:
            cp.start()
        row = lambda j: vec_ref[j : j + 1, :]
        bo, g1, c1, bd, g2, c2 = [row(j) for j in range(2, 8)]
        per = wd_s.shape[0] // nf
        down = lambda j: wd_s[pl.ds(j * per, per)].reshape(w, w)
        for cp in copies(0) + [c_o0, c_o1, c_x]:
            cp.wait()

        def first(i, _):
            rows = pl.ds(pl.multiple_of(i * t, t), t)
            x1, n1, inv1 = norm(x_s[rows, :].astype(F32) + (nn(o_s[rows, :], wo_s[...]) + bo), g1, c1)
            n1_s[rows, :] = n1
            inv_s[rows, :] = jnp.broadcast_to(inv1, (t, 128))
            x1b_s[rows, :] = x1.astype(BF)
            acc_s[rows, :] = x1 + bd
            return 0

        lax.fori_loop(0, 2, first, 0)
        for cp in copies(1) + copies(2):
            cp.wait()

        def up(j, _):
            for i in range(2):
                rows = slice(i * t, (i + 1) * t)
                h = nn(x1b_s[rows, :], wi_s[j]) + bias_ref[j, 0:1, :]
                cdf = 0.5 * (1.0 + lax.erf(h * SQH))
                hb = (h * cdf).astype(BF)
                sl_s[j, rows, :] = (cdf + h * (jnp.exp(-0.5 * (h * h)) * PHI0)).astype(BF)
                hb_s[j, rows, :] = hb
                acc_s[rows, :] += nn(hb, down(j))
            return 0

        lax.fori_loop(0, nf, up, 0)
        c_dy.wait()
        vs_ref[...] = jnp.zeros_like(vs_ref)

        def top(i, _):
            rows = pl.ds(pl.multiple_of(i * t, t), t)
            y, n2, inv2 = norm(acc_s[rows, :], g2, c2)
            y_s[rows, :] = y
            dyf = dy_s[rows, :].astype(F32)
            dr2 = norm_back(dyf, g2, n2, inv2)
            acc_s[rows, :] = dr2
            dfb_s[rows, :] = dr2.astype(BF)
            vs_ref[5:6, :] += colsum(dr2)
            vs_ref[6:7, :] += colsum(dyf * n2)
            vs_ref[7:8, :] += colsum(dyf)
            return 0

        lax.fori_loop(0, 2, top, 0)
        c_y = pltpu.make_async_copy(y_s, y_ref, osem.at[0])
        c_y.start()

        def back(j, _):
            for i in range(2):
                rows = slice(i * t, (i + 1) * t)
                dh = (nt(dfb_s[rows, :], down(j)) * sl_s[j, rows, :].astype(F32)).astype(BF)
                sl_s[j, rows, :] = dh
                s = jnp.broadcast_to(colsum(dh.astype(F32)), (8, w))
                bs_ref[j] = s if i == 0 else bs_ref[j] + s
                acc_s[rows, :] += nt(dh, wi_s[j])
            gd = tn(hb_s[j], dfb_s[...]).astype(BF)
            for h in range(2):
                sel = 1 - (core_ref[0] ^ h)
                for q in range(nq):
                    r0 = (h * nq + q) * db
                    pos = ord_ref[h, j * nq + q]
                    for k in range(2):
                        g_s[sel, pos, k * db : (k + 1) * db, :] = gd[r0 : r0 + db, k * unit : (k + 1) * unit]
            gi = tn(x1b_s[...], sl_s[j]).astype(BF)
            h = j // (nf // 2)
            sel = 1 - (core_ref[0] ^ h)
            for a in range(nblk):
                pos = ord_ref[h, a]
                for k in range(2):
                    at = pl.multiple_of(2 * db + ((j % (nf // 2)) * 2 + k) * rb, 16)
                    g_s[sel, pos, pl.ds(at, rb), :] = gi[a * rb : (a + 1) * rb, k * unit : (k + 1) * unit]
            return 0

        lax.fori_loop(0, nf, back, 0)

        def low(i, _):
            rows = pl.ds(pl.multiple_of(i * t, t), t)
            dx1 = acc_s[rows, :]
            n1 = n1_s[rows, :]
            dr1 = norm_back(dx1, g1, n1, inv_s[rows, 0:1])
            acc_s[rows, :] = dr1
            dab = dr1.astype(BF)
            x_s[rows, :] = dab
            dy_s[rows, :] = nt(dab, wo_s[...]).astype(BF)
            vs_ref[2:3, :] += colsum(dr1)
            vs_ref[3:4, :] += colsum(dx1 * n1)
            vs_ref[4:5, :] += colsum(dx1)
            return 0

        lax.fori_loop(0, 2, low, 0)
        c_dr1 = pltpu.make_async_copy(acc_s, dr1_ref, osem.at[3])
        c_do = pltpu.make_async_copy(dy_s, do_ref, osem.at[4])
        c_dr1.start()
        c_do.start()
        go = tn(o_s[...], x_s[...]).astype(BF)
        for h in range(2):
            sel = 1 - (core_ref[0] ^ h)
            for a in range(nblk):
                g_s[sel, ord_ref[h, a], 2 * db + nf * rb : 2 * db + (nf + 1) * rb, :] = go[a * rb : (a + 1) * rb, h * unit : (h + 1) * unit]
        c_s1 = pltpu.make_async_copy(g_s.at[0], s1_ref, osem.at[1])
        c_k1 = pltpu.make_async_copy(g_s.at[1], k1_ref, osem.at[2])
        c_s1.start()
        c_k1.start()
        for cp in (c_y, c_s1, c_k1, c_dr1, c_do):
            cp.wait()

    gs = (nblk, 2 * db + (nf + 1) * rb, unit)
    vm = lambda s, dt=BF: pltpu.VMEM(s, dt)
    return pl.pallas_call(
        kern,
        in_specs=[SMEM, SMEM, SMEM, VMEM, VMEM] + [ANY] * 9,
        out_specs=[ANY] * 5 + [VMEM, VMEM],
        out_shape=[sds((n, w), F32), sds((n, w), F32), sds((n, w), BF), sds(gs, BF), sds(gs, BF), sds((8, w), F32), sds((nf, 8, w), F32)],
        scratch_shapes=[vm((w, w)), vm((nf, w, w)), vm((ff // half, half, w)), vm((n, w)), vm((n, w)), vm((n, w)), vm((n, w), F32), vm((n, 128), F32),
                        vm((n, w)), vm((nf, n, w)), vm((nf, n, w)), vm((n, w), F32), vm((n, w)), vm((n, w), F32), vm((2,) + gs),
                        pltpu.SemaphoreType.DMA((3, 8)), pltpu.SemaphoreType.DMA((4,)), pltpu.SemaphoreType.DMA((5,))],
        compiler_params=params(),
        cost_estimate=cost(2 * n * w * (3 * w + 6 * ff), 2 * (n * 8 * w + 3 * w * (w + 2 * ff)), 2 * n * ff),
        name="token",
    )(table, core, orders, vec, bias, x, dy, *os, *parts)


def grad_input(dr1, parts, w, t=256):
    n, d = dr1.shape
    k = len(parts)

    def kern(r_ref, w_ref, *refs):
        out_ref = refs[-1]
        out = r_ref[...]
        for part in range(3):
            g = jnp.concatenate([refs[3 * p + part][...] for p in range(k)], axis=1)
            out = out + nt(g, w_ref[:, part * d : (part + 1) * d])
        out_ref[...] = out

    rows = lambda c: pl.BlockSpec((t, c), lambda i: (i, 0))
    flat = [a for p in parts for a in p[:3]]
    return pl.pallas_call(
        kern,
        grid=(n // t,),
        in_specs=[rows(d), pl.BlockSpec(w.shape, lambda i: (0, 0))] + [rows(a.shape[1]) for a in flat],
        out_specs=rows(d),
        out_shape=sds((n, d), F32),
        compiler_params=params(),
        cost_estimate=cost(6 * n * d * d, n * d * 14 + 2 * w.size),
        name="grad_input",
    )(dr1, w, *flat)


def total(*terms):
    out = terms[0].astype(F32)
    for a in terms[1:]:
        out = out + a.astype(F32)
    return out.astype(BF)


def reduce_rep(terms, perms):
    b = terms[0].shape[0]
    m, e = b // 2, b // 4
    z1 = pperm(total(*[k[m:] for k in terms]), perms["z1"])
    z2 = pperm(total(*[k[e:m] for k in terms], z1[e:]), perms["z2"])
    t0 = total(*[k[:e] for k in terms], z1[:e], z2)
    for extra in perms["far"]:
        t0 = total(t0, pperm(t0, extra))
    t1 = pperm(t0, perms["z2"])
    t01 = jnp.concatenate([t0, t1], axis=0)
    t23 = pperm(t01, perms["z1"])
    return t01, t23, pperm(t01, perms["core"]), pperm(t23, perms["core"])


def reduce_rep_whole(terms, perms):
    t = total(*terms)
    for step in [perms["z1"], perms["z2"]] + perms["far"]:
        t = total(t, pperm(t, step))
    m = t.shape[0] // 2
    s = pperm(t, perms["core"])
    return t[:m], t[m:], s[:m], s[m:]


def adam(w, m, u, g, decay):
    correct = 1.0 - 0.5**STEP
    m = 0.5 * m + 0.5 * g
    u = 0.5 * u + 0.5 * g * g
    return w - step_rate * (m / correct / (jnp.sqrt(u / correct) + adam_eps) + decay * w), m, u


def pick(lo_ref, hi_ref, t, rows=slice(None)):
    lo = lo_ref[t % 2, rows, :].astype(F32)
    hi = hi_ref[t % 2, rows, :].astype(F32)
    return jnp.where(t < 2, lo, hi)


def adam_down(where, tabs, sums, w, mom, count):
    rows, cols = w.shape
    rb = rows // 8

    def kern(where_ref, tab_ref, a0, a1, b0, b1, w_ref, m_ref, g_out, w_out, m_out):
        i = pl.program_id(0)
        mine = i // 4 == where_ref[1]
        q = i % 4
        gr = slice(0, 2 * rb)
        g = jnp.where(mine, pick(a0, a1, tab_ref[q], gr), pick(b0, b1, tab_ref[4 + q], gr)) * count
        g = jnp.concatenate([g[:rb], g[rb:]], axis=1)
        g_out[...] = g
        w_out[...], m_out[0], m_out[1] = adam(w_ref[...], m_ref[0], m_ref[1], g, matrix_decay)

    full = lambda s: pl.BlockSpec(s, lambda i: (0,) * len(s))
    blk = pl.BlockSpec((rb, cols), lambda i: (i, 0))
    blk2 = pl.BlockSpec((2, rb, cols), lambda i: (0, i, 0))
    return pl.pallas_call(
        kern,
        grid=(8,),
        in_specs=[SMEM, SMEM] + [full(s.shape) for s in sums] + [blk, blk2],
        out_specs=[blk, blk, blk2],
        out_shape=[sds(w.shape, F32), sds(w.shape, F32), sds(mom.shape, F32)],
        compiler_params=params(),
        cost_estimate=cost(20 * w.size, 28 * w.size, 2 * w.size),
        name="adam_down",
    )(where, tabs, *sums, w, mom)


def adam_cols(where, tabs, sums, mats, at, count, name):
    unit = sums[0].shape[2]
    k = len(mats)

    def kern(where_ref, tab_ref, a0, a1, b0, b1, *refs):
        q = pl.program_id(0)
        flip = where_ref[1] == 1
        ta, tb = tab_ref[q], tab_ref[4 + q]
        p = at
        for i, (w, _, parts, per) in enumerate(mats):
            w_ref, m_ref = refs[2 * i], refs[2 * i + 1]
            g_out, w_out, m_out = refs[2 * k + 3 * i : 2 * k + 3 * i + 3]
            rb = w.shape[0] // 4
            for part in range(parts):
                for j in range(per):
                    rows = slice(p, p + rb)
                    a, b = pick(a0, a1, ta, rows) * count, pick(b0, b1, tb, rows) * count
                    p += rb
                    for h in range(2):
                        g = jnp.where(flip, b, a) if h == 0 else jnp.where(flip, a, b)
                        c0 = ((part * 2 + h) * per + j) * unit
                        cs = slice(c0, c0 + unit)
                        g_out[:, cs] = g
                        w_out[:, cs], m_out[0, :, cs], m_out[1, :, cs] = adam(w_ref[:, cs], m_ref[0, :, cs], m_ref[1, :, cs], g, matrix_decay)

    full = lambda s: pl.BlockSpec(s, lambda i: (0,) * len(s))
    ins, outs, shapes, args = [], [], [], []
    for w, mom, _, _ in mats:
        blk = pl.BlockSpec((w.shape[0] // 4, w.shape[1]), lambda i: (i, 0))
        blk2 = pl.BlockSpec((2, w.shape[0] // 4, w.shape[1]), lambda i: (0, i, 0))
        ins += [blk, blk2]
        outs += [blk, blk, blk2]
        shapes += [sds(w.shape, F32), sds(w.shape, F32), sds(mom.shape, F32)]
        args += [w, mom]
    size = sum(w.size for w, _, _, _ in mats)
    return pl.pallas_call(
        kern,
        grid=(4,),
        in_specs=[SMEM, SMEM] + [full(s.shape) for s in sums] + ins,
        out_specs=outs,
        out_shape=shapes,
        compiler_params=params(),
        cost_estimate=cost(20 * size, 28 * size, 2 * size),
        name=name,
    )(where, tabs, *sums, *args)


def permutations(groups, reps):
    flat = lambda f: [(g * reps + r, f(g, r)) for g in range(groups) for r in range(reps)]
    at = lambda g, r: g * reps + r
    far = []
    bit = 8
    while bit < reps:
        far.append(flat(lambda g, r, bit=bit: at(g, r ^ bit)))
        bit *= 2
    return {
        "core": flat(lambda g, r: at(g, r ^ 1)),
        "s1": flat(lambda g, r: at(g ^ (1 + r % 2), r)),
        "s2": flat(lambda g, r: at(g ^ (2 - r % 2), r)),
        "z1": flat(lambda g, r: at(g, r ^ (2 + 2 * (r % 2)))),
        "z2": flat(lambda g, r: at(g, r ^ (4 - 2 * (r % 2)))),
        "far": far,
    }


def local(groups, reps, hidden_in, out_grad, segment_ids, rand_blocks, w_qkv, w_out, w_in, w_down, vec_params, bias_hidden,
          moments_qkv, moments_out, moments_in, moments_down, moments_vec, moments_bias):
    perms = permutations(groups, reps)
    seqs, n, d = hidden_in.shape
    nb = rand_blocks.shape[1]
    g = lax.axis_index("group").astype(I32)
    r = lax.axis_index("rep").astype(I32)
    c, z = r % 2, (r // 2) % 4
    where = jnp.stack([g, c, z])
    one, two = 1 + c, 2 - c
    table = jnp.stack([2 * g + c, 2 * g + 1 - c, 2 * (g ^ one) + c, 2 * (g ^ one) + 1 - c,
                       2 * (g ^ two) + 1 - c, 2 * (g ^ two) + c, 2 * (g ^ 3) + c, 2 * (g ^ 3) + 1 - c])
    four = jnp.arange(4, dtype=I32)

    def turn(core, v):
        return jnp.where(core == 0, (v % 2) * 2 + v // 2, v)

    def order(core):
        return (turn(core, four ^ g)[:, None] * 4 + turn(core, four ^ z)[None, :]).reshape(16)

    tabs = jnp.concatenate([turn(c, four ^ z), turn(1 - c, four ^ z)])
    core, orders = c[None], jnp.stack([order(0), order(1)])

    def plain(core):
        return (turn(core, four ^ g)[:, None] * 4 + four[None, :]).reshape(16)

    orders3 = jnp.stack([plain(0), plain(1)])
    tabs3 = jnp.concatenate([four, four])

    pa = pack_a(where, w_qkv, vec_params.T, jnp.broadcast_to(bias_hidden[None], (8, bias_hidden.shape[0])))
    near_a = pperm(pa, perms["s1"])
    wo_in, wi_in, wd_in, _ = after((w_out, w_in, w_down), pa)
    pb = pack_b(where, wo_in, wi_in, wd_in)
    far_a = pperm(near_a[0:1], perms["s2"])
    side_a = pperm(near_a, perms["core"])
    back_a = pperm(far_a, perms["core"])
    pb, _ = after((pb,), far_a)
    near_b = pperm(pb, perms["s1"])

    x = hidden_in.reshape(n, d)
    dy = out_grad.reshape(n, d)
    seg_col = jnp.broadcast_to(segment_ids.reshape(n, 1), (n, PAIR))
    rr = jnp.pad(rand_blocks[0].T, ((0, 0), (0, HEAD_DIM - nb)), constant_values=-1)
    rand_rows = jnp.concatenate([rr, rr], axis=1)

    qkv, wq_full, vec, bias = project(x, table, (pa, near_a, side_a, far_a, back_a), groups)
    o1, f1 = attn_fwd(qkv, seg_col, rand_rows, nb, 0, 4)
    near_b, _ = after((near_b,), o1)
    near_b0 = near_b[0:1]
    far_b = pperm(near_b0, perms["s2"])
    side_b = pperm(near_b, perms["core"])
    qkv_l, _ = after((qkv,), near_b0)
    o2, f2 = attn_fwd(qkv_l, seg_col, rand_rows, nb, 4, 6)
    far_b, _ = after((far_b,), o2)
    back_b = pperm(far_b, perms["core"])
    y, dr1, do, send, keep, vs, bs = token(x, dy, (o1, o2), vec, bias, table, core, orders, (pb, near_b, side_b, far_b, back_b))

    nblk = keep.shape[0]
    a, b = nblk // 2, nblk // 4
    attend = lambda qkv, do, f, o, p0, p1, off: attn_bwd(qkv, f, o, do, seg_col, rand_rows, nb, p0, p1, off)
    got = pperm(send, perms["core"])
    part0 = attend(qkv, do, f1, o1, 0, 2, 0)
    got, _ = after((got,), part0[0])
    up1 = total(keep[a:], got[a:])
    x1 = pperm(up1, perms["s1"])
    do, _ = after((do,), up1)
    part1 = attend(qkv, do, f1, o1, 2, 4, 0)
    do, _ = after((do,), part1[0])
    part2 = attend(qkv, do, f2, o2, 4, 6, 4)
    x1, _ = after((x1,), part2[0])
    up2 = total(keep[b:a], got[b:a], x1[b:])
    x2 = pperm(up2, perms["s2"])
    vs, _ = after((vs,), up2)
    send3, keep3 = grad_qkv(x, (part0, part1, part2), vs, bs, core, orders3)

    got3 = pperm(send3, perms["core"])
    up3 = total(keep3[a:], got3[a:])
    x3 = pperm(up3, perms["s1"])
    x2, _ = after((x2,), up3)
    sums1 = reduce_rep((keep[:b], got[:b], x1[:b], x2), perms)
    dr1, _ = after((dr1,), up3)
    gin = grad_input(dr1, (part0, part1, part2), wq_full)
    up4 = total(keep3[b:a], got3[b:a], x3[b:])
    x4 = pperm(up4, perms["s2"])
    sums3 = reduce_rep_whole((keep3[:b], got3[:b], x3[:b], x4), perms)

    count = 1.0 / (seqs * groups * reps)
    g_down, n_down, m_down = adam_down(where, tabs, sums1, w_down, moments_down, count)
    g_in, n_in, m_in, g_out, n_out, m_out = adam_cols(where, tabs, sums1, [(w_in, moments_in, 1, 4), (w_out, moments_out, 1, 1)], w_down.shape[0] // 4, count, "adam_in_out")
    g_qkv, n_qkv, m_qkv = adam_cols(where, tabs3, sums3, [(w_qkv, moments_qkv, 3, 1)], 0, count, "adam_qkv")

    last = [jnp.concatenate([a[:, -1, :], b[:, -1, :]], axis=0) for a, b in ((sums3[0], sums3[1]), (sums3[2], sums3[3]))]
    own, sib = last
    rows8 = jnp.where(c == 0, jnp.concatenate([own, sib]), jnp.concatenate([sib, own])).astype(F32) * count
    g_vec = rows8[:4].reshape(8, d // groups).T
    g_bias = rows8[4:6].reshape(-1)
    n_vec, m1, u1 = adam(vec_params, moments_vec[0], moments_vec[1], g_vec, 0.0)
    n_bias, m2, u2 = adam(bias_hidden, moments_bias[0], moments_bias[1], g_bias, 0.0)
    return (y.reshape(hidden_in.shape), gin.reshape(hidden_in.shape), g_qkv, g_out, g_in, g_down, g_vec, g_bias,
            n_qkv, n_out, n_in, n_down, n_vec, n_bias, m_qkv, m_out, m_in, m_down, jnp.stack([m1, u1]), jnp.stack([m2, u2]))


def solution(mesh):
    groups, reps = mesh.shape["group"], mesh.shape["rep"]
    tok = P(AX, None, None)
    row, mom = P("group", None), P(None, "group", None)

    def run(*args):
        return local(groups, reps, *args)

    return jax.shard_map(
        run,
        mesh=mesh,
        in_specs=(tok, tok, P(AX, None), tok, row, row, row, row, row, P("group"), mom, mom, mom, mom, mom, P(None, "group")),
        out_specs=(tok, tok, row, row, row, row, row, P("group"), row, row, row, row, row, P("group"), mom, mom, mom, mom, mom, P(None, "group")),
        check_vma=False,
    )
```

```python
import jax
import jax.numpy as jnp
from jax import lax
from jax.experimental import pallas as pl
from jax.experimental.pallas import tpu as pltpu
from jax.sharding import PartitionSpec as P

HEAD_DIM = 64
STEP = 4
norm_eps = 1e-05
adam_eps = 1e-08
matrix_decay = 0.1
step_rate = 0.1
BF = jnp.bfloat16
F32 = jnp.float32
I32 = jnp.int32
NEG = -1e30
PAIR = 2 * HEAD_DIM
SQH = 0.7071067811865476
PHI0 = 0.3989422804014327
AX = ("group", "rep")
ANY = pl.BlockSpec(memory_space=pl.ANY)
SMEM = pl.BlockSpec(memory_space=pltpu.SMEM)
VMEM = pl.BlockSpec(memory_space=pltpu.VMEM)
sds = jax.ShapeDtypeStruct


def cost(flops, nbytes, trans=0):
    return pl.CostEstimate(flops=500 * int(flops), bytes_accessed=500 * int(nbytes), transcendentals=500 * int(trans))


def params(mb=60):
    return pltpu.CompilerParams(vmem_limit_bytes=mb * 1024 * 1024)

def nt(a, b):
    return lax.dot_general(a, b, (((1,), (1,)), ((), ())), preferred_element_type=F32)


def nn(a, b):
    return lax.dot_general(a, b, (((1,), (0,)), ((), ())), preferred_element_type=F32)


def tn(a, b):
    return lax.dot_general(a, b, (((0,), (0,)), ((), ())), preferred_element_type=F32)


def split3(v):
    hi = v.astype(BF).astype(F32)
    mid = (v - hi).astype(BF).astype(F32)
    return hi, mid, v - hi - mid


def attn_feats(seg_col, rand_rows, nb):
    n = seg_col.shape[0]

    def kern(seg_ref, rand_ref, fq_ref, fk_ref):
        lane = lax.broadcasted_iota(I32, (n, PAIR), 1) % HEAD_DIM
        blk = lax.broadcasted_iota(I32, (n, PAIR), 0) // (n // nb)
        seg = jnp.broadcast_to(seg_ref[...], (n, PAIR))
        fq = (lane == blk) | ((lane >= nb) & (lane - nb == seg))
        fq_ref[...] = jnp.where(fq, 1.0, 0.0).astype(BF)
        allow = (jnp.abs(lane - blk) <= 1) | (lane == 0) | (lane == nb - 1) | (blk == 0) | (blk == nb - 1)
        for j in range(rand_ref.shape[0]):
            allow = allow | (rand_ref[j : j + 1, :] == blk)
        bad = ((lane < nb) & jnp.logical_not(allow)) | ((lane >= nb) & (lane < nb + 4) & (lane - nb != seg))
        off = (lane >= nb + 4) & (lane < nb + 7)
        fk_ref[...] = jnp.where(bad, NEG, jnp.where(off, -1.0, 0.0)).astype(BF)

    return pl.pallas_call(
        kern,
        out_shape=[sds((n, PAIR), BF)] * 2,
        compiler_params=params(),
        cost_estimate=cost(20 * n * PAIR, 4 * n * PAIR),
        name="attn_feats",
    )(seg_col, rand_rows)


def attn_fwd_kernel(nb, fq_s, fk_s, q_ref, k_ref, v_ref, o_ref, f_ref):
    n = q_ref.shape[0]
    t = 256
    low1 = lax.broadcasted_iota(jnp.int32, (n, PAIR), 1) < HEAD_DIM
    k = k_ref[...]
    v = v_ref[...]
    fk = fk_s[...]
    one = jnp.ones((n, PAIR), BF)
    ks = (jnp.where(low1, k, fk), jnp.where(low1, fk, k))
    vs = (jnp.where(low1, v, one), jnp.where(low1, one, v))
    lowt = lax.broadcasted_iota(jnp.int32, (t, PAIR), 1) < HEAD_DIM
    lane = lax.broadcasted_iota(jnp.int32, (t, PAIR), 1) % HEAD_DIM
    for i in range(n // t):
        rows = pl.ds(i * t, t)
        q = q_ref[rows, :] * jnp.asarray(HEAD_DIM**-0.5, BF)
        fq = fq_s[rows, :]
        acc, top = [], []
        for h in range(2):
            qh = jnp.where(lowt, q, fq) if h == 0 else jnp.where(lowt, fq, q)
            s = nt(qh, ks[h])
            m = jnp.max(s, axis=-1, keepdims=True)
            p = jnp.exp(s - m).astype(BF)
            acc.append(nn(p, vs[h]))
            top.append(m)
        lsw = jnp.where(lowt, acc[1], acc[0])
        o = jnp.where(lowt, acc[0], acc[1]) / pltpu.roll(lsw, HEAD_DIM, 1)
        o_ref[rows, :] = o.astype(BF)
        hi, mid, lo = split3(jnp.where(lowt, top[1], top[0]) + jnp.log(lsw))
        f = jnp.where(lane == nb + 4, hi, jnp.where(lane == nb + 5, mid, lo))
        f_ref[rows, :] = jnp.where((lane >= nb + 4) & (lane < nb + 7), f.astype(BF), fq)


def attn_fwd(qkv, fq, fk, nb, p0, p1, into=()):
    n, w3 = qkv.shape
    w = w3 // 3
    pairs = w // PAIR
    blk = lambda off: pl.BlockSpec((n, PAIR), lambda p, off=off: (0, p + off))
    full = lambda a: pl.BlockSpec(a.shape, lambda p: (0, 0))

    def kern(*refs):
        attn_fwd_kernel(nb, *refs[:5], *refs[5 + len(into) :])

    return pl.pallas_call(
        kern,
        grid=(p1 - p0,),
        in_specs=[full(fq), full(fk), blk(p0), blk(pairs + p0), blk(2 * pairs + p0)] + [ANY] * len(into),
        out_specs=[blk(p0), blk(p0)],
        out_shape=[sds((n, w), BF)] * 2,
        input_output_aliases={5 + i: i for i in range(len(into))},
        compiler_params=params(28),
        cost_estimate=cost(16 * n * n * (p1 - p0) * PAIR, 12 * n * (p1 - p0) * PAIR, 2 * n * n * (p1 - p0)),
        name="attn_fwd",
    )(fq, fk, qkv, qkv, qkv, *into)


def attn_bwd_kernel(nb, fk_s, q_ref, k_ref, v_ref, f_ref, o_ref, do_ref, dq_ref, dk_ref, dv_ref, b_ref):
    n = q_ref.shape[0]
    t = 256
    low1 = lax.broadcasted_iota(jnp.int32, (n, PAIR), 1) < HEAD_DIM
    lane = lax.broadcasted_iota(jnp.int32, (n, PAIR), 1) % HEAD_DIM
    scale = jnp.asarray(HEAD_DIM**-0.5, BF)
    q = q_ref[...] * scale
    f = f_ref[...]
    do = do_ref[...]
    prod = do.astype(F32) * o_ref[...].astype(F32)
    d0 = jnp.sum(jnp.where(low1, prod, 0.0), axis=-1, keepdims=True)
    d1 = jnp.sum(jnp.where(low1, 0.0, prod), axis=-1, keepdims=True)
    hi, mid, lo = split3(jnp.where(low1, d1, d0))
    fd = jnp.where(lane == nb + 4, hi, jnp.where(lane == nb + 5, mid, jnp.where(lane == nb + 6, lo, 0.0))).astype(BF)
    qs = (jnp.where(low1, q, f), jnp.where(low1, f, q))
    dos = (jnp.where(low1, do, fd), jnp.where(low1, fd, do))
    kT = jnp.transpose(k_ref[...] * scale)
    lowt = lax.broadcasted_iota(jnp.int32, (t, PAIR), 1) < HEAD_DIM
    dqT = [None, None]
    dv_sum = jnp.zeros((1, PAIR), F32)
    for i in range(n // t):
        rows = pl.ds(i * t, t)
        k = k_ref[rows, :]
        v = v_ref[rows, :]
        fk = fk_s[rows, :]
        fv = jnp.where(fk == -1.0, fk, jnp.zeros_like(fk))
        dvh, dkh = [], []
        for h in range(2):
            kh = jnp.where(lowt, k, fk) if h == 0 else jnp.where(lowt, fk, k)
            vh = jnp.where(lowt, v, fv) if h == 0 else jnp.where(lowt, fv, v)
            p = jnp.exp(nt(kh, qs[h]))
            ds = (p * nt(vh, dos[h])).astype(BF)
            dvh.append(nn(p.astype(BF), do))
            dkh.append(nn(ds, q))
            part = nn(kT[h * HEAD_DIM : (h + 1) * HEAD_DIM, i * t : (i + 1) * t], ds)
            dqT[h] = part if dqT[h] is None else dqT[h] + part
        dk = jnp.where(lowt, dkh[0], dkh[1]).astype(BF)
        dv = jnp.where(lowt, dvh[0], dvh[1]).astype(BF)
        dk_ref[rows, :] = dk
        dv_ref[rows, :] = dv
        dv_sum = dv_sum + colsum(dv.astype(F32))
    dq = jnp.transpose(jnp.concatenate(dqT, axis=0)).astype(BF)
    dq_ref[...] = dq
    b_ref[...] = jnp.concatenate([colsum(dq.astype(F32)), dv_sum, jnp.zeros((6, PAIR), F32)], axis=0)


def attn_bwd(qkv, f, o, do, fk, nb, p0, p1, turn):
    n, w3 = qkv.shape
    pairs = w3 // 3 // PAIR
    cols = (p1 - p0) * PAIR
    blk = lambda off: pl.BlockSpec((n, PAIR), lambda p, off=off: (0, p + off))
    full = lambda a: pl.BlockSpec(a.shape, lambda p: (0,) * a.ndim)
    return pl.pallas_call(
        lambda turn_ref, *refs: attn_bwd_kernel(nb, *refs),
        grid=(p1 - p0,),
        in_specs=[SMEM, full(fk), blk(p0), blk(pairs + p0), blk(2 * pairs + p0), blk(p0), blk(p0), blk(p0)],
        out_specs=[blk(0), blk(0), blk(0), pl.BlockSpec((8, PAIR), lambda p: (0, p))],
        out_shape=[sds((n, cols), BF)] * 3 + [sds((8, cols), F32)],
        compiler_params=params(28),
        cost_estimate=cost(40 * n * n * cols, 20 * n * cols, n * n * cols // HEAD_DIM),
        name="attn_bwd",
    )(turn, fk, qkv, qkv, qkv, f, o, do)


def grad_qkv(x, parts, core, orders, small=()):
    n, d = x.shape
    blocks = orders.shape[1]
    np_ = len(parts)
    unit, rb = sum(p[0].shape[1] for p in parts) // 2, d // blocks
    rows = 3 * rb + (16 if small else 0)
    g = (blocks, rows, unit)
    ns = len(small)

    def kern(core_ref, ord_ref, x_ref, *refs):
        ds = [[refs[3 * p + part] for p in range(np_)] for part in range(3)]
        extra = refs[3 * np_ : 3 * np_ + ns]
        send_ref, keep_ref, g_s, osem = refs[3 * np_ + ns :]
        x = x_ref[...]
        sels = [1 - (core_ref[0] ^ h) for h in range(2)]
        cat = lambda rs: rs[0][...] if len(rs) == 1 else jnp.concatenate([r[...] for r in rs], axis=1)
        for part in range(3):
            r = tn(x, cat(ds[part])).astype(BF)
            for h in range(2):
                for a in range(blocks):
                    g_s[sels[h], ord_ref[h, a], part * rb : (part + 1) * rb, :] = r[a * rb : (a + 1) * rb, h * unit : (h + 1) * unit]
        if ns:
            vs_ref, bs_ref = extra[-2:]
            groups = bs_ref.shape[0]
            quarters = blocks // groups
            vec = jnp.concatenate([cat(extra[:-2])[0:2], vs_ref[2:8, :]], axis=0)
            share = d // groups
            for gr in range(groups):
                gs = slice(gr * share, (gr + 1) * share)
                lines = [jnp.concatenate([vec[2 * i : 2 * i + 1, gs], vec[2 * i + 1 : 2 * i + 2, gs]], axis=1) for i in range(4)]
                lines += [bs_ref[gr, 0:1, i * (d // 2) : (i + 1) * (d // 2)] for i in range(2)]
                for i in range(2 * quarters):
                    h, q = i // quarters, i % quarters
                    line = lines[i] if i < len(lines) else jnp.zeros((1, d // 2), F32)
                    pieces = [line[:, k * unit : (k + 1) * unit] for k in range(d // 2 // unit)]
                    tile = jnp.concatenate(pieces + [jnp.zeros((16 - len(pieces), unit), F32)], axis=0)
                    g_s[sels[h], ord_ref[h, gr * quarters + q], 3 * rb : 3 * rb + 16, :] = tile.astype(BF)
        out = [pltpu.make_async_copy(g_s.at[0], send_ref, osem.at[0]), pltpu.make_async_copy(g_s.at[1], keep_ref, osem.at[1])]
        for cp in out:
            cp.start()
        for cp in out:
            cp.wait()

    flat = [a for p in parts for a in p[:3]] + list(small)
    return pl.pallas_call(
        kern,
        in_specs=[SMEM, SMEM] + [VMEM] * (1 + len(flat)),
        out_specs=[ANY, ANY],
        out_shape=[sds(g, BF)] * 2,
        scratch_shapes=[pltpu.VMEM((2,) + g, BF), pltpu.SemaphoreType.DMA((2,))],
        compiler_params=params(28),
        cost_estimate=cost(12 * n * d * unit, 14 * n * d),
        name="grad_qkv",
    )(core, orders, x, *flat)


def norm(r, g, c):
    w = r.shape[-1]
    center = r - jnp.sum(r, axis=-1, keepdims=True) * (1.0 / w)
    inv = lax.rsqrt(jnp.sum(center * center, axis=-1, keepdims=True) * (1.0 / w) + norm_eps)
    n = center * inv
    return n * g + c, n, inv


def norm_back(dy, g, n, inv):
    w = dy.shape[-1]
    e = dy * g
    a = jnp.sum(e, axis=-1, keepdims=True) * (1.0 / w)
    b = jnp.sum(e * n, axis=-1, keepdims=True) * (1.0 / w)
    return inv * (e - a - n * b)


def colsum(a):
    return jnp.sum(a, axis=0, keepdims=True)


def pack_a(where, w, vec_t, bias):
    rows, cols = w.shape
    half = rows // 2

    def kern(where_ref, w_ref, vec_ref, bias_ref, out_ref):
        for h in range(2):
            pos = h ^ where_ref[1]
            out_ref[pos, 0:half, :] = w_ref[h * half : (h + 1) * half, :].astype(BF)
            small = vec_ref[...] if h == 0 else bias_ref[...]
            small = jnp.concatenate([small, jnp.zeros((small.shape[0], cols - small.shape[1]), F32)], axis=1)
            out_ref[pos, half : half + 16, :] = jnp.concatenate([small, small], axis=0).astype(BF)

    return pl.pallas_call(
        kern,
        in_specs=[SMEM, VMEM, VMEM, VMEM],
        out_specs=VMEM,
        out_shape=sds((2, half + 16, cols), BF),
        compiler_params=params(),
        cost_estimate=cost(0, 3 * w.size * 2),
        name="pack_a",
    )(where, w, vec_t, bias)


def pack_b(where, wo, wi, wd):
    rows, w = wo.shape
    half = rows // 2
    nf = wi.shape[1] // w
    nd = wd.shape[0] // rows

    def kern(where_ref, wo_ref, wi_ref, wd_ref, out_ref):
        for h in range(2):
            pos = h ^ where_ref[1]
            hs = slice(h * half, (h + 1) * half)
            out_ref[pos, 0] = wo_ref[hs, :].astype(BF)
            for j in range(nf):
                out_ref[pos, 1 + j] = wi_ref[hs, j * w : (j + 1) * w].astype(BF)
            for j in range(nd):
                at = (h * nd + j) * half
                out_ref[pos, 1 + nf + j] = wd_ref[at : at + half, :].astype(BF)

    return pl.pallas_call(
        kern,
        in_specs=[SMEM, VMEM, VMEM, VMEM],
        out_specs=VMEM,
        out_shape=sds((2, 1 + nf + nd, half, w), BF),
        compiler_params=params(),
        cost_estimate=cost(0, 6 * (wo.size + wi.size + wd.size)),
        name="pack_b",
    )(where, wo, wi, wd)


def pperm(a, pairs):
    return lax.ppermute(a, AX, pairs)


def after(late, *early):
    out = lax.optimization_barrier(tuple(late) + early)
    return out[: len(late) + 1]


def piece_refs(refs):
    out = []
    for ref in refs:
        out += [ref.at[k] for k in range(ref.shape[0])]
    return out


def project(x, table, parts, groups, t=256):
    n, d = x.shape
    _, hp, cols = parts[0].shape
    half = hp - 16
    share = 2 * half

    def kern(tab_ref, x_ref, *refs):
        pieces = piece_refs(refs[:5])
        qkv_ref, w_out, vec_ref, bias_ref, w_s, e_s, sems, osem = refs[5:]
        first = pl.program_id(0) == 0
        last = pl.program_id(0) == pl.num_programs(0) - 1

        def copies():
            out = []
            for i, p in enumerate(pieces):
                u = tab_ref[i]
                out.append(pltpu.make_async_copy(p.at[pl.ds(0, half)], w_s.at[pl.ds(pl.multiple_of(u * half, 16), half)], sems.at[2 * i]))
                out.append(pltpu.make_async_copy(p.at[pl.ds(half, 16)], e_s.at[u], sems.at[2 * i + 1]))
            return out

        def whole():
            return pltpu.make_async_copy(w_s, w_out, osem)

        @pl.when(first)
        def _():
            for cp in copies():
                cp.start()
            for cp in copies():
                cp.wait()
            whole().start()
            vec_ref[...] = jnp.concatenate([e_s[2 * g, 0:8, 0:share].astype(F32) for g in range(groups)], axis=1)
            for g in range(groups):
                bias_ref[g] = e_s[2 * g + 1, 0:8, 0:d].astype(F32)

        qb = jnp.concatenate([vec_ref[0:1, :], jnp.zeros((1, d), F32), vec_ref[1:2, :]], axis=1)
        qkv_ref[...] = (nn(x_ref[...], w_s[...]) + qb).astype(BF)

        @pl.when(last)
        def _():
            whole().wait()

    return pl.pallas_call(
        kern,
        grid=(n // t,),
        in_specs=[SMEM, pl.BlockSpec((t, d), lambda i: (i, 0))] + [ANY] * 5,
        out_specs=[pl.BlockSpec((t, cols), lambda i: (i, 0)), ANY, pl.BlockSpec((8, d), lambda i: (0, 0)), pl.BlockSpec((groups, 8, d), lambda i: (0, 0, 0))],
        out_shape=[sds((n, cols), BF), sds((d, cols), BF), sds((8, d), F32), sds((groups, 8, d), F32)],
        scratch_shapes=[pltpu.VMEM((d, cols), BF), pltpu.VMEM((2 * groups, 16, cols), BF), pltpu.SemaphoreType.DMA((16,)), pltpu.SemaphoreType.DMA],
        compiler_params=params(),
        cost_estimate=cost(2 * n * d * cols, 2 * (n * d + 2 * d * cols + n * cols)),
        name="project",
    )(table, x, *parts)


def token(x, dy, o, vec, bias, table, core, orders, parts):
    n, w = x.shape
    _, k9, half, _ = parts[0].shape
    nf = bias.shape[0]
    nd = k9 - 1 - nf
    ff = nf * w
    nblk = orders.shape[1]
    nq = nblk // nf
    unit = w // 2
    rb = w // nblk
    db = w // (2 * nq)
    t = n // 2

    def kern(tab_ref, core_ref, ord_ref, vec_ref, bias_ref, x_ref, dy_ref, o_ref, *refs):
        pieces = piece_refs(refs[:7])
        (y_ref, dr1_ref, do_ref, send_ref, keep_ref, vs_ref, bs_ref,
         wo_s, wi_s, wd_s, x_s, dy_s, o_s, n1_s, inv_s, x1b_s, hb_s, sl_s, acc_s, dfb_s, y_s, g_s, sems, isem, osem) = refs[7:]

        def copies(kind):
            out = []
            for i, p in enumerate(pieces):
                u = tab_ref[i]
                rows = pl.ds(pl.multiple_of(u * half, 16), half)
                if kind == 0:
                    out.append(pltpu.make_async_copy(p.at[0], wo_s.at[rows], sems.at[0, i]))
                elif kind == 1:
                    out.append(pltpu.make_async_copy(p.at[pl.ds(1, nf)], wi_s.at[:, rows], sems.at[1, i]))
                else:
                    out.append(pltpu.make_async_copy(p.at[pl.ds(1 + nf, nd)], wd_s.at[pl.ds(u * nd, nd)], sems.at[2, i]))
            return out

        c_o = pltpu.make_async_copy(o_ref, o_s, isem.at[0])
        c_x = pltpu.make_async_copy(x_ref, x_s, isem.at[1])
        c_dy = pltpu.make_async_copy(dy_ref, dy_s, isem.at[2])
        for cp in copies(0) + [c_o, c_x] + copies(1) + copies(2) + [c_dy]:
            cp.start()
        row = lambda j: vec_ref[j : j + 1, :]
        bo, g1, c1, bd, g2, c2 = [row(j) for j in range(2, 8)]
        per = wd_s.shape[0] // nf
        down = lambda j: wd_s[pl.ds(j * per, per)].reshape(w, w)
        for cp in copies(0) + [c_o, c_x]:
            cp.wait()

        def first(i, _):
            rows = pl.ds(pl.multiple_of(i * t, t), t)
            x1, n1, inv1 = norm(x_s[rows, :].astype(F32) + (nn(o_s[rows, :], wo_s[...]) + bo), g1, c1)
            n1_s[rows, :] = n1
            inv_s[rows, :] = jnp.broadcast_to(inv1, (t, 128))
            x1b_s[rows, :] = x1.astype(BF)
            acc_s[rows, :] = x1 + bd
            return 0

        lax.fori_loop(0, 2, first, 0)
        for cp in copies(1):
            cp.wait()

        def up(j, _):
            for i in range(2):
                rows = slice(i * t, (i + 1) * t)
                h = nn(x1b_s[rows, :], wi_s[j]) + bias_ref[j, 0:1, :]
                cdf = 0.5 * (1.0 + lax.erf(h * SQH))
                hb_s[j, rows, :] = (h * cdf).astype(BF)
                sl_s[j, rows, :] = (cdf + h * (jnp.exp(-0.5 * (h * h)) * PHI0)).astype(BF)
            return 0

        lax.fori_loop(0, nf, up, 0)
        for cp in copies(2) + [c_dy]:
            cp.wait()
        vs_ref[...] = jnp.zeros_like(vs_ref)

        def top(i, _):
            rows = pl.ds(pl.multiple_of(i * t, t), t)
            r2 = acc_s[rows, :]
            for j in range(nf):
                r2 = r2 + nn(hb_s[j, rows, :], down(j))
            y, n2, inv2 = norm(r2, g2, c2)
            y_s[rows, :] = y
            dyf = dy_s[rows, :].astype(F32)
            dr2 = norm_back(dyf, g2, n2, inv2)
            acc_s[rows, :] = dr2
            dfb_s[rows, :] = dr2.astype(BF)
            vs_ref[5:6, :] += colsum(dr2)
            vs_ref[6:7, :] += colsum(dyf * n2)
            vs_ref[7:8, :] += colsum(dyf)
            return 0

        lax.fori_loop(0, n // t, top, 0)
        c_y = pltpu.make_async_copy(y_s, y_ref, osem.at[0])
        c_y.start()

        def back(j, _):
            for i in range(2):
                rows = slice(i * t, (i + 1) * t)
                dh = (nt(dfb_s[rows, :], down(j)) * sl_s[j, rows, :].astype(F32)).astype(BF)
                sl_s[j, rows, :] = dh
                s = jnp.broadcast_to(colsum(dh.astype(F32)), (8, w))
                bs_ref[j] = s if i == 0 else bs_ref[j] + s
                acc_s[rows, :] += nt(dh, wi_s[j])
            gd = tn(hb_s[j], dfb_s[...]).astype(BF)
            for h in range(2):
                sel = 1 - (core_ref[0] ^ h)
                for q in range(nq):
                    r0 = (h * nq + q) * db
                    pos = ord_ref[h, j * nq + q]
                    for k in range(2):
                        g_s[sel, pos, k * db : (k + 1) * db, :] = gd[r0 : r0 + db, k * unit : (k + 1) * unit]
            gi = tn(x1b_s[...], sl_s[j]).astype(BF)
            h = j // (nf // 2)
            sel = 1 - (core_ref[0] ^ h)
            for a in range(nblk):
                pos = ord_ref[h, a]
                for k in range(2):
                    at = pl.multiple_of(2 * db + ((j % (nf // 2)) * 2 + k) * rb, 16)
                    g_s[sel, pos, pl.ds(at, rb), :] = gi[a * rb : (a + 1) * rb, k * unit : (k + 1) * unit]
            return 0

        lax.fori_loop(0, nf, back, 0)
        most = pl.ds(0, 2 * db + nf * rb)
        outs = [pltpu.make_async_copy(g_s.at[k, :, most], (send_ref, keep_ref)[k].at[:, most], osem.at[1 + k]) for k in range(2)]
        for cp in outs:
            cp.start()

        def leave(i):
            rows = pl.ds(pl.multiple_of(i * t, t), t)
            return [pltpu.make_async_copy(acc_s.at[rows], dr1_ref.at[rows], osem.at[5 + 2 * i]), pltpu.make_async_copy(dy_s.at[rows], do_ref.at[rows], osem.at[6 + 2 * i])]

        def low(i, _):
            rows = pl.ds(pl.multiple_of(i * t, t), t)
            dx1 = acc_s[rows, :]
            n1 = n1_s[rows, :]
            dr1 = norm_back(dx1, g1, n1, inv_s[rows, 0:1])
            acc_s[rows, :] = dr1
            dab = dr1.astype(BF)
            x_s[rows, :] = dab
            dy_s[rows, :] = nt(dab, wo_s[...]).astype(BF)
            vs_ref[2:3, :] += colsum(dr1)
            vs_ref[3:4, :] += colsum(dx1 * n1)
            vs_ref[4:5, :] += colsum(dx1)
            for cp in leave(i):
                cp.start()
            return 0

        lax.fori_loop(0, 2, low, 0)
        go = tn(o_s[...], x_s[...]).astype(BF)
        for h in range(2):
            sel = 1 - (core_ref[0] ^ h)
            for a in range(nblk):
                g_s[sel, ord_ref[h, a], 2 * db + nf * rb : 2 * db + (nf + 1) * rb, :] = go[a * rb : (a + 1) * rb, h * unit : (h + 1) * unit]
        last = pl.ds(2 * db + nf * rb, rb)
        more = [pltpu.make_async_copy(g_s.at[k, :, last], (send_ref, keep_ref)[k].at[:, last], osem.at[3 + k]) for k in range(2)]
        for cp in more:
            cp.start()
        for cp in [c_y] + outs + leave(0) + leave(1) + more:
            cp.wait()

    gs = (nblk, 2 * db + (nf + 1) * rb, unit)
    vm = lambda s, dt=BF: pltpu.VMEM(s, dt)
    return pl.pallas_call(
        kern,
        in_specs=[SMEM, SMEM, SMEM, VMEM, VMEM] + [ANY] * 10,
        out_specs=[ANY] * 5 + [VMEM, VMEM],
        out_shape=[sds((n, w), F32), sds((n, w), F32), sds((n, w), BF), sds(gs, BF), sds(gs, BF), sds((8, w), F32), sds((nf, 8, w), F32)],
        scratch_shapes=[vm((w, w)), vm((nf, w, w)), vm((ff // half, half, w)), vm((n, w)), vm((n, w)), vm((n, w)), vm((n, w), F32), vm((n, 128), F32),
                        vm((n, w)), vm((nf, n, w)), vm((nf, n, w)), vm((n, w), F32), vm((n, w)), vm((n, w), F32), vm((2,) + gs),
                        pltpu.SemaphoreType.DMA((3, 8)), pltpu.SemaphoreType.DMA((3,)), pltpu.SemaphoreType.DMA((9,))],
        compiler_params=params(),
        cost_estimate=cost(2 * n * w * (3 * w + 6 * ff), 2 * (n * 8 * w + 3 * w * (w + 2 * ff)), 2 * n * ff),
        name="token",
    )(table, core, orders, vec, bias, x, dy, o, *parts)


def grad_input(dr1, parts, w, turn, i0, i1, into=(), t=256):
    n, d = dr1.shape
    k = len(parts)

    def kern(turn_ref, r_ref, w_ref, *refs):
        out_ref = refs[-1]
        out = r_ref[...]
        for part in range(3):
            g = jnp.concatenate([refs[3 * p + part][...] for p in range(k)], axis=1)
            out = out + nt(g, w_ref[:, part * d : (part + 1) * d])
        out_ref[...] = out

    rows = lambda c: pl.BlockSpec((t, c), lambda i: (i + i0, 0))
    flat = [a for p in parts for a in p[:3]]
    return pl.pallas_call(
        kern,
        grid=(i1 - i0,),
        in_specs=[SMEM, rows(d), pl.BlockSpec(w.shape, lambda i: (0, 0))] + [rows(a.shape[1]) for a in flat] + [ANY] * len(into),
        out_specs=rows(d),
        out_shape=sds((n, d), F32),
        input_output_aliases={3 + len(flat): 0} if into else {},
        compiler_params=params(28),
        cost_estimate=cost(6 * (i1 - i0) * t * d * d, (i1 - i0) * t * d * 14 + 2 * w.size),
        name="grad_input",
    )(turn, dr1, w, *flat, *into)


def total(*terms):
    out = terms[0].astype(F32)
    for a in terms[1:]:
        out = out + a.astype(F32)
    return out.astype(BF)


def total_kernel(turn, n, *terms):
    block = terms[0][0].shape[1:]
    k = len(terms)

    def kern(turn_ref, *refs):
        ins, out_ref, scr, out_s, isem, osem = refs[:k], refs[k], refs[k + 1], refs[k + 2], refs[k + 3], refs[k + 4]

        def come(i):
            return [pltpu.make_async_copy(ins[t].at[terms[t][1] + i], scr.at[t, i], isem.at[t, i]) for t in range(k)]

        def go(i):
            return pltpu.make_async_copy(out_s.at[i], out_ref.at[i], osem.at[i])

        for i in range(n):
            for cp in come(i):
                cp.start()
        for i in range(n):
            for cp in come(i):
                cp.wait()
            out = scr[0, i].astype(F32)
            for t in range(1, k):
                out = out + scr[t, i].astype(F32)
            out_s[i] = out.astype(BF)
            go(i).start()
        for i in range(n):
            go(i).wait()

    return pl.pallas_call(
        kern,
        in_specs=[SMEM] + [ANY] * k,
        out_specs=ANY,
        out_shape=sds((n,) + block, BF),
        scratch_shapes=[pltpu.VMEM((k, n) + block, BF), pltpu.VMEM((n,) + block, BF), pltpu.SemaphoreType.DMA((k, n)), pltpu.SemaphoreType.DMA((n,))],
        compiler_params=params(16),
        cost_estimate=cost(10**9, 0),
        name="total",
    )(turn, *[a for a, _ in terms])


class Line:
    def __init__(self, mark, core):
        self.mark = mark
        self.core = core

    def hold(self, *arrays):
        out = lax.optimization_barrier(arrays + (self.mark,))
        return out[0] if len(arrays) == 1 else out[:-1]

    def add(self, n, *terms):
        held = (self.hold(terms[0][0]),) + tuple(a for a, _ in terms[1:])
        self.mark = total(*[a[first : first + n] for a, (_, first) in zip(held, terms)])
        return self.mark

    def add_kernel(self, n, *terms):
        self.mark = total_kernel(self.hold(self.core), n, *terms)
        return self.mark

    def join(self, a, b):
        self.mark = jnp.concatenate([self.hold(a), b], axis=0)
        return self.mark


def adam(w, m, u, g, decay):
    correct = 1.0 - 0.5**STEP
    m = 0.5 * m + 0.5 * g
    u = 0.5 * u + 0.5 * g * g
    return w - step_rate * (m * (1.0 / correct) / (jnp.sqrt(u * (1.0 / correct)) + adam_eps) + decay * w), m, u


def adam_some(spots, mine, other, mats, count, into=()):
    half = mine.shape[0]
    (w_down, _), (w_in, _), (w_out, _) = mats
    rd, ri, unit = w_down.shape[0] // 8, w_in.shape[0] // 4, mine.shape[2]
    ki = w_in.shape[1] // 2 // unit
    blocks = [(rd, w_down.shape[1]), (ri, w_in.shape[1] // 2), (ri, w_out.shape[1] // 2)]
    steps = 2 * half
    ni = len(into)

    def kern(spots_ref, a_ref, b_ref, *refs):
        olds, news = refs[:6], refs[6 + ni : 15 + ni]
        src_s, isem, osem = refs[15 + ni], refs[16 + ni], refs[17 + ni]
        bufs = [refs[18 + ni + 3 * k : 21 + ni + 3 * k] for k in range(3)]

        def place(k, s):
            h, q = spots_ref[2 * s], spots_ref[2 * s + 1]
            r, c = blocks[k]
            if k == 0:
                return pl.ds(pl.multiple_of((h * 4 + q) * r, 8), r), pl.ds(0, c)
            return pl.ds(pl.multiple_of(q * r, 8), r), pl.ds(pl.multiple_of(h * c, 128), c)

        def come(s):
            out = [pltpu.make_async_copy((a_ref, b_ref)[s // half].at[s % half], src_s.at[s], isem.at[s, 0])]
            for k in range(3):
                rows, cols = place(k, s)
                out.append(pltpu.make_async_copy(olds[2 * k].at[rows, cols], bufs[k][0].at[s], isem.at[s, 1 + 2 * k]))
                out.append(pltpu.make_async_copy(olds[2 * k + 1].at[:, rows, cols], bufs[k][1].at[s], isem.at[s, 2 + 2 * k]))
            return out

        def go(s):
            out = []
            for k in range(3):
                rows, cols = place(k, s)
                out.append(pltpu.make_async_copy(bufs[k][2].at[s], news[3 * k].at[rows, cols], osem.at[s, 3 * k]))
                out.append(pltpu.make_async_copy(bufs[k][0].at[s], news[3 * k + 1].at[rows, cols], osem.at[s, 3 * k + 1]))
                out.append(pltpu.make_async_copy(bufs[k][1].at[s], news[3 * k + 2].at[:, rows, cols], osem.at[s, 3 * k + 2]))
            return out

        for s in range(steps):
            for cp in come(s):
                cp.start()
        for s in range(steps):
            for cp in come(s):
                cp.wait()
            g = src_s[s].astype(F32) * count
            at = 2 * rd
            grads = [jnp.concatenate([g[:rd], g[rd:at]], axis=1),
                     jnp.concatenate([g[at + k * ri : at + (k + 1) * ri] for k in range(ki)], axis=1),
                     g[at + ki * ri : at + (ki + 1) * ri]]
            for k in range(3):
                w_s, m_s, g_s = bufs[k]
                g_s[s] = grads[k]
                w_s[s], m_s[s, 0], m_s[s, 1] = adam(w_s[s], m_s[s, 0], m_s[s, 1], grads[k], matrix_decay)
            for cp in go(s):
                cp.start()
        for s in range(steps):
            for cp in go(s):
                cp.wait()

    shapes, args, scratch = [], [], []
    for (w, m), b in zip(mats, blocks):
        shapes += [sds(w.shape, F32), sds(w.shape, F32), sds(m.shape, F32)]
        args += [w, m]
        scratch += [pltpu.VMEM((steps,) + b, F32), pltpu.VMEM((steps, 2) + b, F32), pltpu.VMEM((steps,) + b, F32)]
    size = sum(w.size for w, _ in mats) // 2
    return pl.pallas_call(
        kern,
        in_specs=[SMEM] + [ANY] * (8 + ni),
        out_specs=[ANY] * 9,
        out_shape=shapes,
        scratch_shapes=[pltpu.VMEM((steps,) + mine.shape[1:], BF), pltpu.SemaphoreType.DMA((steps, 7)), pltpu.SemaphoreType.DMA((steps, 9))] + scratch,
        input_output_aliases={9 + k: k for k in range(ni)},
        compiler_params=params(28),
        cost_estimate=cost(20 * size, 28 * size, 2 * size),
        name="adam_some",
    )(spots, mine, other, *args, *into)


def adam_qkv(core, mine, other, w, mom, count):
    rb, cols = w.shape[0] // 4, w.shape[1]

    def kern(core_ref, a_ref, b_ref, w_ref, m_ref, g_out, w_out, m_out, w_s, m_s, g_s, isem, osem):
        at = lambda s: pl.ds(s * rb, rb)

        def come(s):
            return [pltpu.make_async_copy(w_ref.at[at(s)], w_s.at[at(s)], isem.at[s, 0]),
                    pltpu.make_async_copy(m_ref.at[:, at(s)], m_s.at[:, at(s)], isem.at[s, 1])]

        def go(s):
            return [pltpu.make_async_copy(g_s.at[at(s)], g_out.at[at(s)], osem.at[s, 0]),
                    pltpu.make_async_copy(w_s.at[at(s)], w_out.at[at(s)], osem.at[s, 1]),
                    pltpu.make_async_copy(m_s.at[:, at(s)], m_out.at[:, at(s)], osem.at[s, 2])]

        for s in range(4):
            for cp in come(s):
                cp.start()
        flip = core_ref[0] == 1
        for s in range(4):
            for cp in come(s):
                cp.wait()
            a, b = a_ref[s, 0 : 3 * rb, :].astype(F32) * count, b_ref[s, 0 : 3 * rb, :].astype(F32) * count
            first, second = jnp.where(flip, b, a), jnp.where(flip, a, b)
            g = jnp.concatenate([v[p * rb : (p + 1) * rb] for p in range(3) for v in (first, second)], axis=1)
            rows = slice(s * rb, (s + 1) * rb)
            g_s[rows, :] = g
            w_s[rows, :], m_s[0, rows, :], m_s[1, rows, :] = adam(w_s[rows, :], m_s[0, rows, :], m_s[1, rows, :], g, matrix_decay)
            for cp in go(s):
                cp.start()
        for s in range(4):
            for cp in go(s):
                cp.wait()

    return pl.pallas_call(
        kern,
        in_specs=[SMEM, VMEM, VMEM, ANY, ANY],
        out_specs=[ANY] * 3,
        out_shape=[sds(w.shape, F32), sds(w.shape, F32), sds(mom.shape, F32)],
        scratch_shapes=[pltpu.VMEM(w.shape, F32), pltpu.VMEM(mom.shape, F32), pltpu.VMEM(w.shape, F32), pltpu.SemaphoreType.DMA((4, 2)), pltpu.SemaphoreType.DMA((4, 3))],
        compiler_params=params(28),
        cost_estimate=cost(20 * w.size, 28 * w.size, 2 * w.size),
        name="adam_qkv",
    )(core, mine, other, w, mom)


def permutations(groups, reps):
    flat = lambda f: [(g * reps + r, f(g, r)) for g in range(groups) for r in range(reps)]
    at = lambda g, r: g * reps + r
    far = []
    bit = 8
    while bit < reps:
        far.append(flat(lambda g, r, bit=bit: at(g, r ^ bit)))
        bit *= 2
    return {
        "core": flat(lambda g, r: at(g, r ^ 1)),
        "s1": flat(lambda g, r: at(g ^ (1 + r % 2), r)),
        "s2": flat(lambda g, r: at(g ^ (2 - r % 2), r)),
        "z1": flat(lambda g, r: at(g, r ^ (2 + 2 * (r % 2)))),
        "z2": flat(lambda g, r: at(g, r ^ (4 - 2 * (r % 2)))),
        "far": far,
        "cores": [[r for r in range(reps) if r % 2 == c] for c in range(2)],
    }


def local(groups, reps, hidden_in, out_grad, segment_ids, rand_blocks, w_qkv, w_out, w_in, w_down, vec_params, bias_hidden,
          moments_qkv, moments_out, moments_in, moments_down, moments_vec, moments_bias):
    perms = permutations(groups, reps)
    seqs, n, d = hidden_in.shape
    nb = rand_blocks.shape[1]
    g = lax.axis_index("group").astype(I32)
    r = lax.axis_index("rep").astype(I32)
    c, z = r % 2, (r // 2) % 4
    where = jnp.stack([g, c, z])
    one, two = 1 + c, 2 - c
    table = jnp.stack([2 * g + c, 2 * g + 1 - c, 2 * (g ^ one) + c, 2 * (g ^ one) + 1 - c,
                       2 * (g ^ two) + 1 - c, 2 * (g ^ two) + c, 2 * (g ^ 3) + c, 2 * (g ^ 3) + 1 - c])
    four = jnp.arange(4, dtype=I32)

    def turn(core, v):
        return jnp.where(core == 0, (v % 2) * 2 + v // 2, v)

    def order(core, quarters):
        return (turn(core, four ^ g)[:, None] * 4 + quarters[None, :]).reshape(16)

    core = c[None]
    orders = jnp.stack([order(k, turn(k, four ^ z)) for k in range(2)])
    plain = jnp.stack([order(k, four) for k in range(2)])
    spots = [jnp.stack([v for src in (c, 1 - c) for k in (p, p + 1) for v in (src, turn(src, jnp.int32(k)) ^ z)]) for p in (0, 2)]
    orders = jnp.where(orders < 8, orders, 8 + 4 * (orders % 4 // 2) + 2 * (orders // 4 % 2) + orders % 2)

    pa = pack_a(where, w_qkv, vec_params.T, jnp.broadcast_to(bias_hidden[None], (8, bias_hidden.shape[0])))
    near_a = pperm(pa, perms["s1"])
    wo_in, wi_in, wd_in, _ = after((w_out, w_in, w_down), pa)
    pb = pack_b(where, wo_in, wi_in, wd_in)
    x = hidden_in.reshape(n, d)
    dy = out_grad.reshape(n, d)
    seg_col = segment_ids.reshape(n, 1)
    rr = jnp.pad(rand_blocks[0].T, ((0, 0), (0, HEAD_DIM - nb)), constant_values=-1)
    rand_rows = jnp.concatenate([rr, rr], axis=1)

    fq, fk = attn_feats(seg_col, rand_rows, nb)
    near_a, _ = after((near_a,), table, orders, plain, fk, pb, *spots)
    far_a = pperm(near_a[0:1], perms["s2"])
    side_a = pperm(near_a, perms["core"])
    back_a = pperm(far_a, perms["core"])
    pb, _ = after((pb,), far_a)
    near_b0 = pperm(pb[0:1], perms["s1"])

    qkv, wq_full, vec, bias = project(x, table, (pa, near_a, side_a, far_a, back_a), groups)
    pb, _ = after((pb,), qkv)
    near_b1 = pperm(pb[1:2], perms["s1"])
    o1, f1 = attn_fwd(qkv, fq, fk, nb, 0, 3)
    near_b0, near_b1, o1 = after((near_b0, near_b1), o1)
    far_b = pperm(near_b0, perms["s2"])
    side_b0 = pperm(near_b0, perms["core"])
    qkv_l, _ = after((qkv,), near_b0)
    o, f = attn_fwd(qkv_l, fq, fk, nb, 3, 6, (o1, f1))
    side_b1 = pperm(near_b1, perms["core"])
    far_b, o = after((far_b,), o)
    back_b = pperm(far_b, perms["core"])
    y, dr1, do, send, keep, vs, bs = token(x, dy, o, vec, bias, table, core, orders, (pb, near_b0, near_b1, side_b0, side_b1, far_b, back_b))

    nblk = keep.shape[0]
    up, lo = nblk // 2, nblk // 4
    m, e = lo // 2, lo // 4
    s1, s2, z1, z2, swap = [lambda v, k=k: pperm(v, perms[k]) for k in ("s1", "s2", "z1", "z2", "core")]
    line = Line(vs, core)
    attend = lambda p0, p1: attn_bwd(qkv, f, o, do, fk, nb, p0, p1, line.hold(core))
    got = swap(send)
    part0 = attend(0, 2)
    line.mark = part0[3]
    x1a = s1(line.add(lo, (keep, up + lo), (got, up + lo)))
    part1 = attend(2, 4)
    line.mark = part1[3]
    x2a = s2(line.add(m, (keep, lo + m), (got, lo + m), (x1a, m)))
    x1b = s1(line.add(lo, (keep, up), (got, up)))
    part2 = attend(4, 6)
    line.mark = part2[3]
    v1 = z1(line.add(m, (keep, m), (got, m), (x1a, 0), (x2a, 0)))
    x2b = s2(line.add(m, (keep, lo), (got, lo), (x1b, m)))
    parts = (part0, part1, part2)
    send3, keep3 = grad_qkv(x, parts, line.hold(core), plain, tuple(p[3] for p in parts) + (vs, bs))
    line.mark = send3
    got3 = swap(send3)
    v2 = z2(line.add_kernel(e, (keep, e), (got, e), (x1b, e), (x2b, e), (v1, e)))
    x1_3 = s1(line.add(up, (keep3, up), (got3, up)))
    gin = grad_input(dr1, parts, wq_full, line.hold(core), 0, 2)
    line.mark = gin
    t0 = line.add(e, (keep, 0), (got, 0), (x1b, 0), (x2b, 0), (v1, 0), (v2, 0))
    for extra in perms["far"]:
        t0 = line.add(e, (t0, 0), (pperm(t0, extra), 0))
    t1 = z2(t0)
    gin = grad_input(dr1, parts, wq_full, line.hold(core), 2, 4, (gin,))
    line.mark = gin
    x2_3 = s2(line.add(lo, (keep3, lo), (got3, lo), (x1_3, lo)))
    t01 = line.join(t0, t1)
    t23 = z1(t01)
    u01 = swap(t01)
    sum3 = line.add(lo, (keep3, 0), (got3, 0), (x1_3, 0), (x2_3, 0))
    y1 = z1(sum3)
    count = 1.0 / (seqs * groups * reps)
    mats = ((w_down, moments_down), (w_in, moments_in), (w_out, moments_out))
    done = adam_some(line.hold(spots[0]), t01, u01, mats, count)
    line.mark = done[6]
    sum3 = line.add(lo, (sum3, 0), (y1, 0))
    y2 = z2(sum3)
    t23 = line.hold(t23)
    u23 = swap(t23)
    g_down, n_down, m_down, g_in, n_in, m_in, g_out, n_out, m_out = adam_some(line.hold(spots[1]), t23, u23, mats, count, done)
    line.mark = g_out
    sum3 = line.add(lo, (sum3, 0), (y2, 0))
    for extra in perms["far"]:
        sum3 = line.add(lo, (sum3, 0), (pperm(sum3, extra), 0))
    other3 = swap(sum3)
    g_qkv, n_qkv, m_qkv = adam_qkv(line.hold(core), sum3, other3, w_qkv, moments_qkv, count)

    rq = w_qkv.shape[0] // 4
    own, sib = [v[:, 3 * rq, :] for v in (sum3, other3)]
    rows8 = jnp.where(c == 0, jnp.concatenate([own, sib]), jnp.concatenate([sib, own])).astype(F32) * count
    g_vec = rows8[:4].reshape(8, d // groups).T
    g_bias = rows8[4:6].reshape(-1)
    n_vec, m1, u1 = adam(vec_params, moments_vec[0], moments_vec[1], g_vec, 0.0)
    n_bias, m2, u2 = adam(bias_hidden, moments_bias[0], moments_bias[1], g_bias, 0.0)
    return (y.reshape(hidden_in.shape), gin.reshape(hidden_in.shape), g_qkv, g_out, g_in, g_down, g_vec, g_bias,
            n_qkv, n_out, n_in, n_down, n_vec, n_bias, m_qkv, m_out, m_in, m_down, jnp.stack([m1, u1]), jnp.stack([m2, u2]))


def solution(mesh):
    groups, reps = mesh.shape["group"], mesh.shape["rep"]
    tok = P(AX, None, None)
    row, mom = P("group", None), P(None, "group", None)

    def run(*args):
        return local(groups, reps, *args)

    return jax.shard_map(
        run,
        mesh=mesh,
        in_specs=(tok, tok, P(AX, None), tok, row, row, row, row, row, P("group"), mom, mom, mom, mom, mom, P(None, "group")),
        out_specs=(tok, tok, row, row, row, row, row, P("group"), row, row, row, row, row, P("group"), mom, mom, mom, mom, mom, P(None, "group")),
        check_vma=False,
    )
```

```python
import jax
import jax.numpy as jnp
from jax import lax
from jax.experimental import pallas as pl
from jax.experimental.pallas import tpu as pltpu
from jax.sharding import PartitionSpec as P

HEAD_DIM = 64
STEP = 4
norm_eps = 1e-05
adam_eps = 1e-08
matrix_decay = 0.1
step_rate = 0.1
BF = jnp.bfloat16
F32 = jnp.float32
I32 = jnp.int32
NEG = -1e30
PAIR = 2 * HEAD_DIM
SQH = 0.7071067811865476
PHI0 = 0.3989422804014327
AX = ("group", "rep")
ANY = pl.BlockSpec(memory_space=pl.ANY)
SMEM = pl.BlockSpec(memory_space=pltpu.SMEM)
VMEM = pl.BlockSpec(memory_space=pltpu.VMEM)
sds = jax.ShapeDtypeStruct


def cost(flops, nbytes, trans=0):
    return pl.CostEstimate(flops=500 * int(flops), bytes_accessed=500 * int(nbytes), transcendentals=500 * int(trans))


def params(mb=60):
    return pltpu.CompilerParams(vmem_limit_bytes=mb * 1024 * 1024)

def nt(a, b):
    return lax.dot_general(a, b, (((1,), (1,)), ((), ())), preferred_element_type=F32)


def nn(a, b):
    return lax.dot_general(a, b, (((1,), (0,)), ((), ())), preferred_element_type=F32)


def tn(a, b):
    return lax.dot_general(a, b, (((0,), (0,)), ((), ())), preferred_element_type=F32)


def split3(v):
    hi = v.astype(BF).astype(F32)
    mid = (v - hi).astype(BF).astype(F32)
    return hi, mid, v - hi - mid


def attn_feats(seg_col, rand_rows, nb):
    n = seg_col.shape[0]

    def kern(seg_ref, rand_ref, fq_ref, fk_ref):
        lane = lax.broadcasted_iota(I32, (n, PAIR), 1) % HEAD_DIM
        blk = lax.broadcasted_iota(I32, (n, PAIR), 0) // (n // nb)
        seg = jnp.broadcast_to(seg_ref[...], (n, PAIR))
        fq = (lane == blk) | ((lane >= nb) & (lane - nb == seg))
        fq_ref[...] = jnp.where(fq, 1.0, 0.0).astype(BF)
        allow = (jnp.abs(lane - blk) <= 1) | (lane == 0) | (lane == nb - 1) | (blk == 0) | (blk == nb - 1)
        for j in range(rand_ref.shape[0]):
            allow = allow | (rand_ref[j : j + 1, :] == blk)
        bad = ((lane < nb) & jnp.logical_not(allow)) | ((lane >= nb) & (lane < nb + 4) & (lane - nb != seg))
        off = (lane >= nb + 4) & (lane < nb + 7)
        fk_ref[...] = jnp.where(bad, NEG, jnp.where(off, -1.0, 0.0)).astype(BF)

    return pl.pallas_call(
        kern,
        out_shape=[sds((n, PAIR), BF)] * 2,
        compiler_params=params(),
        cost_estimate=cost(20 * n * PAIR, 4 * n * PAIR),
        name="attn_feats",
    )(seg_col, rand_rows)


def attn_fwd_kernel(nb, fq_s, fk_s, q_ref, k_ref, v_ref, o_ref, f_ref):
    n = q_ref.shape[0]
    t = 256
    low1 = lax.broadcasted_iota(jnp.int32, (n, PAIR), 1) < HEAD_DIM
    k = k_ref[...]
    v = v_ref[...]
    fk = fk_s[...]
    one = jnp.ones((n, PAIR), BF)
    ks = (jnp.where(low1, k, fk), jnp.where(low1, fk, k))
    vs = (jnp.where(low1, v, one), jnp.where(low1, one, v))
    lowt = lax.broadcasted_iota(jnp.int32, (t, PAIR), 1) < HEAD_DIM
    lane = lax.broadcasted_iota(jnp.int32, (t, PAIR), 1) % HEAD_DIM
    for i in range(n // t):
        rows = pl.ds(i * t, t)
        q = q_ref[rows, :] * jnp.asarray(HEAD_DIM**-0.5, BF)
        fq = fq_s[rows, :]
        acc, top = [], []
        for h in range(2):
            qh = jnp.where(lowt, q, fq) if h == 0 else jnp.where(lowt, fq, q)
            s = nt(qh, ks[h])
            m = jnp.max(s, axis=-1, keepdims=True)
            p = jnp.exp(s - m).astype(BF)
            acc.append(nn(p, vs[h]))
            top.append(m)
        lsw = jnp.where(lowt, acc[1], acc[0])
        o = jnp.where(lowt, acc[0], acc[1]) / pltpu.roll(lsw, HEAD_DIM, 1)
        o_ref[rows, :] = o.astype(BF)
        hi, mid, lo = split3(jnp.where(lowt, top[1], top[0]) + jnp.log(lsw))
        f = jnp.where(lane == nb + 4, hi, jnp.where(lane == nb + 5, mid, lo))
        f_ref[rows, :] = jnp.where((lane >= nb + 4) & (lane < nb + 7), f.astype(BF), fq)


def attn_fwd(qkv, fq, fk, nb, p0, p1, into=()):
    n, w3 = qkv.shape
    w = w3 // 3
    pairs = w // PAIR
    blk = lambda off: pl.BlockSpec((n, PAIR), lambda p, off=off: (0, p + off))
    full = lambda a: pl.BlockSpec(a.shape, lambda p: (0, 0))

    def kern(*refs):
        attn_fwd_kernel(nb, *refs[:5], *refs[5 + len(into) :])

    return pl.pallas_call(
        kern,
        grid=(p1 - p0,),
        in_specs=[full(fq), full(fk), blk(p0), blk(pairs + p0), blk(2 * pairs + p0)] + [ANY] * len(into),
        out_specs=[blk(p0), blk(p0)],
        out_shape=[sds((n, w), BF)] * 2,
        input_output_aliases={5 + i: i for i in range(len(into))},
        compiler_params=params(28),
        cost_estimate=cost(16 * n * n * (p1 - p0) * PAIR, 12 * n * (p1 - p0) * PAIR, 2 * n * n * (p1 - p0)),
        name="attn_fwd",
    )(fq, fk, qkv, qkv, qkv, *into)


def attn_bwd_kernel(nb, fk_s, q_ref, k_ref, v_ref, f_ref, o_ref, do_ref, dq_ref, dk_ref, dv_ref, b_ref):
    n = q_ref.shape[0]
    t = 256
    low1 = lax.broadcasted_iota(jnp.int32, (n, PAIR), 1) < HEAD_DIM
    lane = lax.broadcasted_iota(jnp.int32, (n, PAIR), 1) % HEAD_DIM
    scale = jnp.asarray(HEAD_DIM**-0.5, BF)
    q = q_ref[...] * scale
    f = f_ref[...]
    do = do_ref[...]
    prod = do.astype(F32) * o_ref[...].astype(F32)
    d0 = jnp.sum(jnp.where(low1, prod, 0.0), axis=-1, keepdims=True)
    d1 = jnp.sum(jnp.where(low1, 0.0, prod), axis=-1, keepdims=True)
    hi, mid, lo = split3(jnp.where(low1, d1, d0))
    fd = jnp.where(lane == nb + 4, hi, jnp.where(lane == nb + 5, mid, jnp.where(lane == nb + 6, lo, 0.0))).astype(BF)
    qs = (jnp.where(low1, q, f), jnp.where(low1, f, q))
    dos = (jnp.where(low1, do, fd), jnp.where(low1, fd, do))
    kT = jnp.transpose(k_ref[...] * scale)
    lowt = lax.broadcasted_iota(jnp.int32, (t, PAIR), 1) < HEAD_DIM
    dqT = [None, None]
    dv_sum = jnp.zeros((1, PAIR), F32)
    for i in range(n // t):
        rows = pl.ds(i * t, t)
        k = k_ref[rows, :]
        v = v_ref[rows, :]
        fk = fk_s[rows, :]
        fv = jnp.where(fk == -1.0, fk, jnp.zeros_like(fk))
        dvh, dkh = [], []
        for h in range(2):
            kh = jnp.where(lowt, k, fk) if h == 0 else jnp.where(lowt, fk, k)
            vh = jnp.where(lowt, v, fv) if h == 0 else jnp.where(lowt, fv, v)
            p = jnp.exp(nt(kh, qs[h]))
            ds = (p * nt(vh, dos[h])).astype(BF)
            dvh.append(nn(p.astype(BF), do))
            dkh.append(nn(ds, q))
            part = nn(kT[h * HEAD_DIM : (h + 1) * HEAD_DIM, i * t : (i + 1) * t], ds)
            dqT[h] = part if dqT[h] is None else dqT[h] + part
        dk = jnp.where(lowt, dkh[0], dkh[1]).astype(BF)
        dv = jnp.where(lowt, dvh[0], dvh[1]).astype(BF)
        dk_ref[rows, :] = dk
        dv_ref[rows, :] = dv
        dv_sum = dv_sum + colsum(dv.astype(F32))
    dq = jnp.transpose(jnp.concatenate(dqT, axis=0)).astype(BF)
    dq_ref[...] = dq
    b_ref[...] = jnp.concatenate([colsum(dq.astype(F32)), dv_sum, jnp.zeros((6, PAIR), F32)], axis=0)


def attn_bwd(qkv, f, o, do, fk, nb, p0, p1, turn):
    n, w3 = qkv.shape
    pairs = w3 // 3 // PAIR
    cols = (p1 - p0) * PAIR
    blk = lambda off: pl.BlockSpec((n, PAIR), lambda p, off=off: (0, p + off))
    full = lambda a: pl.BlockSpec(a.shape, lambda p: (0,) * a.ndim)
    return pl.pallas_call(
        lambda turn_ref, *refs: attn_bwd_kernel(nb, *refs),
        grid=(p1 - p0,),
        in_specs=[SMEM, full(fk), blk(p0), blk(pairs + p0), blk(2 * pairs + p0), blk(p0), blk(p0), blk(p0)],
        out_specs=[blk(0), blk(0), blk(0), pl.BlockSpec((8, PAIR), lambda p: (0, p))],
        out_shape=[sds((n, cols), BF)] * 3 + [sds((8, cols), F32)],
        compiler_params=params(28),
        cost_estimate=cost(40 * n * n * cols, 20 * n * cols, n * n * cols // HEAD_DIM),
        name="attn_bwd",
    )(turn, fk, qkv, qkv, qkv, f, o, do)


def grad_qkv(x, parts, core, orders, small=()):
    n, d = x.shape
    blocks = orders.shape[1]
    np_ = len(parts)
    unit, rb = sum(p[0].shape[1] for p in parts) // 2, d // blocks
    rows = 3 * rb + (16 if small else 0)
    g = (blocks, rows, unit)
    ns = len(small)

    def kern(core_ref, ord_ref, x_ref, *refs):
        ds = [[refs[3 * p + part] for p in range(np_)] for part in range(3)]
        extra = refs[3 * np_ : 3 * np_ + ns]
        send_ref, keep_ref, g_s, osem = refs[3 * np_ + ns :]
        x = x_ref[...]
        sels = [1 - (core_ref[0] ^ h) for h in range(2)]
        cat = lambda rs: rs[0][...] if len(rs) == 1 else jnp.concatenate([r[...] for r in rs], axis=1)
        for part in range(3):
            r = tn(x, cat(ds[part])).astype(BF)
            for h in range(2):
                for a in range(blocks):
                    g_s[sels[h], ord_ref[h, a], part * rb : (part + 1) * rb, :] = r[a * rb : (a + 1) * rb, h * unit : (h + 1) * unit]
        if ns:
            vs_ref, bs_ref = extra[-2:]
            groups = bs_ref.shape[0]
            quarters = blocks // groups
            vec = jnp.concatenate([cat(extra[:-2])[0:2], vs_ref[2:8, :]], axis=0)
            share = d // groups
            for gr in range(groups):
                gs = slice(gr * share, (gr + 1) * share)
                lines = [jnp.concatenate([vec[2 * i : 2 * i + 1, gs], vec[2 * i + 1 : 2 * i + 2, gs]], axis=1) for i in range(4)]
                lines += [bs_ref[gr, 0:1, i * (d // 2) : (i + 1) * (d // 2)] for i in range(2)]
                for i in range(2 * quarters):
                    h, q = i // quarters, i % quarters
                    line = lines[i] if i < len(lines) else jnp.zeros((1, d // 2), F32)
                    pieces = [line[:, k * unit : (k + 1) * unit] for k in range(d // 2 // unit)]
                    tile = jnp.concatenate(pieces + [jnp.zeros((16 - len(pieces), unit), F32)], axis=0)
                    g_s[sels[h], ord_ref[h, gr * quarters + q], 3 * rb : 3 * rb + 16, :] = tile.astype(BF)
        out = [pltpu.make_async_copy(g_s.at[0], send_ref, osem.at[0]), pltpu.make_async_copy(g_s.at[1], keep_ref, osem.at[1])]
        for cp in out:
            cp.start()
        for cp in out:
            cp.wait()

    flat = [a for p in parts for a in p[:3]] + list(small)
    return pl.pallas_call(
        kern,
        in_specs=[SMEM, SMEM] + [VMEM] * (1 + len(flat)),
        out_specs=[ANY, ANY],
        out_shape=[sds(g, BF)] * 2,
        scratch_shapes=[pltpu.VMEM((2,) + g, BF), pltpu.SemaphoreType.DMA((2,))],
        compiler_params=params(28),
        cost_estimate=cost(12 * n * d * unit, 14 * n * d),
        name="grad_qkv",
    )(core, orders, x, *flat)


def norm(r, g, c):
    w = r.shape[-1]
    center = r - jnp.sum(r, axis=-1, keepdims=True) * (1.0 / w)
    inv = lax.rsqrt(jnp.sum(center * center, axis=-1, keepdims=True) * (1.0 / w) + norm_eps)
    n = center * inv
    return n * g + c, n, inv


def norm_back(dy, g, n, inv):
    w = dy.shape[-1]
    e = dy * g
    a = jnp.sum(e, axis=-1, keepdims=True) * (1.0 / w)
    b = jnp.sum(e * n, axis=-1, keepdims=True) * (1.0 / w)
    return inv * (e - a - n * b)


def colsum(a):
    return jnp.sum(a, axis=0, keepdims=True)


def pack_a(where, w, vec_t, bias):
    rows, cols = w.shape
    half = rows // 2

    def kern(where_ref, w_ref, vec_ref, bias_ref, *outs):
        for pos in range(2):
            h = pos ^ where_ref[1]
            outs[pos][0, 0:half, :] = w_ref[pl.ds(pl.multiple_of(h * half, 8), half), :].astype(BF)
            pad = lambda v: jnp.concatenate([v, jnp.zeros((v.shape[0], cols - v.shape[1]), F32)], axis=1)
            small = jnp.where(h == 0, pad(vec_ref[...]), pad(bias_ref[...]))
            outs[pos][0, half : half + 16, :] = jnp.concatenate([small, small], axis=0).astype(BF)

    return pl.pallas_call(
        kern,
        in_specs=[SMEM, VMEM, VMEM, VMEM],
        out_specs=[VMEM, VMEM],
        out_shape=[sds((1, half + 16, cols), BF)] * 2,
        compiler_params=params(28),
        cost_estimate=cost(0, 3 * w.size * 2),
        name="pack_a",
    )(where, w, vec_t, bias)


def pack_b(where, wo, wi, wd):
    rows, w = wo.shape
    half = rows // 2
    nf = wi.shape[1] // w
    nd = wd.shape[0] // rows

    def kern(where_ref, wo_ref, wi_ref, wd_ref, *outs):
        for pos in range(2):
            h = pos ^ where_ref[1]
            hs = pl.ds(pl.multiple_of(h * half, 8), half)
            outs[pos][0, 0] = wo_ref[hs, :].astype(BF)
            for j in range(nf):
                outs[pos][0, 1 + j] = wi_ref[hs, j * w : (j + 1) * w].astype(BF)
            for j in range(nd):
                at = pl.multiple_of((h * nd + j) * half, 8)
                outs[pos][0, 1 + nf + j] = wd_ref[pl.ds(at, half), :].astype(BF)
        part = pl.ds(pl.multiple_of(where_ref[2] % 2 * (half // 2), 16), half // 2)
        outs[2][...] = outs[1][:, :, part, :]

    blocks = 1 + nf + nd
    return pl.pallas_call(
        kern,
        in_specs=[SMEM, VMEM, VMEM, VMEM],
        out_specs=[VMEM] * 3,
        out_shape=[sds((1, blocks, half, w), BF)] * 2 + [sds((1, blocks, half // 2, w), BF)],
        compiler_params=params(28),
        cost_estimate=cost(0, 6 * (wo.size + wi.size + wd.size)),
        name="pack_b",
    )(where, wo, wi, wd)


def pperm(a, pairs):
    return lax.ppermute(a, AX, pairs)


def after(late, *early):
    out = lax.optimization_barrier(tuple(late) + early)
    return out[: len(late) + 1]


def piece_refs(refs):
    out = []
    for ref in refs:
        out += [ref.at[k] for k in range(ref.shape[0])]
    return out


def project(x, table, parts, groups, t=256):
    n, d = x.shape
    _, hp, cols = parts[0].shape
    half = hp - 16
    share = 2 * half

    def kern(tab_ref, x_ref, *refs):
        pieces = piece_refs(refs[:8])
        qkv_ref, w_out, vec_ref, bias_ref, w_s, e_s, sems, osem = refs[8:]
        first = pl.program_id(0) == 0
        last = pl.program_id(0) == pl.num_programs(0) - 1

        def copies():
            out = []
            for i, p in enumerate(pieces):
                u = tab_ref[i]
                out.append(pltpu.make_async_copy(p.at[pl.ds(0, half)], w_s.at[pl.ds(pl.multiple_of(u * half, 16), half)], sems.at[2 * i]))
                out.append(pltpu.make_async_copy(p.at[pl.ds(half, 16)], e_s.at[u], sems.at[2 * i + 1]))
            return out

        def whole():
            return pltpu.make_async_copy(w_s, w_out, osem)

        @pl.when(first)
        def _():
            for cp in copies():
                cp.start()
            for cp in copies():
                cp.wait()
            whole().start()
            vec_ref[...] = jnp.concatenate([e_s[2 * g, 0:8, 0:share].astype(F32) for g in range(groups)], axis=1)
            for g in range(groups):
                bias_ref[g] = e_s[2 * g + 1, 0:8, 0:d].astype(F32)

        qb = jnp.concatenate([vec_ref[0:1, :], jnp.zeros((1, d), F32), vec_ref[1:2, :]], axis=1)
        qkv_ref[...] = (nn(x_ref[...], w_s[...]) + qb).astype(BF)

        @pl.when(last)
        def _():
            whole().wait()

    return pl.pallas_call(
        kern,
        grid=(n // t,),
        in_specs=[SMEM, pl.BlockSpec((t, d), lambda i: (i, 0))] + [ANY] * 8,
        out_specs=[pl.BlockSpec((t, cols), lambda i: (i, 0)), ANY, pl.BlockSpec((8, d), lambda i: (0, 0)), pl.BlockSpec((groups, 8, d), lambda i: (0, 0, 0))],
        out_shape=[sds((n, cols), BF), sds((d, cols), BF), sds((8, d), F32), sds((groups, 8, d), F32)],
        scratch_shapes=[pltpu.VMEM((d, cols), BF), pltpu.VMEM((2 * groups, 16, cols), BF), pltpu.SemaphoreType.DMA((16,)), pltpu.SemaphoreType.DMA],
        compiler_params=params(),
        cost_estimate=cost(2 * n * d * cols, 2 * (n * d + 2 * d * cols + n * cols)),
        name="project",
    )(table, x, *parts)


def token(x, dy, o, vec, bias, table, core, orders, parts):
    n, w = x.shape
    _, k9, half, _ = parts[0].shape
    nf = bias.shape[0]
    nd = k9 - 1 - nf
    ff = nf * w
    nblk = orders.shape[1]
    nq = nblk // nf
    unit = w // 2
    rb = w // nblk
    db = w // (2 * nq)
    t = n // 2

    def kern(tab_ref, core_ref, ord_ref, vec_ref, bias_ref, x_ref, dy_ref, o_ref, *refs):
        parity = core_ref[1]
        whole, upper = [(0, 0), (1, 1), (2, 2), (3, 4), (4, 6), (5, 7)], [(6, 3, parity), (7, 3, 1 - parity), (8, 5, parity), (9, 5, 1 - parity)]
        pieces = [(refs[k].at[0], tab_ref[u], 0, half) for k, u in whole] + [(refs[k].at[0], tab_ref[u], p * (half // 2), half // 2) for k, u, p in upper]
        (y_ref, dr1_ref, do_ref, send_ref, keep_ref, vs_ref, bs_ref,
         wo_s, wi_s, wd_s, x_s, dy_s, o_s, n1_s, inv_s, x1b_s, hb_s, sl_s, acc_s, dfb_s, y_s, g_s, sems, isem, osem) = refs[10:]

        def copies(kind):
            out = []
            for i, (p, u, r0, size) in enumerate(pieces):
                rows = pl.ds(pl.multiple_of(u * half + r0, 16), size)
                if kind == 0:
                    out.append(pltpu.make_async_copy(p.at[0], wo_s.at[rows], sems.at[0, i]))
                elif kind == 1:
                    out.append(pltpu.make_async_copy(p.at[pl.ds(1, nf)], wi_s.at[:, rows], sems.at[1, i]))
                else:
                    out.append(pltpu.make_async_copy(p.at[pl.ds(1 + nf, nd)], wd_s.at[pl.ds(u * nd, nd), pl.ds(pl.multiple_of(r0, 16), size)], sems.at[2, i]))
            return out

        c_o = pltpu.make_async_copy(o_ref, o_s, isem.at[0])
        c_x = pltpu.make_async_copy(x_ref, x_s, isem.at[1])
        c_dy = pltpu.make_async_copy(dy_ref, dy_s, isem.at[2])
        for cp in copies(0) + [c_o, c_x] + copies(1) + copies(2) + [c_dy]:
            cp.start()
        row = lambda j: vec_ref[j : j + 1, :]
        bo, g1, c1, bd, g2, c2 = [row(j) for j in range(2, 8)]
        per = wd_s.shape[0] // nf
        down = lambda j: wd_s[pl.ds(j * per, per)].reshape(w, w)
        for cp in copies(0) + [c_o, c_x]:
            cp.wait()

        def first(i, _):
            rows = pl.ds(pl.multiple_of(i * t, t), t)
            x1, n1, inv1 = norm(x_s[rows, :].astype(F32) + (nn(o_s[rows, :], wo_s[...]) + bo), g1, c1)
            n1_s[rows, :] = n1
            inv_s[rows, :] = jnp.broadcast_to(inv1, (t, 128))
            x1b_s[rows, :] = x1.astype(BF)
            acc_s[rows, :] = x1 + bd
            return 0

        lax.fori_loop(0, 2, first, 0)
        for cp in copies(1):
            cp.wait()

        def up(j, _):
            for i in range(2):
                rows = slice(i * t, (i + 1) * t)
                h = nn(x1b_s[rows, :], wi_s[j]) + bias_ref[j, 0:1, :]
                cdf = 0.5 * (1.0 + lax.erf(h * SQH))
                hb_s[j, rows, :] = (h * cdf).astype(BF)
                sl_s[j, rows, :] = (cdf + h * (jnp.exp(-0.5 * (h * h)) * PHI0)).astype(BF)
            return 0

        lax.fori_loop(0, nf, up, 0)
        for cp in copies(2) + [c_dy]:
            cp.wait()
        vs_ref[...] = jnp.zeros_like(vs_ref)

        def top(i, _):
            rows = pl.ds(pl.multiple_of(i * t, t), t)
            r2 = acc_s[rows, :]
            for j in range(nf):
                r2 = r2 + nn(hb_s[j, rows, :], down(j))
            y, n2, inv2 = norm(r2, g2, c2)
            y_s[rows, :] = y
            dyf = dy_s[rows, :].astype(F32)
            dr2 = norm_back(dyf, g2, n2, inv2)
            acc_s[rows, :] = dr2
            dfb_s[rows, :] = dr2.astype(BF)
            vs_ref[5:6, :] += colsum(dr2)
            vs_ref[6:7, :] += colsum(dyf * n2)
            vs_ref[7:8, :] += colsum(dyf)
            return 0

        lax.fori_loop(0, n // t, top, 0)
        c_y = pltpu.make_async_copy(y_s, y_ref, osem.at[0])
        c_y.start()

        def back(j, _):
            for i in range(2):
                rows = slice(i * t, (i + 1) * t)
                dh = (nt(dfb_s[rows, :], down(j)) * sl_s[j, rows, :].astype(F32)).astype(BF)
                sl_s[j, rows, :] = dh
                s = jnp.broadcast_to(colsum(dh.astype(F32)), (8, w))
                bs_ref[j] = s if i == 0 else bs_ref[j] + s
                acc_s[rows, :] += nt(dh, wi_s[j])
            gd = tn(hb_s[j], dfb_s[...]).astype(BF)
            for h in range(2):
                sel = 1 - (core_ref[0] ^ h)
                for q in range(nq):
                    r0 = (h * nq + q) * db
                    pos = ord_ref[h, j * nq + q]
                    for k in range(2):
                        g_s[sel, pos, k * db : (k + 1) * db, :] = gd[r0 : r0 + db, k * unit : (k + 1) * unit]
            gi = tn(x1b_s[...], sl_s[j]).astype(BF)
            h = j // (nf // 2)
            sel = 1 - (core_ref[0] ^ h)
            for a in range(nblk):
                pos = ord_ref[h, a]
                for k in range(2):
                    at = pl.multiple_of(2 * db + ((j % (nf // 2)) * 2 + k) * rb, 16)
                    g_s[sel, pos, pl.ds(at, rb), :] = gi[a * rb : (a + 1) * rb, k * unit : (k + 1) * unit]
            return 0

        lax.fori_loop(0, nf, back, 0)
        most = pl.ds(0, 2 * db + nf * rb)
        outs = [pltpu.make_async_copy(g_s.at[k, :, most], (send_ref, keep_ref)[k].at[:, most], osem.at[1 + k]) for k in range(2)]
        for cp in outs:
            cp.start()

        def leave(i):
            rows = pl.ds(pl.multiple_of(i * t, t), t)
            return [pltpu.make_async_copy(acc_s.at[rows], dr1_ref.at[rows], osem.at[5 + 2 * i]), pltpu.make_async_copy(dy_s.at[rows], do_ref.at[rows], osem.at[6 + 2 * i])]

        def low(i, _):
            rows = pl.ds(pl.multiple_of(i * t, t), t)
            dx1 = acc_s[rows, :]
            n1 = n1_s[rows, :]
            dr1 = norm_back(dx1, g1, n1, inv_s[rows, 0:1])
            acc_s[rows, :] = dr1
            dab = dr1.astype(BF)
            x_s[rows, :] = dab
            dy_s[rows, :] = nt(dab, wo_s[...]).astype(BF)
            vs_ref[2:3, :] += colsum(dr1)
            vs_ref[3:4, :] += colsum(dx1 * n1)
            vs_ref[4:5, :] += colsum(dx1)
            for cp in leave(i):
                cp.start()
            return 0

        lax.fori_loop(0, 2, low, 0)
        go = tn(o_s[...], x_s[...]).astype(BF)
        for h in range(2):
            sel = 1 - (core_ref[0] ^ h)
            for a in range(nblk):
                g_s[sel, ord_ref[h, a], 2 * db + nf * rb : 2 * db + (nf + 1) * rb, :] = go[a * rb : (a + 1) * rb, h * unit : (h + 1) * unit]
        last = pl.ds(2 * db + nf * rb, rb)
        more = [pltpu.make_async_copy(g_s.at[k, :, last], (send_ref, keep_ref)[k].at[:, last], osem.at[3 + k]) for k in range(2)]
        for cp in more:
            cp.start()
        for cp in [c_y] + outs + leave(0) + leave(1) + more:
            cp.wait()

    gs = (nblk, 2 * db + (nf + 1) * rb, unit)
    vm = lambda s, dt=BF: pltpu.VMEM(s, dt)
    return pl.pallas_call(
        kern,
        in_specs=[SMEM, SMEM, SMEM, VMEM, VMEM] + [ANY] * 13,
        out_specs=[ANY] * 5 + [VMEM, VMEM],
        out_shape=[sds((n, w), F32), sds((n, w), F32), sds((n, w), BF), sds(gs, BF), sds(gs, BF), sds((8, w), F32), sds((nf, 8, w), F32)],
        scratch_shapes=[vm((w, w)), vm((nf, w, w)), vm((ff // half, half, w)), vm((n, w)), vm((n, w)), vm((n, w)), vm((n, w), F32), vm((n, 128), F32),
                        vm((n, w)), vm((nf, n, w)), vm((nf, n, w)), vm((n, w), F32), vm((n, w)), vm((n, w), F32), vm((2,) + gs),
                        pltpu.SemaphoreType.DMA((3, 10)), pltpu.SemaphoreType.DMA((3,)), pltpu.SemaphoreType.DMA((9,))],
        compiler_params=params(),
        cost_estimate=cost(2 * n * w * (3 * w + 6 * ff), 2 * (n * 8 * w + 3 * w * (w + 2 * ff)), 2 * n * ff),
        name="token",
    )(table, core, orders, vec, bias, x, dy, o, *parts)


def grad_input(dr1, parts, w, turn, t=256):
    n, d = dr1.shape
    k = len(parts)

    def kern(turn_ref, r_ref, w_ref, *refs):
        out_ref = refs[-1]
        out = r_ref[...]
        for part in range(3):
            g = jnp.concatenate([refs[3 * p + part][...] for p in range(k)], axis=1)
            out = out + nt(g, w_ref[:, part * d : (part + 1) * d])
        out_ref[...] = out

    rows = lambda c: pl.BlockSpec((t, c), lambda i: (i, 0))
    flat = [a for p in parts for a in p[:3]]
    return pl.pallas_call(
        kern,
        grid=(n // t,),
        in_specs=[SMEM, rows(d), pl.BlockSpec(w.shape, lambda i: (0, 0))] + [rows(a.shape[1]) for a in flat],
        out_specs=rows(d),
        out_shape=sds((n, d), F32),
        compiler_params=params(28),
        cost_estimate=cost(6 * n * d * d, n * d * 14 + 2 * w.size),
        name="grad_input",
    )(turn, dr1, w, *flat)


def total(*terms):
    out = terms[0].astype(F32)
    for a in terms[1:]:
        out = out + a.astype(F32)
    return out.astype(BF)


def total_kernel(turn, n, *terms):
    block = terms[0][0].shape[1:]
    k = len(terms)

    def kern(turn_ref, *refs):
        ins, out_ref, scr, out_s, isem, osem = refs[:k], refs[k], refs[k + 1], refs[k + 2], refs[k + 3], refs[k + 4]

        def come(i):
            return [pltpu.make_async_copy(ins[t].at[terms[t][1] + i], scr.at[t, i], isem.at[t, i]) for t in range(k)]

        def go(i):
            return pltpu.make_async_copy(out_s.at[i], out_ref.at[i], osem.at[i])

        for i in range(n):
            for cp in come(i):
                cp.start()
        for i in range(n):
            for cp in come(i):
                cp.wait()
            out = scr[0, i].astype(F32)
            for t in range(1, k):
                out = out + scr[t, i].astype(F32)
            out_s[i] = out.astype(BF)
            go(i).start()
        for i in range(n):
            go(i).wait()

    return pl.pallas_call(
        kern,
        in_specs=[SMEM] + [ANY] * k,
        out_specs=ANY,
        out_shape=sds((n,) + block, BF),
        scratch_shapes=[pltpu.VMEM((k, n) + block, BF), pltpu.VMEM((n,) + block, BF), pltpu.SemaphoreType.DMA((k, n)), pltpu.SemaphoreType.DMA((n,))],
        compiler_params=params(16),
        cost_estimate=cost(10**9, 0),
        name="total",
    )(turn, *[a for a, _ in terms])


class Line:
    def __init__(self, mark, core):
        self.mark = mark
        self.core = core

    def hold(self, *arrays):
        out = lax.optimization_barrier(arrays + (self.mark,))
        return out[0] if len(arrays) == 1 else out[:-1]

    def add(self, n, *terms):
        held = (self.hold(terms[0][0]),) + tuple(a for a, _ in terms[1:])
        self.mark = total(*[a[first : first + n] for a, (_, first) in zip(held, terms)])
        return self.mark

    def add_kernel(self, n, *terms):
        self.mark = total_kernel(self.hold(self.core), n, *terms)
        return self.mark

    def join(self, a, b):
        self.mark = jnp.concatenate([self.hold(a), b], axis=0)
        return self.mark


def adam(w, m, u, g, decay):
    correct = 1.0 - 0.5**STEP
    m = 0.5 * m + 0.5 * g
    u = 0.5 * u + 0.5 * g * g
    return w - step_rate * (m * (1.0 / correct) / (jnp.sqrt(u * (1.0 / correct)) + adam_eps) + decay * w), m, u


def adam_some(spots, mine, other, mats, count, into=()):
    half = mine.shape[0]
    (w_down, _), (w_in, _), (w_out, _) = mats
    rd, ri, unit = w_down.shape[0] // 8, w_in.shape[0] // 4, mine.shape[2]
    ki = w_in.shape[1] // 2 // unit
    blocks = [(rd, w_down.shape[1]), (ri, w_in.shape[1] // 2), (ri, w_out.shape[1] // 2)]
    steps = 2 * half
    ni = len(into)

    def kern(spots_ref, a_ref, b_ref, *refs):
        olds, news = refs[:6], refs[6 + ni : 15 + ni]
        src_s, isem, osem = refs[15 + ni], refs[16 + ni], refs[17 + ni]
        bufs = [refs[18 + ni + 3 * k : 21 + ni + 3 * k] for k in range(3)]

        def place(k, s):
            h, q = spots_ref[2 * s], spots_ref[2 * s + 1]
            r, c = blocks[k]
            if k == 0:
                return pl.ds(pl.multiple_of((h * 4 + q) * r, 8), r), pl.ds(0, c)
            return pl.ds(pl.multiple_of(q * r, 8), r), pl.ds(pl.multiple_of(h * c, 128), c)

        def come(s):
            out = [pltpu.make_async_copy((a_ref, b_ref)[s // half].at[s % half], src_s.at[s], isem.at[s, 0])]
            for k in range(3):
                rows, cols = place(k, s)
                out.append(pltpu.make_async_copy(olds[2 * k].at[rows, cols], bufs[k][0].at[s], isem.at[s, 1 + 2 * k]))
                out.append(pltpu.make_async_copy(olds[2 * k + 1].at[:, rows, cols], bufs[k][1].at[s], isem.at[s, 2 + 2 * k]))
            return out

        def go(s):
            out = []
            for k in range(3):
                rows, cols = place(k, s)
                out.append(pltpu.make_async_copy(bufs[k][2].at[s], news[3 * k].at[rows, cols], osem.at[s, 3 * k]))
                out.append(pltpu.make_async_copy(bufs[k][0].at[s], news[3 * k + 1].at[rows, cols], osem.at[s, 3 * k + 1]))
                out.append(pltpu.make_async_copy(bufs[k][1].at[s], news[3 * k + 2].at[:, rows, cols], osem.at[s, 3 * k + 2]))
            return out

        for s in range(steps):
            for cp in come(s):
                cp.start()
        for s in range(steps):
            for cp in come(s):
                cp.wait()
            g = src_s[s].astype(F32) * count
            at = 2 * rd
            grads = [jnp.concatenate([g[:rd], g[rd:at]], axis=1),
                     jnp.concatenate([g[at + k * ri : at + (k + 1) * ri] for k in range(ki)], axis=1),
                     g[at + ki * ri : at + (ki + 1) * ri]]
            for k in range(3):
                w_s, m_s, g_s = bufs[k]
                g_s[s] = grads[k]
                w_s[s], m_s[s, 0], m_s[s, 1] = adam(w_s[s], m_s[s, 0], m_s[s, 1], grads[k], matrix_decay)
            for cp in go(s):
                cp.start()
        for s in range(steps):
            for cp in go(s):
                cp.wait()

    shapes, args, scratch = [], [], []
    for (w, m), b in zip(mats, blocks):
        shapes += [sds(w.shape, F32), sds(w.shape, F32), sds(m.shape, F32)]
        args += [w, m]
        scratch += [pltpu.VMEM((steps,) + b, F32), pltpu.VMEM((steps, 2) + b, F32), pltpu.VMEM((steps,) + b, F32)]
    size = sum(w.size for w, _ in mats) // 2
    return pl.pallas_call(
        kern,
        in_specs=[SMEM] + [ANY] * (8 + ni),
        out_specs=[ANY] * 9,
        out_shape=shapes,
        scratch_shapes=[pltpu.VMEM((steps,) + mine.shape[1:], BF), pltpu.SemaphoreType.DMA((steps, 7)), pltpu.SemaphoreType.DMA((steps, 9))] + scratch,
        input_output_aliases={9 + k: k for k in range(ni)},
        compiler_params=params(28),
        cost_estimate=cost(20 * size, 28 * size, 2 * size),
        name="adam_some",
    )(spots, mine, other, *args, *into)


def adam_qkv(core, mine, other, w, mom, vec, mom_vec, bias, mom_bias, count):
    rb, cols = w.shape[0] // 4, w.shape[1]
    unit = mine.shape[2]
    share = vec.shape[1]

    def kern(core_ref, a_ref, b_ref, w_ref, m_ref, v_ref, mv_ref, c_ref, mc_ref,
             g_out, w_out, m_out, gv_out, v_out, mv_out, gc_out, c_out, mc_out, w_s, m_s, g_s, isem, osem):
        at = lambda s: pl.ds(s * rb, rb)

        def come(s):
            return [pltpu.make_async_copy(w_ref.at[at(s)], w_s.at[at(s)], isem.at[s, 0]),
                    pltpu.make_async_copy(m_ref.at[:, at(s)], m_s.at[:, at(s)], isem.at[s, 1])]

        def go(s):
            return [pltpu.make_async_copy(g_s.at[at(s)], g_out.at[at(s)], osem.at[s, 0]),
                    pltpu.make_async_copy(w_s.at[at(s)], w_out.at[at(s)], osem.at[s, 1]),
                    pltpu.make_async_copy(m_s.at[:, at(s)], m_out.at[:, at(s)], osem.at[s, 2])]

        for s in range(4):
            for cp in come(s):
                cp.start()
        flip = core_ref[0] == 1
        for s in range(4):
            for cp in come(s):
                cp.wait()
            a, b = a_ref[s, 0 : 3 * rb, :].astype(F32) * count, b_ref[s, 0 : 3 * rb, :].astype(F32) * count
            first, second = jnp.where(flip, b, a), jnp.where(flip, a, b)
            g = jnp.concatenate([v[p * rb : (p + 1) * rb] for p in range(3) for v in (first, second)], axis=1)
            rows = slice(s * rb, (s + 1) * rb)
            g_s[rows, :] = g
            w_s[rows, :], m_s[0, rows, :], m_s[1, rows, :] = adam(w_s[rows, :], m_s[0, rows, :], m_s[1, rows, :], g, matrix_decay)
            for cp in go(s):
                cp.start()
        line = lambda ref: [ref[q, 3 * rb : 3 * rb + 8, :].astype(F32)[0:1] * count for q in range(4)]
        own, sib = line(a_ref), line(b_ref)
        first, second = [jnp.where(flip, y, x) for x, y in zip(own, sib)], [jnp.where(flip, x, y) for x, y in zip(own, sib)]
        g = jnp.concatenate([v[:, k * share : (k + 1) * share] for v in first for k in range(unit // share)], axis=0)
        gv_out[...] = g
        v_out[...], mv_out[0], mv_out[1] = adam(v_ref[...], mv_ref[0], mv_ref[1], g, 0.0)
        for k in range(2):
            ks = slice(k * unit, (k + 1) * unit)
            n_c, mc_out[0:1, ks], mc_out[1:2, ks] = adam(c_ref[ks].reshape(1, unit), mc_ref[0:1, ks], mc_ref[1:2, ks], second[k], 0.0)
            gc_out[ks] = second[k].reshape(unit)
            c_out[ks] = n_c.reshape(unit)
        for s in range(4):
            for cp in go(s):
                cp.wait()

    like = lambda *vs: [sds(v.shape, F32) for v in vs]
    out = pl.pallas_call(
        kern,
        in_specs=[SMEM, VMEM, VMEM, ANY, ANY, VMEM, VMEM, VMEM, VMEM],
        out_specs=[ANY] * 3 + [VMEM] * 6,
        out_shape=like(w, w, mom, vec, vec, mom_vec, bias, bias, mom_bias),
        scratch_shapes=[pltpu.VMEM(w.shape, F32), pltpu.VMEM(mom.shape, F32), pltpu.VMEM(w.shape, F32), pltpu.SemaphoreType.DMA((4, 2)), pltpu.SemaphoreType.DMA((4, 3))],
        compiler_params=params(28),
        cost_estimate=cost(20 * w.size, 28 * w.size, 2 * w.size),
        name="adam_qkv",
    )(core, mine, other, w, mom, vec, mom_vec, bias, mom_bias)
    return out


def permutations(groups, reps):
    flat = lambda f: [(g * reps + r, f(g, r)) for g in range(groups) for r in range(reps)]
    at = lambda g, r: g * reps + r
    far = []
    bit = 8
    while bit < reps:
        far.append(flat(lambda g, r, bit=bit: at(g, r ^ bit)))
        bit *= 2
    return {
        "core": flat(lambda g, r: at(g, r ^ 1)),
        "s1": flat(lambda g, r: at(g ^ (1 + r % 2), r)),
        "s2": flat(lambda g, r: at(g ^ (2 - r % 2), r)),
        "z1": flat(lambda g, r: at(g, r ^ (2 + 2 * (r % 2)))),
        "z2": flat(lambda g, r: at(g, r ^ (4 - 2 * (r % 2)))),
        "twin": flat(lambda g, r: at(g, r ^ 2)),
        "far": far,
        "cores": [[r for r in range(reps) if r % 2 == c] for c in range(2)],
    }


def local(groups, reps, hidden_in, out_grad, segment_ids, rand_blocks, w_qkv, w_out, w_in, w_down, vec_params, bias_hidden,
          moments_qkv, moments_out, moments_in, moments_down, moments_vec, moments_bias):
    perms = permutations(groups, reps)
    seqs, n, d = hidden_in.shape
    nb = rand_blocks.shape[1]
    g = lax.axis_index("group").astype(I32)
    r = lax.axis_index("rep").astype(I32)
    c, z = r % 2, (r // 2) % 4
    where = jnp.stack([g, c, z])
    one, two = 1 + c, 2 - c
    table = jnp.stack([2 * g + c, 2 * g + 1 - c, 2 * (g ^ one) + c, 2 * (g ^ one) + 1 - c,
                       2 * (g ^ two) + 1 - c, 2 * (g ^ two) + c, 2 * (g ^ 3) + c, 2 * (g ^ 3) + 1 - c])
    four = jnp.arange(4, dtype=I32)

    def turn(core, v):
        return jnp.where(core == 0, (v % 2) * 2 + v // 2, v)

    def order(core, quarters):
        return (turn(core, four ^ g)[:, None] * 4 + quarters[None, :]).reshape(16)

    core = c[None]
    orders = jnp.stack([order(k, turn(k, four ^ z)) for k in range(2)])
    plain = jnp.stack([order(k, four) for k in range(2)])
    spots = [jnp.stack([v for src in (c, 1 - c) for k in (p, p + 1) for v in (src, turn(src, jnp.int32(k)) ^ z)]) for p in (0, 2)]
    orders = jnp.where(orders < 8, orders, 8 + 4 * (orders % 4 // 2) + 2 * (orders // 4 % 2) + orders % 2)

    s1, s2, z1, z2, swap = [lambda v, k=k: pperm(v, perms[k]) for k in ("s1", "s2", "z1", "z2", "core")]
    pa0, pa1 = pack_a(where, w_qkv, vec_params.T, jnp.broadcast_to(bias_hidden[None], (8, bias_hidden.shape[0])))
    near_a0 = s1(pa0)
    wo_in, wi_in, wd_in, _ = after((w_out, w_in, w_down), pa0)
    pb0, pb1, pb1_part = pack_b(where, wo_in, wi_in, wd_in)
    near_a0, pb0 = after((near_a0,), pb0)
    far_a = s2(near_a0)
    pa1_l, _ = after((pa1,), near_a0)
    near_a1 = s1(pa1_l)
    side_a0 = swap(near_a0)

    x = hidden_in.reshape(n, d)
    dy = out_grad.reshape(n, d)
    seg_col = segment_ids.reshape(n, 1)
    rr = jnp.pad(rand_blocks[0].T, ((0, 0), (0, HEAD_DIM - nb)), constant_values=-1)
    rand_rows, _ = after((jnp.concatenate([rr, rr], axis=1),), near_a0)

    fq, fk = attn_feats(seg_col, rand_rows, nb)
    far_a, near_a1, _ = after((far_a, near_a1), table, orders, plain, fk, *spots)[:3]
    back_a = swap(far_a)
    side_a1 = swap(near_a1)
    pb0_l, _ = after((pb0,), far_a)
    near_b0 = s1(pb0_l)

    qkv, wq_full, vec, bias = project(x, table, (pa0, pa1, near_a0, near_a1, side_a0, side_a1, far_a, back_a), groups)
    pb1_part, _ = after((pb1_part,), qkv)
    near_b1 = s1(pb1_part)
    o1, f1 = attn_fwd(qkv, fq, fk, nb, 0, 3)
    near_b0, near_b1, o1 = after((near_b0, near_b1), o1)
    far_b = s2(near_b0)
    twin_b1 = pperm(near_b1, perms["twin"])
    side_b0 = swap(near_b0)
    side_b1 = swap(near_b1)
    qkv_l, _ = after((qkv,), near_b0)
    o, f = attn_fwd(qkv_l, fq, fk, nb, 3, 6, (o1, f1))
    far_b, twin_b1, o = after((far_b, twin_b1), o)
    back_b = swap(far_b)
    tail_b1 = swap(twin_b1)
    y, dr1, do, send, keep, vs, bs = token(
        x, dy, o, vec, bias, table, jnp.stack([c, z % 2]), orders, (pb0, pb1, near_b0, side_b0, far_b, back_b, near_b1, twin_b1, side_b1, tail_b1))

    nblk = keep.shape[0]
    up, lo = nblk // 2, nblk // 4
    m, e = lo // 2, lo // 4
    line = Line(vs, core)
    attend = lambda p0, p1: attn_bwd(qkv, f, o, do, fk, nb, p0, p1, line.hold(core))
    got = swap(send)
    part0 = attend(0, 1)
    line.mark = part0[3]
    x1a = s1(line.add(lo, (keep, up + lo), (got, up + lo)))
    part1 = attend(1, 4)
    line.mark = part1[3]
    x2a = s2(line.add(m, (keep, lo + m), (got, lo + m), (x1a, m)))
    x1b = s1(line.add(lo, (keep, up), (got, up)))
    part2 = attend(4, 6)
    line.mark = part2[3]
    v1 = z1(line.add(m, (keep, m), (got, m), (x1a, 0), (x2a, 0)))
    x2b = s2(line.add(m, (keep, lo), (got, lo), (x1b, m)))
    parts = (part0, part1, part2)
    send3, keep3 = grad_qkv(x, parts, line.hold(core), plain, tuple(p[3] for p in parts) + (vs, bs))
    line.mark = send3
    got3 = swap(send3)
    v2 = z2(line.add_kernel(e, (keep, e), (got, e), (x1b, e), (x2b, e), (v1, e)))
    x1_3 = s1(line.add(up, (keep3, up), (got3, up)))
    t0 = line.add(e, (keep, 0), (got, 0), (x1b, 0), (x2b, 0), (v1, 0), (v2, 0))
    for extra in perms["far"]:
        t0 = line.add(e, (t0, 0), (pperm(t0, extra), 0))
    t1 = z2(t0)
    gin = grad_input(dr1, parts, wq_full, line.hold(core))
    line.mark = gin
    x2_3 = s2(line.add(lo, (keep3, lo), (got3, lo), (x1_3, lo)))
    t01 = line.join(t0, t1)
    t23 = z1(t01)
    u01 = swap(t01)
    sum3 = line.add(lo, (keep3, 0), (got3, 0), (x1_3, 0), (x2_3, 0))
    y1 = z1(sum3)
    count = 1.0 / (seqs * groups * reps)
    mats = ((w_down, moments_down), (w_in, moments_in), (w_out, moments_out))
    done = adam_some(line.hold(spots[0]), t01, u01, mats, count)
    line.mark = done[6]
    sum3 = line.add(lo, (sum3, 0), (y1, 0))
    y2 = z2(sum3)
    t23 = line.hold(t23)
    u23 = swap(t23)
    g_down, n_down, m_down, g_in, n_in, m_in, g_out, n_out, m_out = adam_some(line.hold(spots[1]), t23, u23, mats, count, done)
    line.mark = g_out
    sum3 = line.add(lo, (sum3, 0), (y2, 0))
    for extra in perms["far"]:
        sum3 = line.add(lo, (sum3, 0), (pperm(sum3, extra), 0))
    other3 = swap(sum3)
    g_qkv, n_qkv, m_qkv, g_vec, n_vec, m_vec, g_bias, n_bias, m_bias = adam_qkv(
        line.hold(core), sum3, other3, w_qkv, moments_qkv, vec_params.T, moments_vec.transpose(0, 2, 1), bias_hidden, moments_bias, count)
    g_vec, n_vec, m_vec = g_vec.T, n_vec.T, m_vec.transpose(0, 2, 1)
    return (y.reshape(hidden_in.shape), gin.reshape(hidden_in.shape), g_qkv, g_out, g_in, g_down, g_vec, g_bias,
            n_qkv, n_out, n_in, n_down, n_vec, n_bias, m_qkv, m_out, m_in, m_down, m_vec, m_bias)


def solution(mesh):
    groups, reps = mesh.shape["group"], mesh.shape["rep"]
    tok = P(AX, None, None)
    row, mom = P("group", None), P(None, "group", None)

    def run(*args):
        return local(groups, reps, *args)

    return jax.shard_map(
        run,
        mesh=mesh,
        in_specs=(tok, tok, P(AX, None), tok, row, row, row, row, row, P("group"), mom, mom, mom, mom, mom, P(None, "group")),
        out_specs=(tok, tok, row, row, row, row, row, P("group"), row, row, row, row, row, P("group"), mom, mom, mom, mom, mom, P(None, "group")),
        check_vma=False,
    )
```

```python
import jax
import jax.numpy as jnp
from jax import lax
from jax.experimental import pallas as pl
from jax.experimental.pallas import tpu as pltpu
from jax.sharding import PartitionSpec as P

HEAD_DIM = 64
STEP = 4
norm_eps = 1e-05
adam_eps = 1e-08
matrix_decay = 0.1
step_rate = 0.1
BF = jnp.bfloat16
F32 = jnp.float32
I32 = jnp.int32
NEG = -1e30
PAIR = 2 * HEAD_DIM
SQH = 0.7071067811865476
PHI0 = 0.3989422804014327
AX = ("group", "rep")
ANY = pl.BlockSpec(memory_space=pl.ANY)
SMEM = pl.BlockSpec(memory_space=pltpu.SMEM)
VMEM = pl.BlockSpec(memory_space=pltpu.VMEM)
sds = jax.ShapeDtypeStruct


def cost(flops, nbytes, trans=0):
    return pl.CostEstimate(flops=500 * int(flops), bytes_accessed=500 * int(nbytes), transcendentals=500 * int(trans))


def params(mb=60):
    return pltpu.CompilerParams(vmem_limit_bytes=mb * 1024 * 1024)

def nt(a, b):
    return lax.dot_general(a, b, (((1,), (1,)), ((), ())), preferred_element_type=F32)


def nn(a, b):
    return lax.dot_general(a, b, (((1,), (0,)), ((), ())), preferred_element_type=F32)


def tn(a, b):
    return lax.dot_general(a, b, (((0,), (0,)), ((), ())), preferred_element_type=F32)


def split3(v):
    hi = v.astype(BF).astype(F32)
    mid = (v - hi).astype(BF).astype(F32)
    return hi, mid, v - hi - mid


def attn_feats(seg_col, rand_rows, nb):
    n = seg_col.shape[0]

    def kern(seg_ref, rand_ref, fq_ref, fk_ref):
        lane = lax.broadcasted_iota(I32, (n, PAIR), 1) % HEAD_DIM
        blk = lax.broadcasted_iota(I32, (n, PAIR), 0) // (n // nb)
        seg = jnp.broadcast_to(seg_ref[...], (n, PAIR))
        fq = (lane == blk) | ((lane >= nb) & (lane - nb == seg))
        fq_ref[...] = jnp.where(fq, 1.0, 0.0).astype(BF)
        allow = (jnp.abs(lane - blk) <= 1) | (lane == 0) | (lane == nb - 1) | (blk == 0) | (blk == nb - 1)
        for j in range(rand_ref.shape[0]):
            allow = allow | (rand_ref[j : j + 1, :] == blk)
        bad = ((lane < nb) & jnp.logical_not(allow)) | ((lane >= nb) & (lane < nb + 4) & (lane - nb != seg))
        off = (lane >= nb + 4) & (lane < nb + 7)
        fk_ref[...] = jnp.where(bad, NEG, jnp.where(off, -1.0, 0.0)).astype(BF)

    return pl.pallas_call(
        kern,
        out_shape=[sds((n, PAIR), BF)] * 2,
        compiler_params=params(),
        cost_estimate=cost(20 * n * PAIR, 4 * n * PAIR),
        name="attn_feats",
    )(seg_col, rand_rows)


def attn_fwd_kernel(nb, fq_s, fk_s, q_ref, k_ref, v_ref, o_ref, f_ref):
    n = q_ref.shape[0]
    t = 256
    low1 = lax.broadcasted_iota(jnp.int32, (n, PAIR), 1) < HEAD_DIM
    k = k_ref[...]
    v = v_ref[...]
    fk = fk_s[...]
    one = jnp.ones((n, PAIR), BF)
    ks = (jnp.where(low1, k, fk), jnp.where(low1, fk, k))
    vs = (jnp.where(low1, v, one), jnp.where(low1, one, v))
    lowt = lax.broadcasted_iota(jnp.int32, (t, PAIR), 1) < HEAD_DIM
    lane = lax.broadcasted_iota(jnp.int32, (t, PAIR), 1) % HEAD_DIM
    for i in range(n // t):
        rows = pl.ds(i * t, t)
        q = q_ref[rows, :] * jnp.asarray(HEAD_DIM**-0.5, BF)
        fq = fq_s[rows, :]
        acc, top = [], []
        for h in range(2):
            qh = jnp.where(lowt, q, fq) if h == 0 else jnp.where(lowt, fq, q)
            s = nt(qh, ks[h])
            m = jnp.max(s, axis=-1, keepdims=True)
            p = jnp.exp(s - m).astype(BF)
            acc.append(nn(p, vs[h]))
            top.append(m)
        lsw = jnp.where(lowt, acc[1], acc[0])
        o = jnp.where(lowt, acc[0], acc[1]) / pltpu.roll(lsw, HEAD_DIM, 1)
        o_ref[rows, :] = o.astype(BF)
        hi, mid, lo = split3(jnp.where(lowt, top[1], top[0]) + jnp.log(lsw))
        f = jnp.where(lane == nb + 4, hi, jnp.where(lane == nb + 5, mid, lo))
        f_ref[rows, :] = jnp.where((lane >= nb + 4) & (lane < nb + 7), f.astype(BF), fq)


def attn_fwd(qkv, fq, fk, nb, p0, p1, into=(), mb=28):
    n, w3 = qkv.shape
    w = w3 // 3
    pairs = w // PAIR
    blk = lambda off: pl.BlockSpec((n, PAIR), lambda p, off=off: (0, p + off))
    full = lambda a: pl.BlockSpec(a.shape, lambda p: (0, 0))

    def kern(*refs):
        attn_fwd_kernel(nb, *refs[:5], *refs[5 + len(into) :])

    return pl.pallas_call(
        kern,
        grid=(p1 - p0,),
        in_specs=[full(fq), full(fk), blk(p0), blk(pairs + p0), blk(2 * pairs + p0)] + [ANY] * len(into),
        out_specs=[blk(p0), blk(p0)],
        out_shape=[sds((n, w), BF)] * 2,
        input_output_aliases={5 + i: i for i in range(len(into))},
        compiler_params=params(mb),
        cost_estimate=cost(16 * n * n * (p1 - p0) * PAIR, 12 * n * (p1 - p0) * PAIR, 2 * n * n * (p1 - p0)),
        name="attn_fwd",
    )(fq, fk, qkv, qkv, qkv, *into)


def attn_bwd_kernel(nb, fk_s, q_ref, k_ref, v_ref, f_ref, o_ref, do_ref, dq_ref, dk_ref, dv_ref, b_ref):
    n = q_ref.shape[0]
    t = 256
    low1 = lax.broadcasted_iota(jnp.int32, (n, PAIR), 1) < HEAD_DIM
    lane = lax.broadcasted_iota(jnp.int32, (n, PAIR), 1) % HEAD_DIM
    scale = jnp.asarray(HEAD_DIM**-0.5, BF)
    q = q_ref[...] * scale
    f = f_ref[...]
    do = do_ref[...]
    prod = do.astype(F32) * o_ref[...].astype(F32)
    d0 = jnp.sum(jnp.where(low1, prod, 0.0), axis=-1, keepdims=True)
    d1 = jnp.sum(jnp.where(low1, 0.0, prod), axis=-1, keepdims=True)
    hi, mid, lo = split3(jnp.where(low1, d1, d0))
    fd = jnp.where(lane == nb + 4, hi, jnp.where(lane == nb + 5, mid, jnp.where(lane == nb + 6, lo, 0.0))).astype(BF)
    qs = (jnp.where(low1, q, f), jnp.where(low1, f, q))
    dos = (jnp.where(low1, do, fd), jnp.where(low1, fd, do))
    kT = jnp.transpose(k_ref[...] * scale)
    lowt = lax.broadcasted_iota(jnp.int32, (t, PAIR), 1) < HEAD_DIM
    dqT = [None, None]
    dv_sum = jnp.zeros((1, PAIR), F32)
    for i in range(n // t):
        rows = pl.ds(i * t, t)
        k = k_ref[rows, :]
        v = v_ref[rows, :]
        fk = fk_s[rows, :]
        fv = jnp.where(fk == -1.0, fk, jnp.zeros_like(fk))
        dvh, dkh = [], []
        for h in range(2):
            kh = jnp.where(lowt, k, fk) if h == 0 else jnp.where(lowt, fk, k)
            vh = jnp.where(lowt, v, fv) if h == 0 else jnp.where(lowt, fv, v)
            p = jnp.exp(nt(kh, qs[h]))
            ds = (p * nt(vh, dos[h])).astype(BF)
            dvh.append(nn(p.astype(BF), do))
            dkh.append(nn(ds, q))
            part = nn(kT[h * HEAD_DIM : (h + 1) * HEAD_DIM, i * t : (i + 1) * t], ds)
            dqT[h] = part if dqT[h] is None else dqT[h] + part
        dk = jnp.where(lowt, dkh[0], dkh[1]).astype(BF)
        dv = jnp.where(lowt, dvh[0], dvh[1]).astype(BF)
        dk_ref[rows, :] = dk
        dv_ref[rows, :] = dv
        dv_sum = dv_sum + colsum(dv.astype(F32))
    dq = jnp.transpose(jnp.concatenate(dqT, axis=0)).astype(BF)
    dq_ref[...] = dq
    b_ref[...] = jnp.concatenate([colsum(dq.astype(F32)), dv_sum, jnp.zeros((6, PAIR), F32)], axis=0)


def attn_bwd(qkv, f, o, do, fk, nb, p0, p1, turn):
    n, w3 = qkv.shape
    pairs = w3 // 3 // PAIR
    cols = (p1 - p0) * PAIR
    blk = lambda off: pl.BlockSpec((n, PAIR), lambda p, off=off: (0, p + off))
    full = lambda a: pl.BlockSpec(a.shape, lambda p: (0,) * a.ndim)
    return pl.pallas_call(
        lambda turn_ref, *refs: attn_bwd_kernel(nb, *refs),
        grid=(p1 - p0,),
        in_specs=[SMEM, full(fk), blk(p0), blk(pairs + p0), blk(2 * pairs + p0), blk(p0), blk(p0), blk(p0)],
        out_specs=[blk(0), blk(0), blk(0), pl.BlockSpec((8, PAIR), lambda p: (0, p))],
        out_shape=[sds((n, cols), BF)] * 3 + [sds((8, cols), F32)],
        compiler_params=params(28),
        cost_estimate=cost(40 * n * n * cols, 20 * n * cols, n * n * cols // HEAD_DIM),
        name="attn_bwd",
    )(turn, fk, qkv, qkv, qkv, f, o, do)


def grad_qkv(x, parts, core, orders, small=()):
    n, d = x.shape
    blocks = orders.shape[1]
    np_ = len(parts)
    unit, rb = sum(p[0].shape[1] for p in parts) // 2, d // blocks
    rows = 3 * rb + (16 if small else 0)
    g = (blocks, rows, unit)
    ns = len(small)

    def kern(core_ref, ord_ref, x_ref, *refs):
        ds = [[refs[3 * p + part] for p in range(np_)] for part in range(3)]
        extra = refs[3 * np_ : 3 * np_ + ns]
        send_ref, keep_ref, g_s, osem = refs[3 * np_ + ns :]
        x = x_ref[...]
        sels = [1 - (core_ref[0] ^ h) for h in range(2)]
        cat = lambda rs: rs[0][...] if len(rs) == 1 else jnp.concatenate([r[...] for r in rs], axis=1)
        for part in range(3):
            r = tn(x, cat(ds[part])).astype(BF)
            for h in range(2):
                for a in range(blocks):
                    g_s[sels[h], ord_ref[h, a], part * rb : (part + 1) * rb, :] = r[a * rb : (a + 1) * rb, h * unit : (h + 1) * unit]
        if ns:
            vs_ref, bs_ref = extra[-2:]
            groups = bs_ref.shape[0]
            quarters = blocks // groups
            vec = jnp.concatenate([cat(extra[:-2])[0:2], vs_ref[2:8, :]], axis=0)
            share = d // groups
            for gr in range(groups):
                gs = slice(gr * share, (gr + 1) * share)
                lines = [jnp.concatenate([vec[2 * i : 2 * i + 1, gs], vec[2 * i + 1 : 2 * i + 2, gs]], axis=1) for i in range(4)]
                lines += [bs_ref[gr, 0:1, i * (d // 2) : (i + 1) * (d // 2)] for i in range(2)]
                for i in range(2 * quarters):
                    h, q = i // quarters, i % quarters
                    line = lines[i] if i < len(lines) else jnp.zeros((1, d // 2), F32)
                    pieces = [line[:, k * unit : (k + 1) * unit] for k in range(d // 2 // unit)]
                    tile = jnp.concatenate(pieces + [jnp.zeros((16 - len(pieces), unit), F32)], axis=0)
                    g_s[sels[h], ord_ref[h, gr * quarters + q], 3 * rb : 3 * rb + 16, :] = tile.astype(BF)
        out = [pltpu.make_async_copy(g_s.at[0], send_ref, osem.at[0]), pltpu.make_async_copy(g_s.at[1], keep_ref, osem.at[1])]
        for cp in out:
            cp.start()
        for cp in out:
            cp.wait()

    flat = [a for p in parts for a in p[:3]] + list(small)
    return pl.pallas_call(
        kern,
        in_specs=[SMEM, SMEM] + [VMEM] * (1 + len(flat)),
        out_specs=[ANY, ANY],
        out_shape=[sds(g, BF)] * 2,
        scratch_shapes=[pltpu.VMEM((2,) + g, BF), pltpu.SemaphoreType.DMA((2,))],
        compiler_params=params(28),
        cost_estimate=cost(12 * n * d * unit, 14 * n * d),
        name="grad_qkv",
    )(core, orders, x, *flat)


def norm(r, g, c):
    w = r.shape[-1]
    center = r - jnp.sum(r, axis=-1, keepdims=True) * (1.0 / w)
    inv = lax.rsqrt(jnp.sum(center * center, axis=-1, keepdims=True) * (1.0 / w) + norm_eps)
    n = center * inv
    return n * g + c, n, inv


def norm_back(dy, g, n, inv):
    w = dy.shape[-1]
    e = dy * g
    a = jnp.sum(e, axis=-1, keepdims=True) * (1.0 / w)
    b = jnp.sum(e * n, axis=-1, keepdims=True) * (1.0 / w)
    return inv * (e - a - n * b)


def colsum(a):
    return jnp.sum(a, axis=0, keepdims=True)


def pack_a(where, w, vec_t, bias):
    rows, cols = w.shape
    half = rows // 2

    def kern(where_ref, w_ref, vec_ref, bias_ref, *outs):
        for pos in range(2):
            h = pos ^ where_ref[1]
            outs[pos][0, 0:half, :] = w_ref[pl.ds(pl.multiple_of(h * half, 8), half), :].astype(BF)
            pad = lambda v: jnp.concatenate([v, jnp.zeros((v.shape[0], cols - v.shape[1]), F32)], axis=1)
            small = jnp.where(h == 0, pad(vec_ref[...]), pad(bias_ref[...]))
            outs[pos][0, half : half + 16, :] = jnp.concatenate([small, small], axis=0).astype(BF)

    return pl.pallas_call(
        kern,
        in_specs=[SMEM, VMEM, VMEM, VMEM],
        out_specs=[VMEM, VMEM],
        out_shape=[sds((1, half + 16, cols), BF)] * 2,
        compiler_params=params(28),
        cost_estimate=cost(0, 3 * w.size * 2),
        name="pack_a",
    )(where, w, vec_t, bias)


def pack_b(where, wo, wi, wd):
    rows, w = wo.shape
    half = rows // 2
    nf = wi.shape[1] // w
    nd = wd.shape[0] // rows

    def kern(where_ref, wo_ref, wi_ref, wd_ref, *outs):
        for pos in range(2):
            h = pos ^ where_ref[1]
            hs = pl.ds(pl.multiple_of(h * half, 8), half)
            outs[pos][0, 0] = wo_ref[hs, :].astype(BF)
            for j in range(nf):
                outs[pos][0, 1 + j] = wi_ref[hs, j * w : (j + 1) * w].astype(BF)
            for j in range(nd):
                at = pl.multiple_of((h * nd + j) * half, 8)
                outs[pos][0, 1 + nf + j] = wd_ref[pl.ds(at, half), :].astype(BF)
        part = pl.ds(pl.multiple_of(where_ref[2] % 2 * (half // 2), 16), half // 2)
        outs[2][...] = outs[1][:, :, part, :]

    blocks = 1 + nf + nd
    return pl.pallas_call(
        kern,
        in_specs=[SMEM, VMEM, VMEM, VMEM],
        out_specs=[VMEM] * 3,
        out_shape=[sds((1, blocks, half, w), BF)] * 2 + [sds((1, blocks, half // 2, w), BF)],
        compiler_params=params(28),
        cost_estimate=cost(0, 6 * (wo.size + wi.size + wd.size)),
        name="pack_b",
    )(where, wo, wi, wd)


def pperm(a, pairs):
    return lax.ppermute(a, AX, pairs)


def after(late, *early):
    out = lax.optimization_barrier(tuple(late) + early)
    return out[: len(late) + 1]


def piece_refs(refs):
    out = []
    for ref in refs:
        out += [ref.at[k] for k in range(ref.shape[0])]
    return out


def project(x, table, parts, groups, t=256):
    n, d = x.shape
    _, hp, cols = parts[0].shape
    half = hp - 16
    share = 2 * half

    def kern(tab_ref, x_ref, *refs):
        pieces = piece_refs(refs[:8])
        qkv_ref, w_out, vec_ref, bias_ref, w_s, e_s, sems, osem = refs[8:]
        first = pl.program_id(0) == 0
        last = pl.program_id(0) == pl.num_programs(0) - 1

        def copies():
            out = []
            for i, p in enumerate(pieces):
                u = tab_ref[i]
                out.append(pltpu.make_async_copy(p.at[pl.ds(0, half)], w_s.at[pl.ds(pl.multiple_of(u * half, 16), half)], sems.at[2 * i]))
                out.append(pltpu.make_async_copy(p.at[pl.ds(half, 16)], e_s.at[u], sems.at[2 * i + 1]))
            return out

        def whole():
            return pltpu.make_async_copy(w_s, w_out, osem)

        @pl.when(first)
        def _():
            for cp in copies():
                cp.start()
            for cp in copies():
                cp.wait()
            whole().start()
            vec_ref[...] = jnp.concatenate([e_s[2 * g, 0:8, 0:share].astype(F32) for g in range(groups)], axis=1)
            for g in range(groups):
                bias_ref[g] = e_s[2 * g + 1, 0:8, 0:d].astype(F32)

        qb = jnp.concatenate([vec_ref[0:1, :], jnp.zeros((1, d), F32), vec_ref[1:2, :]], axis=1)
        qkv_ref[...] = (nn(x_ref[...], w_s[...]) + qb).astype(BF)

        @pl.when(last)
        def _():
            whole().wait()

    return pl.pallas_call(
        kern,
        grid=(n // t,),
        in_specs=[SMEM, pl.BlockSpec((t, d), lambda i: (i, 0))] + [ANY] * 8,
        out_specs=[pl.BlockSpec((t, cols), lambda i: (i, 0)), ANY, pl.BlockSpec((8, d), lambda i: (0, 0)), pl.BlockSpec((groups, 8, d), lambda i: (0, 0, 0))],
        out_shape=[sds((n, cols), BF), sds((d, cols), BF), sds((8, d), F32), sds((groups, 8, d), F32)],
        scratch_shapes=[pltpu.VMEM((d, cols), BF), pltpu.VMEM((2 * groups, 16, cols), BF), pltpu.SemaphoreType.DMA((16,)), pltpu.SemaphoreType.DMA],
        compiler_params=params(),
        cost_estimate=cost(2 * n * d * cols, 2 * (n * d + 2 * d * cols + n * cols)),
        name="project",
    )(table, x, *parts)


def token(x, dy, o, vec, bias, table, core, orders, parts):
    n, w = x.shape
    _, k9, half, _ = parts[0].shape
    nf = bias.shape[0]
    nd = k9 - 1 - nf
    ff = nf * w
    nblk = orders.shape[1]
    nq = nblk // nf
    unit = w // 2
    rb = w // nblk
    db = w // (2 * nq)
    t = n // 2

    def kern(tab_ref, core_ref, ord_ref, vec_any, bias_any, x_ref, dy_ref, o_ref, *refs):
        parity = core_ref[2] % 2
        whole, upper = [(0, 0), (1, 1), (2, 2), (3, 4), (4, 6), (5, 7)], [(6, 3, parity), (7, 3, 1 - parity), (8, 5, parity), (9, 5, 1 - parity)]
        pieces = [(refs[k].at[0], tab_ref[u], 0, half) for k, u in whole] + [(refs[k].at[0], tab_ref[u], p * (half // 2), half // 2) for k, u, p in upper]
        (y_ref, dr1_ref, do_ref, send_ref, keep_ref, vs_ref, bs_ref,
         wo_s, wi_s, wd_s, x_s, dy_s, o_s, n1_s, inv_s, x1b_s, hb_s, sl_s, acc_s, dfb_s, y_s, g_s, vec_ref, bias_ref, sems, isem, osem) = refs[10:]

        def copies(kind):
            out = []
            for i, (p, u, r0, size) in enumerate(pieces):
                rows = pl.ds(pl.multiple_of(u * half + r0, 16), size)
                if kind == 0:
                    out.append(pltpu.make_async_copy(p.at[0], wo_s.at[rows], sems.at[0, i]))
                elif kind == 1:
                    out.append(pltpu.make_async_copy(p.at[pl.ds(1, nf)], wi_s.at[:, rows], sems.at[1, i]))
                else:
                    out.append(pltpu.make_async_copy(p.at[pl.ds(1 + nf, nd)], wd_s.at[pl.ds(u * nd, nd), pl.ds(pl.multiple_of(r0, 16), size)], sems.at[2, i]))
            return out

        c_v = [pltpu.make_async_copy(vec_any, vec_ref, isem.at[3]), pltpu.make_async_copy(bias_any, bias_ref, isem.at[4])]
        c_o = pltpu.make_async_copy(o_ref, o_s, isem.at[0])
        c_x = pltpu.make_async_copy(x_ref, x_s, isem.at[1])
        c_dy = pltpu.make_async_copy(dy_ref, dy_s, isem.at[2])
        for cp in c_v + copies(0) + [c_o, c_x] + copies(1) + copies(2) + [c_dy]:
            cp.start()
        for cp in c_v:
            cp.wait()
        row = lambda j: vec_ref[j : j + 1, :]
        bo, g1, c1, bd, g2, c2 = [row(j) for j in range(2, 8)]
        per = wd_s.shape[0] // nf
        down = lambda j: wd_s[pl.ds(j * per, per)].reshape(w, w)
        for cp in copies(0) + [c_o, c_x]:
            cp.wait()

        def first(i, _):
            rows = pl.ds(pl.multiple_of(i * t, t), t)
            x1, n1, inv1 = norm(x_s[rows, :].astype(F32) + (nn(o_s[rows, :], wo_s[...]) + bo), g1, c1)
            n1_s[rows, :] = n1
            inv_s[rows, :] = jnp.broadcast_to(inv1, (t, 128))
            x1b_s[rows, :] = x1.astype(BF)
            acc_s[rows, :] = x1 + bd
            return 0

        lax.fori_loop(0, 2, first, 0)
        for cp in copies(1):
            cp.wait()

        def up(j, _):
            for i in range(2):
                rows = slice(i * t, (i + 1) * t)
                h = nn(x1b_s[rows, :], wi_s[j]) + bias_ref[j, 0:1, :]
                cdf = 0.5 * (1.0 + lax.erf(h * SQH))
                hb_s[j, rows, :] = (h * cdf).astype(BF)
                sl_s[j, rows, :] = (cdf + h * (jnp.exp(-0.5 * (h * h)) * PHI0)).astype(BF)
            return 0

        lax.fori_loop(0, nf, up, 0)
        for cp in copies(2) + [c_dy]:
            cp.wait()
        vs_ref[...] = jnp.zeros_like(vs_ref)

        def top(i, _):
            rows = pl.ds(pl.multiple_of(i * t, t), t)
            r2 = acc_s[rows, :]
            for j in range(nf):
                r2 = r2 + nn(hb_s[j, rows, :], down(j))
            y, n2, inv2 = norm(r2, g2, c2)
            y_s[rows, :] = y
            dyf = dy_s[rows, :].astype(F32)
            dr2 = norm_back(dyf, g2, n2, inv2)
            acc_s[rows, :] = dr2
            dfb_s[rows, :] = dr2.astype(BF)
            vs_ref[5:6, :] += colsum(dr2)
            vs_ref[6:7, :] += colsum(dyf * n2)
            vs_ref[7:8, :] += colsum(dyf)
            return 0

        lax.fori_loop(0, n // t, top, 0)
        c_y = pltpu.make_async_copy(y_s, y_ref, osem.at[0])
        c_y.start()

        def back(j, _):
            for i in range(2):
                rows = slice(i * t, (i + 1) * t)
                dh = (nt(dfb_s[rows, :], down(j)) * sl_s[j, rows, :].astype(F32)).astype(BF)
                sl_s[j, rows, :] = dh
                s = jnp.broadcast_to(colsum(dh.astype(F32)), (8, w))
                bs_ref[j] = s if i == 0 else bs_ref[j] + s
                acc_s[rows, :] += nt(dh, wi_s[j])
            gd = tn(hb_s[j], dfb_s[...]).astype(BF)
            for h in range(2):
                sel = 1 - (core_ref[1] ^ h)
                for q in range(nq):
                    r0 = (h * nq + q) * db
                    pos = ord_ref[h, j * nq + q]
                    for k in range(2):
                        g_s[sel, pos, k * db : (k + 1) * db, :] = gd[r0 : r0 + db, k * unit : (k + 1) * unit]
            gi = tn(x1b_s[...], sl_s[j]).astype(BF)
            h = j // (nf // 2)
            sel = 1 - (core_ref[1] ^ h)
            for a in range(nblk):
                pos = ord_ref[h, a]
                for k in range(2):
                    at = pl.multiple_of(2 * db + ((j % (nf // 2)) * 2 + k) * rb, 16)
                    g_s[sel, pos, pl.ds(at, rb), :] = gi[a * rb : (a + 1) * rb, k * unit : (k + 1) * unit]
            return 0

        lax.fori_loop(0, nf, back, 0)
        most = pl.ds(0, 2 * db + nf * rb)
        outs = [pltpu.make_async_copy(g_s.at[k, :, most], (send_ref, keep_ref)[k].at[:, most], osem.at[1 + k]) for k in range(2)]
        for cp in outs:
            cp.start()

        def leave(i):
            rows = pl.ds(pl.multiple_of(i * t, t), t)
            return [pltpu.make_async_copy(acc_s.at[rows], dr1_ref.at[rows], osem.at[5 + 2 * i]), pltpu.make_async_copy(dy_s.at[rows], do_ref.at[rows], osem.at[6 + 2 * i])]

        def low(i, _):
            rows = pl.ds(pl.multiple_of(i * t, t), t)
            dx1 = acc_s[rows, :]
            n1 = n1_s[rows, :]
            dr1 = norm_back(dx1, g1, n1, inv_s[rows, 0:1])
            acc_s[rows, :] = dr1
            dab = dr1.astype(BF)
            x_s[rows, :] = dab
            dy_s[rows, :] = nt(dab, wo_s[...]).astype(BF)
            vs_ref[2:3, :] += colsum(dr1)
            vs_ref[3:4, :] += colsum(dx1 * n1)
            vs_ref[4:5, :] += colsum(dx1)
            for cp in leave(i):
                cp.start()
            return 0

        lax.fori_loop(0, 2, low, 0)
        go = tn(o_s[...], x_s[...]).astype(BF)
        for h in range(2):
            sel = 1 - (core_ref[1] ^ h)
            for a in range(nblk):
                g_s[sel, ord_ref[h, a], 2 * db + nf * rb : 2 * db + (nf + 1) * rb, :] = go[a * rb : (a + 1) * rb, h * unit : (h + 1) * unit]
        last = pl.ds(2 * db + nf * rb, rb)
        more = [pltpu.make_async_copy(g_s.at[k, :, last], (send_ref, keep_ref)[k].at[:, last], osem.at[3 + k]) for k in range(2)]
        for cp in more:
            cp.start()
        for cp in [c_y] + outs + leave(0) + leave(1) + more:
            cp.wait()

    gs = (nblk, 2 * db + (nf + 1) * rb, unit)
    vm = lambda s, dt=BF: pltpu.VMEM(s, dt)
    return pl.pallas_call(
        kern,
        in_specs=[SMEM, SMEM, SMEM] + [ANY] * 15,
        out_specs=[ANY] * 5 + [VMEM, VMEM],
        out_shape=[sds((n, w), F32), sds((n, w), F32), sds((n, w), BF), sds(gs, BF), sds(gs, BF), sds((8, w), F32), sds((nf, 8, w), F32)],
        scratch_shapes=[vm((w, w)), vm((nf, w, w)), vm((ff // half, half, w)), vm((n, w)), vm((n, w)), vm((n, w)), vm((n, w), F32), vm((n, 128), F32),
                        vm((n, w)), vm((nf, n, w)), vm((nf, n, w)), vm((n, w), F32), vm((n, w)), vm((n, w), F32), vm((2,) + gs), vm(vec.shape, F32), vm(bias.shape, F32),
                        pltpu.SemaphoreType.DMA((3, 10)), pltpu.SemaphoreType.DMA((5,)), pltpu.SemaphoreType.DMA((9,))],
        compiler_params=params(),
        cost_estimate=cost(2 * n * w * (3 * w + 6 * ff), 2 * (n * 8 * w + 3 * w * (w + 2 * ff)), 2 * n * ff),
        name="token",
    )(table, core, orders, vec, bias, x, dy, o, *parts)


def grad_input(dr1, parts, w, turn, t=256):
    n, d = dr1.shape
    k = len(parts)

    def kern(turn_ref, r_ref, w_ref, *refs):
        out_ref = refs[-1]
        out = r_ref[...]
        for part in range(3):
            g = jnp.concatenate([refs[3 * p + part][...] for p in range(k)], axis=1)
            out = out + nt(g, w_ref[:, part * d : (part + 1) * d])
        out_ref[...] = out

    rows = lambda c: pl.BlockSpec((t, c), lambda i: (i, 0))
    flat = [a for p in parts for a in p[:3]]
    return pl.pallas_call(
        kern,
        grid=(n // t,),
        in_specs=[SMEM, rows(d), pl.BlockSpec(w.shape, lambda i: (0, 0))] + [rows(a.shape[1]) for a in flat],
        out_specs=rows(d),
        out_shape=sds((n, d), F32),
        compiler_params=params(28),
        cost_estimate=cost(6 * n * d * d, n * d * 14 + 2 * w.size),
        name="grad_input",
    )(turn, dr1, w, *flat)


def total(*terms):
    out = terms[0].astype(F32)
    for a in terms[1:]:
        out = out + a.astype(F32)
    return out.astype(BF)


def total_kernel(turn, n, *terms):
    block = terms[0][0].shape[1:]
    k = len(terms)

    def kern(turn_ref, *refs):
        ins, out_ref, scr, out_s, isem, osem = refs[:k], refs[k], refs[k + 1], refs[k + 2], refs[k + 3], refs[k + 4]

        def come(i):
            return [pltpu.make_async_copy(ins[t].at[terms[t][1] + i], scr.at[t, i], isem.at[t, i]) for t in range(k)]

        def go(i):
            return pltpu.make_async_copy(out_s.at[i], out_ref.at[i], osem.at[i])

        for i in range(n):
            for cp in come(i):
                cp.start()
        for i in range(n):
            for cp in come(i):
                cp.wait()
            out = scr[0, i].astype(F32)
            for t in range(1, k):
                out = out + scr[t, i].astype(F32)
            out_s[i] = out.astype(BF)
            go(i).start()
        for i in range(n):
            go(i).wait()

    return pl.pallas_call(
        kern,
        in_specs=[SMEM] + [ANY] * k,
        out_specs=ANY,
        out_shape=sds((n,) + block, BF),
        scratch_shapes=[pltpu.VMEM((k, n) + block, BF), pltpu.VMEM((n,) + block, BF), pltpu.SemaphoreType.DMA((k, n)), pltpu.SemaphoreType.DMA((n,))],
        compiler_params=params(16),
        cost_estimate=cost(10**9, 0),
        name="total",
    )(turn, *[a for a, _ in terms])


class Line:
    def __init__(self, mark, core):
        self.mark = mark
        self.core = core

    def hold(self, *arrays):
        out = lax.optimization_barrier(arrays + (self.mark,))
        return out[0] if len(arrays) == 1 else out[:-1]

    def add(self, n, *terms):
        held = (self.hold(terms[0][0]),) + tuple(a for a, _ in terms[1:])
        self.mark = total(*[a[first : first + n] for a, (_, first) in zip(held, terms)])
        return self.mark

    def add_kernel(self, n, *terms):
        self.mark = total_kernel(self.hold(self.core), n, *terms)
        return self.mark

    def join(self, a, b):
        self.mark = jnp.concatenate([self.hold(a), b], axis=0)
        return self.mark


def adam(w, m, u, g, decay):
    correct = 1.0 - 0.5**STEP
    m = 0.5 * m + 0.5 * g
    u = 0.5 * u + 0.5 * g * g
    return w - step_rate * (m * (1.0 / correct) / (jnp.sqrt(u * (1.0 / correct)) + adam_eps) + decay * w), m, u


def adam_some(spots, mine, other, mats, count, into=()):
    half = mine.shape[0]
    (w_down, _), (w_in, _), (w_out, _) = mats
    rd, ri, unit = w_down.shape[0] // 8, w_in.shape[0] // 4, mine.shape[2]
    ki = w_in.shape[1] // 2 // unit
    blocks = [(rd, w_down.shape[1]), (ri, w_in.shape[1] // 2), (ri, w_out.shape[1] // 2)]
    steps = 2 * half
    ni = len(into)

    def kern(spots_ref, a_ref, b_ref, *refs):
        olds, news = refs[:6], refs[6 + ni : 15 + ni]
        src_s, isem, osem = refs[15 + ni], refs[16 + ni], refs[17 + ni]
        bufs = [refs[18 + ni + 3 * k : 21 + ni + 3 * k] for k in range(3)]

        def place(k, s):
            h, q = spots_ref[2 * s], spots_ref[2 * s + 1]
            r, c = blocks[k]
            if k == 0:
                return pl.ds(pl.multiple_of((h * 4 + q) * r, 8), r), pl.ds(0, c)
            return pl.ds(pl.multiple_of(q * r, 8), r), pl.ds(pl.multiple_of(h * c, 128), c)

        def come(s):
            out = [pltpu.make_async_copy((a_ref, b_ref)[s // half].at[s % half], src_s.at[s], isem.at[s, 0])]
            for k in range(3):
                rows, cols = place(k, s)
                out.append(pltpu.make_async_copy(olds[2 * k].at[rows, cols], bufs[k][0].at[s], isem.at[s, 1 + 2 * k]))
                out.append(pltpu.make_async_copy(olds[2 * k + 1].at[:, rows, cols], bufs[k][1].at[s], isem.at[s, 2 + 2 * k]))
            return out

        def go(s):
            out = []
            for k in range(3):
                rows, cols = place(k, s)
                out.append(pltpu.make_async_copy(bufs[k][2].at[s], news[3 * k].at[rows, cols], osem.at[s, 3 * k]))
                out.append(pltpu.make_async_copy(bufs[k][0].at[s], news[3 * k + 1].at[rows, cols], osem.at[s, 3 * k + 1]))
                out.append(pltpu.make_async_copy(bufs[k][1].at[s], news[3 * k + 2].at[:, rows, cols], osem.at[s, 3 * k + 2]))
            return out

        for s in range(steps):
            for cp in come(s):
                cp.start()
        for s in range(steps):
            for cp in come(s):
                cp.wait()
            g = src_s[s].astype(F32) * count
            at = 2 * rd
            grads = [jnp.concatenate([g[:rd], g[rd:at]], axis=1),
                     jnp.concatenate([g[at + k * ri : at + (k + 1) * ri] for k in range(ki)], axis=1),
                     g[at + ki * ri : at + (ki + 1) * ri]]
            for k in range(3):
                w_s, m_s, g_s = bufs[k]
                g_s[s] = grads[k]
                w_s[s], m_s[s, 0], m_s[s, 1] = adam(w_s[s], m_s[s, 0], m_s[s, 1], grads[k], matrix_decay)
            for cp in go(s):
                cp.start()
        for s in range(steps):
            for cp in go(s):
                cp.wait()

    shapes, args, scratch = [], [], []
    for (w, m), b in zip(mats, blocks):
        shapes += [sds(w.shape, F32), sds(w.shape, F32), sds(m.shape, F32)]
        args += [w, m]
        scratch += [pltpu.VMEM((steps,) + b, F32), pltpu.VMEM((steps, 2) + b, F32), pltpu.VMEM((steps,) + b, F32)]
    size = sum(w.size for w, _ in mats) // 2
    return pl.pallas_call(
        kern,
        in_specs=[SMEM] + [ANY] * (8 + ni),
        out_specs=[ANY] * 9,
        out_shape=shapes,
        scratch_shapes=[pltpu.VMEM((steps,) + mine.shape[1:], BF), pltpu.SemaphoreType.DMA((steps, 7)), pltpu.SemaphoreType.DMA((steps, 9))] + scratch,
        input_output_aliases={9 + k: k for k in range(ni)},
        compiler_params=params(28),
        cost_estimate=cost(20 * size, 28 * size, 2 * size),
        name="adam_some",
    )(spots, mine, other, *args, *into)


def adam_qkv(core, mine, other, w, mom, vec, mom_vec, bias, mom_bias, count):
    rb, cols = w.shape[0] // 4, w.shape[1]
    unit = mine.shape[2]
    share = vec.shape[1]

    def kern(core_ref, a_ref, b_ref, w_ref, m_ref, v_ref, mv_ref, c_ref, mc_ref,
             g_out, w_out, m_out, gv_out, v_out, mv_out, gc_out, c_out, mc_out, w_s, m_s, g_s, isem, osem):
        at = lambda s: pl.ds(s * rb, rb)

        def come(s):
            return [pltpu.make_async_copy(w_ref.at[at(s)], w_s.at[at(s)], isem.at[s, 0]),
                    pltpu.make_async_copy(m_ref.at[:, at(s)], m_s.at[:, at(s)], isem.at[s, 1])]

        def go(s):
            return [pltpu.make_async_copy(g_s.at[at(s)], g_out.at[at(s)], osem.at[s, 0]),
                    pltpu.make_async_copy(w_s.at[at(s)], w_out.at[at(s)], osem.at[s, 1]),
                    pltpu.make_async_copy(m_s.at[:, at(s)], m_out.at[:, at(s)], osem.at[s, 2])]

        for s in range(4):
            for cp in come(s):
                cp.start()
        flip = core_ref[0] == 1
        for s in range(4):
            for cp in come(s):
                cp.wait()
            a, b = a_ref[s, 0 : 3 * rb, :].astype(F32) * count, b_ref[s, 0 : 3 * rb, :].astype(F32) * count
            first, second = jnp.where(flip, b, a), jnp.where(flip, a, b)
            g = jnp.concatenate([v[p * rb : (p + 1) * rb] for p in range(3) for v in (first, second)], axis=1)
            rows = slice(s * rb, (s + 1) * rb)
            g_s[rows, :] = g
            w_s[rows, :], m_s[0, rows, :], m_s[1, rows, :] = adam(w_s[rows, :], m_s[0, rows, :], m_s[1, rows, :], g, matrix_decay)
            for cp in go(s):
                cp.start()
        line = lambda ref: [ref[q, 3 * rb : 3 * rb + 8, :].astype(F32)[0:1] * count for q in range(4)]
        own, sib = line(a_ref), line(b_ref)
        first, second = [jnp.where(flip, y, x) for x, y in zip(own, sib)], [jnp.where(flip, x, y) for x, y in zip(own, sib)]
        g = jnp.concatenate([v[:, k * share : (k + 1) * share] for v in first for k in range(unit // share)], axis=0)
        gv_out[...] = g
        v_out[...], mv_out[0], mv_out[1] = adam(v_ref[...], mv_ref[0], mv_ref[1], g, 0.0)
        for k in range(2):
            ks = slice(k * unit, (k + 1) * unit)
            n_c, mc_out[0:1, ks], mc_out[1:2, ks] = adam(c_ref[ks].reshape(1, unit), mc_ref[0:1, ks], mc_ref[1:2, ks], second[k], 0.0)
            gc_out[ks] = second[k].reshape(unit)
            c_out[ks] = n_c.reshape(unit)
        for s in range(4):
            for cp in go(s):
                cp.wait()

    like = lambda *vs: [sds(v.shape, F32) for v in vs]
    out = pl.pallas_call(
        kern,
        in_specs=[SMEM, VMEM, VMEM, ANY, ANY, VMEM, VMEM, VMEM, VMEM],
        out_specs=[ANY] * 3 + [VMEM] * 6,
        out_shape=like(w, w, mom, vec, vec, mom_vec, bias, bias, mom_bias),
        scratch_shapes=[pltpu.VMEM(w.shape, F32), pltpu.VMEM(mom.shape, F32), pltpu.VMEM(w.shape, F32), pltpu.SemaphoreType.DMA((4, 2)), pltpu.SemaphoreType.DMA((4, 3))],
        compiler_params=params(28),
        cost_estimate=cost(20 * w.size, 28 * w.size, 2 * w.size),
        name="adam_qkv",
    )(core, mine, other, w, mom, vec, mom_vec, bias, mom_bias)
    return out


def permutations(groups, reps):
    flat = lambda f: [(g * reps + r, f(g, r)) for g in range(groups) for r in range(reps)]
    at = lambda g, r: g * reps + r
    far = []
    bit = 8
    while bit < reps:
        far.append(flat(lambda g, r, bit=bit: at(g, r ^ bit)))
        bit *= 2
    return {
        "core": flat(lambda g, r: at(g, r ^ 1)),
        "s1": flat(lambda g, r: at(g ^ (1 + r % 2), r)),
        "s2": flat(lambda g, r: at(g ^ (2 - r % 2), r)),
        "z1": flat(lambda g, r: at(g, r ^ (2 + 2 * (r % 2)))),
        "z2": flat(lambda g, r: at(g, r ^ (4 - 2 * (r % 2)))),
        "twin": flat(lambda g, r: at(g, r ^ 2)),
        "far": far,
        "cores": [[r for r in range(reps) if r % 2 == c] for c in range(2)],
    }


def local(groups, reps, hidden_in, out_grad, segment_ids, rand_blocks, w_qkv, w_out, w_in, w_down, vec_params, bias_hidden,
          moments_qkv, moments_out, moments_in, moments_down, moments_vec, moments_bias):
    perms = permutations(groups, reps)
    seqs, n, d = hidden_in.shape
    nb = rand_blocks.shape[1]
    g = lax.axis_index("group").astype(I32)
    r = lax.axis_index("rep").astype(I32)
    c, z = r % 2, (r // 2) % 4
    where = jnp.stack([g, c, z])
    one, two = 1 + c, 2 - c
    table = jnp.stack([2 * g + c, 2 * g + 1 - c, 2 * (g ^ one) + c, 2 * (g ^ one) + 1 - c,
                       2 * (g ^ two) + 1 - c, 2 * (g ^ two) + c, 2 * (g ^ 3) + c, 2 * (g ^ 3) + 1 - c])
    four = jnp.arange(4, dtype=I32)

    def turn(core, v):
        return jnp.where(core == 0, (v % 2) * 2 + v // 2, v)

    def order(core, quarters):
        return (turn(core, four ^ g)[:, None] * 4 + quarters[None, :]).reshape(16)

    core = c[None]
    orders = jnp.stack([order(k, turn(k, four ^ z)) for k in range(2)])
    plain = jnp.stack([order(k, four) for k in range(2)])
    spots = [jnp.stack([v for src in (c, 1 - c) for k in (p, p + 1) for v in (src, turn(src, jnp.int32(k)) ^ z)]) for p in (0, 2)]
    orders = jnp.where(orders < 8, orders, 8 + 4 * (orders % 4 // 2) + 2 * (orders // 4 % 2) + orders % 2)

    s1, s2, z1, z2, swap = [lambda v, k=k: pperm(v, perms[k]) for k in ("s1", "s2", "z1", "z2", "core")]
    pa0, pa1 = pack_a(where, w_qkv, vec_params.T, jnp.broadcast_to(bias_hidden[None], (8, bias_hidden.shape[0])))
    near_a0 = s1(pa0)
    wo_in, wi_in, wd_in, _ = after((w_out, w_in, w_down), pa0)
    pb0, pb1, pb1_part = pack_b(where, wo_in, wi_in, wd_in)
    near_a0, pb0 = after((near_a0,), pb0)
    far_a = s2(near_a0)
    pa1_l, _ = after((pa1,), near_a0)
    near_a1 = s1(pa1_l)
    side_a0 = swap(near_a0)

    x = hidden_in.reshape(n, d)
    dy = out_grad.reshape(n, d)
    seg_col = segment_ids.reshape(n, 1)
    rr = jnp.pad(rand_blocks[0].T, ((0, 0), (0, HEAD_DIM - nb)), constant_values=-1)
    rand_rows, _ = after((jnp.concatenate([rr, rr], axis=1),), near_a0)

    fq, fk = attn_feats(seg_col, rand_rows, nb)
    far_a, near_a1, _ = after((far_a, near_a1), table, orders, plain, fk, *spots)[:3]
    back_a = swap(far_a)
    side_a1 = swap(near_a1)
    pb0_l, _ = after((pb0,), far_a)
    near_b0 = s1(pb0_l)

    qkv, wq_full, vec, bias = project(x, table, (pa0, pa1, near_a0, near_a1, side_a0, side_a1, far_a, back_a), groups)
    pb1_part, _ = after((pb1_part,), qkv)
    near_b1 = s1(pb1_part)
    o, f = attn_fwd(qkv, fq, fk, nb, 0, 2)
    near_b0, near_b1, o = after((near_b0, near_b1), o)
    far_b = s2(near_b0)
    twin_b1 = pperm(near_b1, perms["twin"])
    side_b0 = swap(near_b0)
    side_b1 = swap(near_b1)
    qkv_l, _ = after((qkv,), near_b0)
    o, f = attn_fwd(qkv_l, fq, fk, nb, 2, 5, (o, f))
    far_b, twin_b1, o = after((far_b, twin_b1), o)
    back_b = swap(far_b)
    tail_b1 = swap(twin_b1)
    qkv_l, _ = after((qkv_l,), far_b)
    o, f = attn_fwd(qkv_l, fq, fk, nb, 5, 6, (o, f), 60)
    y, dr1, do, send, keep, vs, bs = token(
        x, dy, o, vec, bias, table, where, orders, (pb0, pb1, near_b0, side_b0, far_b, back_b, near_b1, twin_b1, side_b1, tail_b1))

    nblk = keep.shape[0]
    up, lo = nblk // 2, nblk // 4
    m, e = lo // 2, lo // 4
    line = Line(vs, core)
    attend = lambda p0, p1: attn_bwd(qkv, f, o, do, fk, nb, p0, p1, line.hold(core))
    got = swap(send)
    part0 = attend(0, 1)
    line.mark = part0[3]
    x1a = s1(line.add(lo, (keep, up + lo), (got, up + lo)))
    part1 = attend(1, 4)
    line.mark = part1[3]
    x2a = s2(line.add(m, (keep, lo + m), (got, lo + m), (x1a, m)))
    x1b = s1(line.add(lo, (keep, up), (got, up)))
    part2 = attend(4, 6)
    line.mark = part2[3]
    v1 = z1(line.add(m, (keep, m), (got, m), (x1a, 0), (x2a, 0)))
    x2b = s2(line.add(m, (keep, lo), (got, lo), (x1b, m)))
    parts = (part0, part1, part2)
    send3, keep3 = grad_qkv(x, parts, line.hold(core), plain, tuple(p[3] for p in parts) + (vs, bs))
    line.mark = send3
    got3 = swap(send3)
    v2 = z2(line.add_kernel(e, (keep, e), (got, e), (x1b, e), (x2b, e), (v1, e)))
    x1_3 = s1(line.add(up, (keep3, up), (got3, up)))
    t0 = line.add(e, (keep, 0), (got, 0), (x1b, 0), (x2b, 0), (v1, 0), (v2, 0))
    for extra in perms["far"]:
        t0 = line.add(e, (t0, 0), (pperm(t0, extra), 0))
    t1 = z2(t0)
    gin = grad_input(dr1, parts, wq_full, line.hold(core))
    line.mark = gin
    x2_3 = s2(line.add(lo, (keep3, lo), (got3, lo), (x1_3, lo)))
    t01 = line.join(t0, t1)
    t23 = z1(t01)
    u01 = swap(t01)
    sum3 = line.add(lo, (keep3, 0), (got3, 0), (x1_3, 0), (x2_3, 0))
    y1 = z1(sum3)
    count = 1.0 / (seqs * groups * reps)
    mats = ((w_down, moments_down), (w_in, moments_in), (w_out, moments_out))
    done = adam_some(line.hold(spots[0]), t01, u01, mats, count)
    line.mark = done[6]
    sum3 = line.add(lo, (sum3, 0), (y1, 0))
    y2 = z2(sum3)
    t23 = line.hold(t23)
    u23 = swap(t23)
    g_down, n_down, m_down, g_in, n_in, m_in, g_out, n_out, m_out = adam_some(line.hold(spots[1]), t23, u23, mats, count, done)
    line.mark = g_out
    sum3 = line.add(lo, (sum3, 0), (y2, 0))
    for extra in perms["far"]:
        sum3 = line.add(lo, (sum3, 0), (pperm(sum3, extra), 0))
    other3 = swap(sum3)
    g_qkv, n_qkv, m_qkv, g_vec, n_vec, m_vec, g_bias, n_bias, m_bias = adam_qkv(
        line.hold(core), sum3, other3, w_qkv, moments_qkv, vec_params.T, moments_vec.transpose(0, 2, 1), bias_hidden, moments_bias, count)
    g_vec, n_vec, m_vec = g_vec.T, n_vec.T, m_vec.transpose(0, 2, 1)
    return (y.reshape(hidden_in.shape), gin.reshape(hidden_in.shape), g_qkv, g_out, g_in, g_down, g_vec, g_bias,
            n_qkv, n_out, n_in, n_down, n_vec, n_bias, m_qkv, m_out, m_in, m_down, m_vec, m_bias)


def solution(mesh):
    groups, reps = mesh.shape["group"], mesh.shape["rep"]
    tok = P(AX, None, None)
    row, mom = P("group", None), P(None, "group", None)

    def run(*args):
        return local(groups, reps, *args)

    return jax.shard_map(
        run,
        mesh=mesh,
        in_specs=(tok, tok, P(AX, None), tok, row, row, row, row, row, P("group"), mom, mom, mom, mom, mom, P(None, "group")),
        out_specs=(tok, tok, row, row, row, row, row, P("group"), row, row, row, row, row, P("group"), mom, mom, mom, mom, mom, P(None, "group")),
        check_vma=False,
    )
```

```python
import jax
import jax.numpy as jnp
from jax import lax
from jax.experimental import pallas as pl
from jax.experimental.pallas import tpu as pltpu
from jax.sharding import PartitionSpec as P

HEAD_DIM = 64
STEP = 4
norm_eps = 1e-05
adam_eps = 1e-08
matrix_decay = 0.1
step_rate = 0.1
BF = jnp.bfloat16
F32 = jnp.float32
I32 = jnp.int32
NEG = -1e30
PAIR = 2 * HEAD_DIM
SQH = 0.7071067811865476
PHI0 = 0.3989422804014327
AX = ("group", "rep")
ANY = pl.BlockSpec(memory_space=pl.ANY)
SMEM = pl.BlockSpec(memory_space=pltpu.SMEM)
VMEM = pl.BlockSpec(memory_space=pltpu.VMEM)
sds = jax.ShapeDtypeStruct


def cost(flops, nbytes, trans=0):
    return pl.CostEstimate(flops=500 * int(flops), bytes_accessed=500 * int(nbytes), transcendentals=500 * int(trans))


def params(mb=60):
    return pltpu.CompilerParams(vmem_limit_bytes=mb * 1024 * 1024)

def nt(a, b):
    return lax.dot_general(a, b, (((1,), (1,)), ((), ())), preferred_element_type=F32)


def nn(a, b):
    return lax.dot_general(a, b, (((1,), (0,)), ((), ())), preferred_element_type=F32)


def tn(a, b):
    return lax.dot_general(a, b, (((0,), (0,)), ((), ())), preferred_element_type=F32)


def split3(v):
    hi = v.astype(BF).astype(F32)
    mid = (v - hi).astype(BF).astype(F32)
    return hi, mid, v - hi - mid


def attn_feats(seg_col, rand_rows, nb):
    n = seg_col.shape[0]

    def kern(seg_ref, rand_ref, fq_ref, fk_ref):
        lane = lax.broadcasted_iota(I32, (n, PAIR), 1) % HEAD_DIM
        blk = lax.broadcasted_iota(I32, (n, PAIR), 0) // (n // nb)
        seg = jnp.broadcast_to(seg_ref[...], (n, PAIR))
        fq = (lane == blk) | ((lane >= nb) & (lane - nb == seg))
        fq_ref[...] = jnp.where(fq, 1.0, 0.0).astype(BF)
        allow = (jnp.abs(lane - blk) <= 1) | (lane == 0) | (lane == nb - 1) | (blk == 0) | (blk == nb - 1)
        for j in range(rand_ref.shape[0]):
            allow = allow | (rand_ref[j : j + 1, :] == blk)
        bad = ((lane < nb) & jnp.logical_not(allow)) | ((lane >= nb) & (lane < nb + 4) & (lane - nb != seg))
        off = (lane >= nb + 4) & (lane < nb + 7)
        fk_ref[...] = jnp.where(bad, NEG, jnp.where(off, -1.0, 0.0)).astype(BF)

    return pl.pallas_call(
        kern,
        out_shape=[sds((n, PAIR), BF)] * 2,
        compiler_params=params(),
        cost_estimate=cost(20 * n * PAIR, 4 * n * PAIR),
        name="attn_feats",
    )(seg_col, rand_rows)


def attn_fwd_kernel(nb, fq_s, fk_s, q_ref, k_ref, v_ref, o_ref, f_ref):
    n = q_ref.shape[0]
    t = 256
    low1 = lax.broadcasted_iota(jnp.int32, (n, PAIR), 1) < HEAD_DIM
    k = k_ref[...]
    v = v_ref[...]
    fk = fk_s[...]
    one = jnp.ones((n, PAIR), BF)
    ks = (jnp.where(low1, k, fk), jnp.where(low1, fk, k))
    vs = (jnp.where(low1, v, one), jnp.where(low1, one, v))
    lowt = lax.broadcasted_iota(jnp.int32, (t, PAIR), 1) < HEAD_DIM
    lane = lax.broadcasted_iota(jnp.int32, (t, PAIR), 1) % HEAD_DIM
    for i in range(n // t):
        rows = pl.ds(i * t, t)
        q = q_ref[rows, :] * jnp.asarray(HEAD_DIM**-0.5, BF)
        fq = fq_s[rows, :]
        acc, top = [], []
        for h in range(2):
            qh = jnp.where(lowt, q, fq) if h == 0 else jnp.where(lowt, fq, q)
            s = nt(qh, ks[h])
            m = jnp.max(s, axis=-1, keepdims=True)
            p = jnp.exp(s - m).astype(BF)
            acc.append(nn(p, vs[h]))
            top.append(m)
        lsw = jnp.where(lowt, acc[1], acc[0])
        o = jnp.where(lowt, acc[0], acc[1]) / pltpu.roll(lsw, HEAD_DIM, 1)
        o_ref[rows, :] = o.astype(BF)
        hi, mid, lo = split3(jnp.where(lowt, top[1], top[0]) + jnp.log(lsw))
        f = jnp.where(lane == nb + 4, hi, jnp.where(lane == nb + 5, mid, lo))
        f_ref[rows, :] = jnp.where((lane >= nb + 4) & (lane < nb + 7), f.astype(BF), fq)


def attn_fwd(qkv, fq, fk, nb, p0, p1, into=(), mb=28):
    n, w3 = qkv.shape
    w = w3 // 3
    pairs = w // PAIR
    blk = lambda off: pl.BlockSpec((n, PAIR), lambda p, off=off: (0, p + off))
    full = lambda a: pl.BlockSpec(a.shape, lambda p: (0, 0))

    def kern(*refs):
        attn_fwd_kernel(nb, *refs[:5], *refs[5 + len(into) :])

    return pl.pallas_call(
        kern,
        grid=(p1 - p0,),
        in_specs=[full(fq), full(fk), blk(p0), blk(pairs + p0), blk(2 * pairs + p0)] + [ANY] * len(into),
        out_specs=[blk(p0), blk(p0)],
        out_shape=[sds((n, w), BF)] * 2,
        input_output_aliases={5 + i: i for i in range(len(into))},
        compiler_params=params(mb),
        cost_estimate=cost(16 * n * n * (p1 - p0) * PAIR, 12 * n * (p1 - p0) * PAIR, 2 * n * n * (p1 - p0)),
        name="attn_fwd",
    )(fq, fk, qkv, qkv, qkv, *into)


def attn_bwd_kernel(nb, fk_s, q_ref, k_ref, v_ref, f_ref, o_ref, do_ref, dq_ref, dk_ref, dv_ref, b_ref):
    n = q_ref.shape[0]
    t = 256
    low1 = lax.broadcasted_iota(jnp.int32, (n, PAIR), 1) < HEAD_DIM
    lane = lax.broadcasted_iota(jnp.int32, (n, PAIR), 1) % HEAD_DIM
    scale = jnp.asarray(HEAD_DIM**-0.5, BF)
    q = q_ref[...] * scale
    f = f_ref[...]
    do = do_ref[...]
    prod = do.astype(F32) * o_ref[...].astype(F32)
    d0 = jnp.sum(jnp.where(low1, prod, 0.0), axis=-1, keepdims=True)
    d1 = jnp.sum(jnp.where(low1, 0.0, prod), axis=-1, keepdims=True)
    hi, mid, lo = split3(jnp.where(low1, d1, d0))
    fd = jnp.where(lane == nb + 4, hi, jnp.where(lane == nb + 5, mid, jnp.where(lane == nb + 6, lo, 0.0))).astype(BF)
    qs = (jnp.where(low1, q, f), jnp.where(low1, f, q))
    dos = (jnp.where(low1, do, fd), jnp.where(low1, fd, do))
    kT = jnp.transpose(k_ref[...] * scale)
    lowt = lax.broadcasted_iota(jnp.int32, (t, PAIR), 1) < HEAD_DIM
    dqT = [None, None]
    dv_sum = jnp.zeros((1, PAIR), F32)
    for i in range(n // t):
        rows = pl.ds(i * t, t)
        k = k_ref[rows, :]
        v = v_ref[rows, :]
        fk = fk_s[rows, :]
        fv = jnp.where(fk == -1.0, fk, jnp.zeros_like(fk))
        dvh, dkh = [], []
        for h in range(2):
            kh = jnp.where(lowt, k, fk) if h == 0 else jnp.where(lowt, fk, k)
            vh = jnp.where(lowt, v, fv) if h == 0 else jnp.where(lowt, fv, v)
            p = jnp.exp(nt(kh, qs[h]))
            ds = (p * nt(vh, dos[h])).astype(BF)
            dvh.append(nn(p.astype(BF), do))
            dkh.append(nn(ds, q))
            part = nn(kT[h * HEAD_DIM : (h + 1) * HEAD_DIM, i * t : (i + 1) * t], ds)
            dqT[h] = part if dqT[h] is None else dqT[h] + part
        dk = jnp.where(lowt, dkh[0], dkh[1]).astype(BF)
        dv = jnp.where(lowt, dvh[0], dvh[1]).astype(BF)
        dk_ref[rows, :] = dk
        dv_ref[rows, :] = dv
        dv_sum = dv_sum + colsum(dv.astype(F32))
    dq = jnp.transpose(jnp.concatenate(dqT, axis=0)).astype(BF)
    dq_ref[...] = dq
    b_ref[...] = jnp.concatenate([colsum(dq.astype(F32)), dv_sum, jnp.zeros((6, PAIR), F32)], axis=0)


def attn_bwd(qkv, f, o, do, fk, nb, p0, p1, turn):
    n, w3 = qkv.shape
    pairs = w3 // 3 // PAIR
    cols = (p1 - p0) * PAIR
    blk = lambda off: pl.BlockSpec((n, PAIR), lambda p, off=off: (0, p + off))
    full = lambda a: pl.BlockSpec(a.shape, lambda p: (0,) * a.ndim)
    return pl.pallas_call(
        lambda turn_ref, *refs: attn_bwd_kernel(nb, *refs),
        grid=(p1 - p0,),
        in_specs=[SMEM, full(fk), blk(p0), blk(pairs + p0), blk(2 * pairs + p0), blk(p0), blk(p0), blk(p0)],
        out_specs=[blk(0), blk(0), blk(0), pl.BlockSpec((8, PAIR), lambda p: (0, p))],
        out_shape=[sds((n, cols), BF)] * 3 + [sds((8, cols), F32)],
        compiler_params=params(28),
        cost_estimate=cost(40 * n * n * cols, 20 * n * cols, n * n * cols // HEAD_DIM),
        name="attn_bwd",
    )(turn, fk, qkv, qkv, qkv, f, o, do)


def grad_qkv(x, parts, core, orders, small=()):
    n, d = x.shape
    blocks = orders.shape[1]
    np_ = len(parts)
    unit, rb = sum(p[0].shape[1] for p in parts) // 2, d // blocks
    rows = 3 * rb + (16 if small else 0)
    g = (blocks, rows, unit)
    ns = len(small)

    def kern(core_ref, ord_ref, x_ref, *refs):
        ds = [[refs[3 * p + part] for p in range(np_)] for part in range(3)]
        extra = refs[3 * np_ : 3 * np_ + ns]
        send_ref, keep_ref, g_s, osem = refs[3 * np_ + ns :]
        x = x_ref[...]
        sels = [1 - (core_ref[0] ^ h) for h in range(2)]
        cat = lambda rs: rs[0][...] if len(rs) == 1 else jnp.concatenate([r[...] for r in rs], axis=1)
        for part in range(3):
            r = tn(x, cat(ds[part])).astype(BF)
            for h in range(2):
                for a in range(blocks):
                    g_s[sels[h], ord_ref[h, a], part * rb : (part + 1) * rb, :] = r[a * rb : (a + 1) * rb, h * unit : (h + 1) * unit]
        if ns:
            vs_ref, bs_ref = extra[-2:]
            groups = bs_ref.shape[0]
            quarters = blocks // groups
            vec = jnp.concatenate([cat(extra[:-2])[0:2], vs_ref[2:8, :]], axis=0)
            share = d // groups
            for gr in range(groups):
                gs = slice(gr * share, (gr + 1) * share)
                lines = [jnp.concatenate([vec[2 * i : 2 * i + 1, gs], vec[2 * i + 1 : 2 * i + 2, gs]], axis=1) for i in range(4)]
                lines += [bs_ref[gr, 0:1, i * (d // 2) : (i + 1) * (d // 2)] for i in range(2)]
                for i in range(2 * quarters):
                    h, q = i // quarters, i % quarters
                    line = lines[i] if i < len(lines) else jnp.zeros((1, d // 2), F32)
                    pieces = [line[:, k * unit : (k + 1) * unit] for k in range(d // 2 // unit)]
                    tile = jnp.concatenate(pieces + [jnp.zeros((16 - len(pieces), unit), F32)], axis=0)
                    g_s[sels[h], ord_ref[h, gr * quarters + q], 3 * rb : 3 * rb + 16, :] = tile.astype(BF)
        out = [pltpu.make_async_copy(g_s.at[0], send_ref, osem.at[0]), pltpu.make_async_copy(g_s.at[1], keep_ref, osem.at[1])]
        for cp in out:
            cp.start()
        for cp in out:
            cp.wait()

    flat = [a for p in parts for a in p[:3]] + list(small)
    return pl.pallas_call(
        kern,
        in_specs=[SMEM, SMEM] + [VMEM] * (1 + len(flat)),
        out_specs=[ANY, ANY],
        out_shape=[sds(g, BF)] * 2,
        scratch_shapes=[pltpu.VMEM((2,) + g, BF), pltpu.SemaphoreType.DMA((2,))],
        compiler_params=params(28),
        cost_estimate=cost(12 * n * d * unit, 14 * n * d),
        name="grad_qkv",
    )(core, orders, x, *flat)


def norm(r, g, c):
    w = r.shape[-1]
    center = r - jnp.sum(r, axis=-1, keepdims=True) * (1.0 / w)
    inv = lax.rsqrt(jnp.sum(center * center, axis=-1, keepdims=True) * (1.0 / w) + norm_eps)
    n = center * inv
    return n * g + c, n, inv


def norm_back(dy, g, n, inv):
    w = dy.shape[-1]
    e = dy * g
    a = jnp.sum(e, axis=-1, keepdims=True) * (1.0 / w)
    b = jnp.sum(e * n, axis=-1, keepdims=True) * (1.0 / w)
    return inv * (e - a - n * b)


def colsum(a):
    return jnp.sum(a, axis=0, keepdims=True)


def pack_a(where, w, vec_t, bias):
    rows, cols = w.shape
    half = rows // 2

    def kern(where_ref, w_ref, vec_ref, bias_ref, *outs):
        for pos in range(2):
            h = pos ^ where_ref[1]
            outs[pos][0, 0:half, :] = w_ref[pl.ds(pl.multiple_of(h * half, 8), half), :].astype(BF)
            pad = lambda v: jnp.concatenate([v, jnp.zeros((v.shape[0], cols - v.shape[1]), F32)], axis=1)
            small = jnp.where(h == 0, pad(vec_ref[...]), pad(bias_ref[...]))
            outs[pos][0, half : half + 16, :] = jnp.concatenate([small, small], axis=0).astype(BF)

    return pl.pallas_call(
        kern,
        in_specs=[SMEM, VMEM, VMEM, VMEM],
        out_specs=[VMEM, VMEM],
        out_shape=[sds((1, half + 16, cols), BF)] * 2,
        compiler_params=params(28),
        cost_estimate=cost(0, 3 * w.size * 2),
        name="pack_a",
    )(where, w, vec_t, bias)


def pack_b(where, wo, wi, wd):
    rows, w = wo.shape
    half = rows // 2
    nf = wi.shape[1] // w
    nd = wd.shape[0] // rows

    def kern(where_ref, wo_ref, wi_ref, wd_ref, *outs):
        for pos in range(2):
            h = pos ^ where_ref[1]
            hs = pl.ds(pl.multiple_of(h * half, 8), half)
            outs[pos][0, 0] = wo_ref[hs, :].astype(BF)
            for j in range(nf):
                outs[pos][0, 1 + j] = wi_ref[hs, j * w : (j + 1) * w].astype(BF)
            for j in range(nd):
                at = pl.multiple_of((h * nd + j) * half, 8)
                outs[pos][0, 1 + nf + j] = wd_ref[pl.ds(at, half), :].astype(BF)
        part = pl.ds(pl.multiple_of(where_ref[2] % 2 * (half // 2), 16), half // 2)
        outs[2][...] = outs[1][:, :, part, :]

    blocks = 1 + nf + nd
    return pl.pallas_call(
        kern,
        in_specs=[SMEM, VMEM, VMEM, VMEM],
        out_specs=[VMEM] * 3,
        out_shape=[sds((1, blocks, half, w), BF)] * 2 + [sds((1, blocks, half // 2, w), BF)],
        compiler_params=params(28),
        cost_estimate=cost(0, 6 * (wo.size + wi.size + wd.size)),
        name="pack_b",
    )(where, wo, wi, wd)


def pperm(a, pairs):
    return lax.ppermute(a, AX, pairs)


def after(late, *early):
    out = lax.optimization_barrier(tuple(late) + early)
    return out[: len(late) + 1]


def piece_refs(refs):
    out = []
    for ref in refs:
        out += [ref.at[k] for k in range(ref.shape[0])]
    return out


def project(x, table, parts, groups, t=256):
    n, d = x.shape
    _, hp, cols = parts[0].shape
    half = hp - 16
    share = 2 * half

    def kern(tab_ref, x_ref, *refs):
        pieces = piece_refs(refs[:8])
        qkv_ref, w_out, vec_ref, bias_ref, w_s, e_s, sems, osem = refs[8:]
        first = pl.program_id(0) == 0
        last = pl.program_id(0) == pl.num_programs(0) - 1

        def copies():
            out = []
            for i, p in enumerate(pieces):
                u = tab_ref[i]
                out.append(pltpu.make_async_copy(p.at[pl.ds(0, half)], w_s.at[pl.ds(pl.multiple_of(u * half, 16), half)], sems.at[2 * i]))
                out.append(pltpu.make_async_copy(p.at[pl.ds(half, 16)], e_s.at[u], sems.at[2 * i + 1]))
            return out

        def whole():
            return pltpu.make_async_copy(w_s, w_out, osem)

        @pl.when(first)
        def _():
            for cp in copies():
                cp.start()
            for cp in copies():
                cp.wait()
            whole().start()
            vec_ref[...] = jnp.concatenate([e_s[2 * g, 0:8, 0:share].astype(F32) for g in range(groups)], axis=1)
            for g in range(groups):
                bias_ref[g] = e_s[2 * g + 1, 0:8, 0:d].astype(F32)

        qb = jnp.concatenate([vec_ref[0:1, :], jnp.zeros((1, d), F32), vec_ref[1:2, :]], axis=1)
        qkv_ref[...] = (nn(x_ref[...], w_s[...]) + qb).astype(BF)

        @pl.when(last)
        def _():
            whole().wait()

    return pl.pallas_call(
        kern,
        grid=(n // t,),
        in_specs=[SMEM, pl.BlockSpec((t, d), lambda i: (i, 0))] + [ANY] * 8,
        out_specs=[pl.BlockSpec((t, cols), lambda i: (i, 0)), ANY, pl.BlockSpec((8, d), lambda i: (0, 0)), pl.BlockSpec((groups, 8, d), lambda i: (0, 0, 0))],
        out_shape=[sds((n, cols), BF), sds((d, cols), BF), sds((8, d), F32), sds((groups, 8, d), F32)],
        scratch_shapes=[pltpu.VMEM((d, cols), BF), pltpu.VMEM((2 * groups, 16, cols), BF), pltpu.SemaphoreType.DMA((16,)), pltpu.SemaphoreType.DMA],
        compiler_params=params(),
        cost_estimate=cost(2 * n * d * cols, 2 * (n * d + 2 * d * cols + n * cols)),
        name="project",
    )(table, x, *parts)


def token(x, dy, o, vec, bias, table, core, orders, parts):
    n, w = x.shape
    _, k9, half, _ = parts[0].shape
    nf = bias.shape[0]
    nd = k9 - 1 - nf
    ff = nf * w
    nblk = orders.shape[1]
    nq = nblk // nf
    unit = w // 2
    rb = w // nblk
    db = w // (2 * nq)
    t = n // 2

    def kern(tab_ref, core_ref, ord_ref, vec_any, bias_any, x_ref, dy_ref, o_ref, *refs):
        parity = core_ref[2] % 2
        whole, upper = [(0, 0), (1, 1), (2, 2), (3, 4), (4, 6), (5, 7)], [(6, 3, parity), (7, 3, 1 - parity), (8, 5, parity), (9, 5, 1 - parity)]
        pieces = [(refs[k].at[0], tab_ref[u], 0, half) for k, u in whole] + [(refs[k].at[0], tab_ref[u], p * (half // 2), half // 2) for k, u, p in upper]
        (y_ref, dr1_ref, do_ref, send_ref, keep_ref, vs_ref, bs_ref,
         wo_s, wi_s, wd_s, x_s, dy_s, o_s, n1_s, inv_s, x1b_s, hb_s, sl_s, acc_s, dfb_s, y_s, g_s, vec_ref, bias_ref, sems, isem, osem) = refs[10:]

        def copies(kind):
            out = []
            for i, (p, u, r0, size) in enumerate(pieces):
                rows = pl.ds(pl.multiple_of(u * half + r0, 16), size)
                if kind == 0:
                    out.append(pltpu.make_async_copy(p.at[0], wo_s.at[rows], sems.at[0, i]))
                elif kind == 1:
                    out.append(pltpu.make_async_copy(p.at[pl.ds(1, nf)], wi_s.at[:, rows], sems.at[1, i]))
                else:
                    out.append(pltpu.make_async_copy(p.at[pl.ds(1 + nf, nd)], wd_s.at[pl.ds(u * nd, nd), pl.ds(pl.multiple_of(r0, 16), size)], sems.at[2, i]))
            return out

        c_v = [pltpu.make_async_copy(vec_any, vec_ref, isem.at[3]), pltpu.make_async_copy(bias_any, bias_ref, isem.at[4])]
        c_o = pltpu.make_async_copy(o_ref, o_s, isem.at[0])
        c_x = pltpu.make_async_copy(x_ref, x_s, isem.at[1])
        c_dy = pltpu.make_async_copy(dy_ref, dy_s, isem.at[2])
        for cp in c_v + copies(0) + [c_o, c_x] + copies(1) + copies(2) + [c_dy]:
            cp.start()
        for cp in c_v:
            cp.wait()
        row = lambda j: vec_ref[j : j + 1, :]
        bo, g1, c1, bd, g2, c2 = [row(j) for j in range(2, 8)]
        per = wd_s.shape[0] // nf
        down = lambda j: wd_s[pl.ds(j * per, per)].reshape(w, w)
        for cp in copies(0) + [c_o, c_x]:
            cp.wait()

        def first(i, _):
            rows = pl.ds(pl.multiple_of(i * t, t), t)
            x1, n1, inv1 = norm(x_s[rows, :].astype(F32) + (nn(o_s[rows, :], wo_s[...]) + bo), g1, c1)
            n1_s[rows, :] = n1
            inv_s[rows, :] = jnp.broadcast_to(inv1, (t, 128))
            x1b_s[rows, :] = x1.astype(BF)
            acc_s[rows, :] = x1 + bd
            return 0

        lax.fori_loop(0, 2, first, 0)
        for cp in copies(1):
            cp.wait()

        def up(j, _):
            for i in range(2):
                rows = slice(i * t, (i + 1) * t)
                h = nn(x1b_s[rows, :], wi_s[j]) + bias_ref[j, 0:1, :]
                cdf = 0.5 * (1.0 + lax.erf(h * SQH))
                hb_s[j, rows, :] = (h * cdf).astype(BF)
                sl_s[j, rows, :] = (cdf + h * (jnp.exp(-0.5 * (h * h)) * PHI0)).astype(BF)
            return 0

        lax.fori_loop(0, nf, up, 0)
        for cp in copies(2) + [c_dy]:
            cp.wait()
        vs_ref[...] = jnp.zeros_like(vs_ref)

        def top(i, _):
            rows = pl.ds(pl.multiple_of(i * t, t), t)
            r2 = acc_s[rows, :]
            for j in range(nf):
                r2 = r2 + nn(hb_s[j, rows, :], down(j))
            y, n2, inv2 = norm(r2, g2, c2)
            y_s[rows, :] = y
            dyf = dy_s[rows, :].astype(F32)
            dr2 = norm_back(dyf, g2, n2, inv2)
            acc_s[rows, :] = dr2
            dfb_s[rows, :] = dr2.astype(BF)
            vs_ref[5:6, :] += colsum(dr2)
            vs_ref[6:7, :] += colsum(dyf * n2)
            vs_ref[7:8, :] += colsum(dyf)
            return 0

        lax.fori_loop(0, n // t, top, 0)
        c_y = pltpu.make_async_copy(y_s, y_ref, osem.at[0])
        c_y.start()

        def back(j, _):
            for i in range(2):
                rows = slice(i * t, (i + 1) * t)
                dh = (nt(dfb_s[rows, :], down(j)) * sl_s[j, rows, :].astype(F32)).astype(BF)
                sl_s[j, rows, :] = dh
                s = jnp.broadcast_to(colsum(dh.astype(F32)), (8, w))
                bs_ref[j] = s if i == 0 else bs_ref[j] + s
                acc_s[rows, :] += nt(dh, wi_s[j])
            gd = tn(hb_s[j], dfb_s[...]).astype(BF)
            for h in range(2):
                sel = 1 - (core_ref[1] ^ h)
                for q in range(nq):
                    r0 = (h * nq + q) * db
                    pos = ord_ref[h, j * nq + q]
                    for k in range(2):
                        g_s[sel, pos, k * db : (k + 1) * db, :] = gd[r0 : r0 + db, k * unit : (k + 1) * unit]
            gi = tn(x1b_s[...], sl_s[j]).astype(BF)
            h = j // (nf // 2)
            sel = 1 - (core_ref[1] ^ h)
            for a in range(nblk):
                pos = ord_ref[h, a]
                for k in range(2):
                    at = pl.multiple_of(2 * db + ((j % (nf // 2)) * 2 + k) * rb, 16)
                    g_s[sel, pos, pl.ds(at, rb), :] = gi[a * rb : (a + 1) * rb, k * unit : (k + 1) * unit]
            return 0

        lax.fori_loop(0, nf, back, 0)
        most = pl.ds(0, 2 * db + nf * rb)
        outs = [pltpu.make_async_copy(g_s.at[k, :, most], (send_ref, keep_ref)[k].at[:, most], osem.at[1 + k]) for k in range(2)]
        for cp in outs:
            cp.start()

        def leave(i):
            rows = pl.ds(pl.multiple_of(i * t, t), t)
            return [pltpu.make_async_copy(acc_s.at[rows], dr1_ref.at[rows], osem.at[5 + 2 * i]), pltpu.make_async_copy(dy_s.at[rows], do_ref.at[rows], osem.at[6 + 2 * i])]

        def low(i, _):
            rows = pl.ds(pl.multiple_of(i * t, t), t)
            dx1 = acc_s[rows, :]
            n1 = n1_s[rows, :]
            dr1 = norm_back(dx1, g1, n1, inv_s[rows, 0:1])
            acc_s[rows, :] = dr1
            dab = dr1.astype(BF)
            x_s[rows, :] = dab
            dy_s[rows, :] = nt(dab, wo_s[...]).astype(BF)
            vs_ref[2:3, :] += colsum(dr1)
            vs_ref[3:4, :] += colsum(dx1 * n1)
            vs_ref[4:5, :] += colsum(dx1)
            for cp in leave(i):
                cp.start()
            return 0

        lax.fori_loop(0, 2, low, 0)
        go = tn(o_s[...], x_s[...]).astype(BF)
        for h in range(2):
            sel = 1 - (core_ref[1] ^ h)
            for a in range(nblk):
                g_s[sel, ord_ref[h, a], 2 * db + nf * rb : 2 * db + (nf + 1) * rb, :] = go[a * rb : (a + 1) * rb, h * unit : (h + 1) * unit]
        last = pl.ds(2 * db + nf * rb, rb)
        more = [pltpu.make_async_copy(g_s.at[k, :, last], (send_ref, keep_ref)[k].at[:, last], osem.at[3 + k]) for k in range(2)]
        for cp in more:
            cp.start()
        for cp in [c_y] + outs + leave(0) + leave(1) + more:
            cp.wait()

    gs = (nblk, 2 * db + (nf + 1) * rb, unit)
    vm = lambda s, dt=BF: pltpu.VMEM(s, dt)
    return pl.pallas_call(
        kern,
        in_specs=[SMEM, SMEM, SMEM] + [ANY] * 15,
        out_specs=[ANY] * 5 + [VMEM, VMEM],
        out_shape=[sds((n, w), F32), sds((n, w), F32), sds((n, w), BF), sds(gs, BF), sds(gs, BF), sds((8, w), F32), sds((nf, 8, w), F32)],
        scratch_shapes=[vm((w, w)), vm((nf, w, w)), vm((ff // half, half, w)), vm((n, w)), vm((n, w)), vm((n, w)), vm((n, w), F32), vm((n, 128), F32),
                        vm((n, w)), vm((nf, n, w)), vm((nf, n, w)), vm((n, w), F32), vm((n, w)), vm((n, w), F32), vm((2,) + gs), vm(vec.shape, F32), vm(bias.shape, F32),
                        pltpu.SemaphoreType.DMA((3, 10)), pltpu.SemaphoreType.DMA((5,)), pltpu.SemaphoreType.DMA((9,))],
        compiler_params=params(),
        cost_estimate=cost(2 * n * w * (3 * w + 6 * ff), 2 * (n * 8 * w + 3 * w * (w + 2 * ff)), 2 * n * ff),
        name="token",
    )(table, core, orders, vec, bias, x, dy, o, *parts)


def grad_input(dr1, parts, w, turn, t=256):
    n, d = dr1.shape
    k = len(parts)

    def kern(turn_ref, r_ref, w_ref, *refs):
        out_ref = refs[-1]
        out = r_ref[...]
        for part in range(3):
            g = jnp.concatenate([refs[3 * p + part][...] for p in range(k)], axis=1)
            out = out + nt(g, w_ref[:, part * d : (part + 1) * d])
        out_ref[...] = out

    rows = lambda c: pl.BlockSpec((t, c), lambda i: (i, 0))
    flat = [a for p in parts for a in p[:3]]
    return pl.pallas_call(
        kern,
        grid=(n // t,),
        in_specs=[SMEM, rows(d), pl.BlockSpec(w.shape, lambda i: (0, 0))] + [rows(a.shape[1]) for a in flat],
        out_specs=rows(d),
        out_shape=sds((n, d), F32),
        compiler_params=params(28),
        cost_estimate=cost(6 * n * d * d, n * d * 14 + 2 * w.size),
        name="grad_input",
    )(turn, dr1, w, *flat)


def total(*terms):
    out = terms[0].astype(F32)
    for a in terms[1:]:
        out = out + a.astype(F32)
    return out.astype(BF)


def total_kernel(turn, n, *terms):
    block = terms[0][0].shape[1:]
    k = len(terms)

    def kern(turn_ref, *refs):
        ins, out_ref, scr, out_s, isem, osem = refs[:k], refs[k], refs[k + 1], refs[k + 2], refs[k + 3], refs[k + 4]

        def come(i):
            return [pltpu.make_async_copy(ins[t].at[terms[t][1] + i], scr.at[t, i], isem.at[t, i]) for t in range(k)]

        def go(i):
            return pltpu.make_async_copy(out_s.at[i], out_ref.at[i], osem.at[i])

        for i in range(n):
            for cp in come(i):
                cp.start()
        for i in range(n):
            for cp in come(i):
                cp.wait()
            out = scr[0, i].astype(F32)
            for t in range(1, k):
                out = out + scr[t, i].astype(F32)
            out_s[i] = out.astype(BF)
            go(i).start()
        for i in range(n):
            go(i).wait()

    return pl.pallas_call(
        kern,
        in_specs=[SMEM] + [ANY] * k,
        out_specs=ANY,
        out_shape=sds((n,) + block, BF),
        scratch_shapes=[pltpu.VMEM((k, n) + block, BF), pltpu.VMEM((n,) + block, BF), pltpu.SemaphoreType.DMA((k, n)), pltpu.SemaphoreType.DMA((n,))],
        compiler_params=params(16),
        cost_estimate=cost(10**9, 0),
        name="total",
    )(turn, *[a for a, _ in terms])


class Line:
    def __init__(self, mark, core):
        self.mark = mark
        self.core = core

    def hold(self, *arrays):
        out = lax.optimization_barrier(arrays + (self.mark,))
        return out[0] if len(arrays) == 1 else out[:-1]

    def add(self, n, *terms):
        held = (self.hold(terms[0][0]),) + tuple(a for a, _ in terms[1:])
        self.mark = total(*[a[first : first + n] for a, (_, first) in zip(held, terms)])
        return self.mark

    def add_kernel(self, n, *terms):
        self.mark = total_kernel(self.hold(self.core), n, *terms)
        return self.mark

    def join(self, a, b):
        self.mark = jnp.concatenate([self.hold(a), b], axis=0)
        return self.mark


def adam(w, m, u, g, decay):
    correct = 1.0 - 0.5**STEP
    m = 0.5 * m + 0.5 * g
    u = 0.5 * u + 0.5 * g * g
    return w - step_rate * (m * (1.0 / correct) / (jnp.sqrt(u * (1.0 / correct)) + adam_eps) + decay * w), m, u


def adam_some(spots, mine, other, mats, count, into=()):
    half = mine.shape[0]
    (w_down, _), (w_in, _), (w_out, _) = mats
    rd, ri, unit = w_down.shape[0] // 8, w_in.shape[0] // 4, mine.shape[2]
    ki = w_in.shape[1] // 2 // unit
    blocks = [(rd, w_down.shape[1]), (ri, w_in.shape[1] // 2), (ri, w_out.shape[1] // 2)]
    steps = 2 * half
    ni = len(into)

    def kern(spots_ref, a_ref, b_ref, *refs):
        olds, news = refs[:6], refs[6 + ni : 15 + ni]
        src_s, isem, osem = refs[15 + ni], refs[16 + ni], refs[17 + ni]
        bufs = [refs[18 + ni + 3 * k : 21 + ni + 3 * k] for k in range(3)]

        def place(k, s):
            h, q = spots_ref[2 * s], spots_ref[2 * s + 1]
            r, c = blocks[k]
            if k == 0:
                return pl.ds(pl.multiple_of((h * 4 + q) * r, 8), r), pl.ds(0, c)
            return pl.ds(pl.multiple_of(q * r, 8), r), pl.ds(pl.multiple_of(h * c, 128), c)

        def come(s):
            out = [pltpu.make_async_copy((a_ref, b_ref)[s // half].at[s % half], src_s.at[s], isem.at[s, 0])]
            for k in range(3):
                rows, cols = place(k, s)
                out.append(pltpu.make_async_copy(olds[2 * k].at[rows, cols], bufs[k][0].at[s], isem.at[s, 1 + 2 * k]))
                out.append(pltpu.make_async_copy(olds[2 * k + 1].at[:, rows, cols], bufs[k][1].at[s], isem.at[s, 2 + 2 * k]))
            return out

        def go(s):
            out = []
            for k in range(3):
                rows, cols = place(k, s)
                out.append(pltpu.make_async_copy(bufs[k][2].at[s], news[3 * k].at[rows, cols], osem.at[s, 3 * k]))
                out.append(pltpu.make_async_copy(bufs[k][0].at[s], news[3 * k + 1].at[rows, cols], osem.at[s, 3 * k + 1]))
                out.append(pltpu.make_async_copy(bufs[k][1].at[s], news[3 * k + 2].at[:, rows, cols], osem.at[s, 3 * k + 2]))
            return out

        for s in range(steps):
            for cp in come(s):
                cp.start()
        for s in range(steps):
            for cp in come(s):
                cp.wait()
            g = src_s[s].astype(F32) * count
            at = 2 * rd
            grads = [jnp.concatenate([g[:rd], g[rd:at]], axis=1),
                     jnp.concatenate([g[at + k * ri : at + (k + 1) * ri] for k in range(ki)], axis=1),
                     g[at + ki * ri : at + (ki + 1) * ri]]
            for k in range(3):
                w_s, m_s, g_s = bufs[k]
                g_s[s] = grads[k]
                w_s[s], m_s[s, 0], m_s[s, 1] = adam(w_s[s], m_s[s, 0], m_s[s, 1], grads[k], matrix_decay)
            for cp in go(s):
                cp.start()
        for s in range(steps):
            for cp in go(s):
                cp.wait()

    shapes, args, scratch = [], [], []
    for (w, m), b in zip(mats, blocks):
        shapes += [sds(w.shape, F32), sds(w.shape, F32), sds(m.shape, F32)]
        args += [w, m]
        scratch += [pltpu.VMEM((steps,) + b, F32), pltpu.VMEM((steps, 2) + b, F32), pltpu.VMEM((steps,) + b, F32)]
    size = sum(w.size for w, _ in mats) // 2
    return pl.pallas_call(
        kern,
        in_specs=[SMEM] + [ANY] * (8 + ni),
        out_specs=[ANY] * 9,
        out_shape=shapes,
        scratch_shapes=[pltpu.VMEM((steps,) + mine.shape[1:], BF), pltpu.SemaphoreType.DMA((steps, 7)), pltpu.SemaphoreType.DMA((steps, 9))] + scratch,
        input_output_aliases={9 + k: k for k in range(ni)},
        compiler_params=params(28),
        cost_estimate=cost(20 * size, 28 * size, 2 * size),
        name="adam_some",
    )(spots, mine, other, *args, *into)


def adam_qkv(core, mine, other, w, mom, vec, mom_vec, bias, mom_bias, count):
    rb, cols = w.shape[0] // 4, w.shape[1]
    unit = mine.shape[2]
    share = vec.shape[1]

    def kern(core_ref, a_ref, b_ref, w_ref, m_ref, v_ref, mv_ref, c_ref, mc_ref,
             g_out, w_out, m_out, gv_out, v_out, mv_out, gc_out, c_out, mc_out, w_s, m_s, g_s, isem, osem):
        at = lambda s: pl.ds(s * rb, rb)

        def come(s):
            return [pltpu.make_async_copy(w_ref.at[at(s)], w_s.at[at(s)], isem.at[s, 0]),
                    pltpu.make_async_copy(m_ref.at[:, at(s)], m_s.at[:, at(s)], isem.at[s, 1])]

        def go(s):
            return [pltpu.make_async_copy(g_s.at[at(s)], g_out.at[at(s)], osem.at[s, 0]),
                    pltpu.make_async_copy(w_s.at[at(s)], w_out.at[at(s)], osem.at[s, 1]),
                    pltpu.make_async_copy(m_s.at[:, at(s)], m_out.at[:, at(s)], osem.at[s, 2])]

        for s in range(4):
            for cp in come(s):
                cp.start()
        flip = core_ref[0] == 1
        for s in range(4):
            for cp in come(s):
                cp.wait()
            a, b = a_ref[s, 0 : 3 * rb, :].astype(F32) * count, b_ref[s, 0 : 3 * rb, :].astype(F32) * count
            first, second = jnp.where(flip, b, a), jnp.where(flip, a, b)
            g = jnp.concatenate([v[p * rb : (p + 1) * rb] for p in range(3) for v in (first, second)], axis=1)
            rows = slice(s * rb, (s + 1) * rb)
            g_s[rows, :] = g
            w_s[rows, :], m_s[0, rows, :], m_s[1, rows, :] = adam(w_s[rows, :], m_s[0, rows, :], m_s[1, rows, :], g, matrix_decay)
            for cp in go(s):
                cp.start()
        line = lambda ref: [ref[q, 3 * rb : 3 * rb + 8, :].astype(F32)[0:1] * count for q in range(4)]
        own, sib = line(a_ref), line(b_ref)
        first, second = [jnp.where(flip, y, x) for x, y in zip(own, sib)], [jnp.where(flip, x, y) for x, y in zip(own, sib)]
        g = jnp.concatenate([v[:, k * share : (k + 1) * share] for v in first for k in range(unit // share)], axis=0)
        gv_out[...] = g
        v_out[...], mv_out[0], mv_out[1] = adam(v_ref[...], mv_ref[0], mv_ref[1], g, 0.0)
        for k in range(2):
            ks = slice(k * unit, (k + 1) * unit)
            n_c, mc_out[0:1, ks], mc_out[1:2, ks] = adam(c_ref[ks].reshape(1, unit), mc_ref[0:1, ks], mc_ref[1:2, ks], second[k], 0.0)
            gc_out[ks] = second[k].reshape(unit)
            c_out[ks] = n_c.reshape(unit)
        for s in range(4):
            for cp in go(s):
                cp.wait()

    like = lambda *vs: [sds(v.shape, F32) for v in vs]
    out = pl.pallas_call(
        kern,
        in_specs=[SMEM, VMEM, VMEM, ANY, ANY, VMEM, VMEM, VMEM, VMEM],
        out_specs=[ANY] * 3 + [VMEM] * 6,
        out_shape=like(w, w, mom, vec, vec, mom_vec, bias, bias, mom_bias),
        scratch_shapes=[pltpu.VMEM(w.shape, F32), pltpu.VMEM(mom.shape, F32), pltpu.VMEM(w.shape, F32), pltpu.SemaphoreType.DMA((4, 2)), pltpu.SemaphoreType.DMA((4, 3))],
        compiler_params=params(28),
        cost_estimate=cost(20 * w.size, 28 * w.size, 2 * w.size),
        name="adam_qkv",
    )(core, mine, other, w, mom, vec, mom_vec, bias, mom_bias)
    return out


def permutations(groups, reps):
    flat = lambda f: [(g * reps + r, f(g, r)) for g in range(groups) for r in range(reps)]
    at = lambda g, r: g * reps + r
    far = []
    bit = 8
    while bit < reps:
        far.append(flat(lambda g, r, bit=bit: at(g, r ^ bit)))
        bit *= 2
    return {
        "core": flat(lambda g, r: at(g, r ^ 1)),
        "s1": flat(lambda g, r: at(g ^ (1 + r % 2), r)),
        "s2": flat(lambda g, r: at(g ^ (2 - r % 2), r)),
        "z1": flat(lambda g, r: at(g, r ^ (2 + 2 * (r % 2)))),
        "z2": flat(lambda g, r: at(g, r ^ (4 - 2 * (r % 2)))),
        "twin": flat(lambda g, r: at(g, r ^ 2)),
        "far": far,
        "cores": [[r for r in range(reps) if r % 2 == c] for c in range(2)],
    }


def local(groups, reps, hidden_in, out_grad, segment_ids, rand_blocks, w_qkv, w_out, w_in, w_down, vec_params, bias_hidden,
          moments_qkv, moments_out, moments_in, moments_down, moments_vec, moments_bias):
    perms = permutations(groups, reps)
    seqs, n, d = hidden_in.shape
    nb = rand_blocks.shape[1]
    g = lax.axis_index("group").astype(I32)
    r = lax.axis_index("rep").astype(I32)
    c, z = r % 2, (r // 2) % 4
    where = jnp.stack([g, c, z])
    one, two = 1 + c, 2 - c
    table = jnp.stack([2 * g + c, 2 * g + 1 - c, 2 * (g ^ one) + c, 2 * (g ^ one) + 1 - c,
                       2 * (g ^ two) + 1 - c, 2 * (g ^ two) + c, 2 * (g ^ 3) + c, 2 * (g ^ 3) + 1 - c])
    four = jnp.arange(4, dtype=I32)

    def turn(core, v):
        return jnp.where(core == 0, (v % 2) * 2 + v // 2, v)

    def order(core, quarters):
        return (turn(core, four ^ g)[:, None] * 4 + quarters[None, :]).reshape(16)

    core = c[None]
    orders = jnp.stack([order(k, turn(k, four ^ z)) for k in range(2)])
    plain = jnp.stack([order(k, four) for k in range(2)])
    spots = [jnp.stack([v for src in (c, 1 - c) for k in (p, p + 1) for v in (src, turn(src, jnp.int32(k)) ^ z)]) for p in (0, 2)]
    orders = jnp.where(orders < 8, orders, 8 + 4 * (orders % 4 // 2) + 2 * (orders // 4 % 2) + orders % 2)

    s1, s2, z1, z2, swap = [lambda v, k=k: pperm(v, perms[k]) for k in ("s1", "s2", "z1", "z2", "core")]
    pa0, pa1 = pack_a(where, w_qkv, vec_params.T, jnp.broadcast_to(bias_hidden[None], (8, bias_hidden.shape[0])))
    near_a0 = s1(pa0)
    wo_in, wi_in, wd_in, _ = after((w_out, w_in, w_down), pa0)
    pb0, pb1, pb1_part = pack_b(where, wo_in, wi_in, wd_in)
    near_a0, pb0 = after((near_a0,), pb0)
    far_a = s2(near_a0)
    pa1_l, _ = after((pa1,), near_a0)
    near_a1 = s1(pa1_l)
    side_a0 = swap(near_a0)

    x = hidden_in.reshape(n, d)
    dy = out_grad.reshape(n, d)
    seg_col = segment_ids.reshape(n, 1)
    rr = jnp.pad(rand_blocks[0].T, ((0, 0), (0, HEAD_DIM - nb)), constant_values=-1)
    rand_rows, _ = after((jnp.concatenate([rr, rr], axis=1),), near_a0)

    fq, fk = attn_feats(seg_col, rand_rows, nb)
    far_a, near_a1, _ = after((far_a, near_a1), table, orders, plain, fk, *spots)[:3]
    back_a = swap(far_a)
    side_a1 = swap(near_a1)
    pb0_l, _ = after((pb0,), far_a)
    near_b0 = s1(pb0_l)

    qkv, wq_full, vec, bias = project(x, table, (pa0, pa1, near_a0, near_a1, side_a0, side_a1, far_a, back_a), groups)
    pb1_part, _ = after((pb1_part,), qkv)
    near_b1 = s1(pb1_part)
    o, f = attn_fwd(qkv, fq, fk, nb, 0, 2)
    near_b0, near_b1, o = after((near_b0, near_b1), o)
    far_b = s2(near_b0)
    twin_b1 = pperm(near_b1, perms["twin"])
    side_b0 = swap(near_b0)
    side_b1 = swap(near_b1)
    qkv_l, _ = after((qkv,), near_b0)
    o, f = attn_fwd(qkv_l, fq, fk, nb, 2, 5, (o, f))
    far_b, twin_b1, o = after((far_b, twin_b1), o)
    back_b = swap(far_b)
    tail_b1 = swap(twin_b1)
    qkv_l, _ = after((qkv_l,), far_b)
    o, f = attn_fwd(qkv_l, fq, fk, nb, 5, 6, (o, f), 60)
    y, dr1, do, send, keep, vs, bs = token(
        x, dy, o, vec, bias, table, where, orders, (pb0, pb1, near_b0, side_b0, far_b, back_b, near_b1, twin_b1, side_b1, tail_b1))

    nblk = keep.shape[0]
    up, lo = nblk // 2, nblk // 4
    m, e = lo // 2, lo // 4
    line = Line(vs, core)
    attend = lambda p0, p1: attn_bwd(qkv, f, o, do, fk, nb, p0, p1, line.hold(core))
    got = swap(send)
    part0 = attend(0, 1)
    line.mark = part0[3]
    x1a = s1(line.add(lo, (keep, up + lo), (got, up + lo)))
    part1 = attend(1, 4)
    line.mark = part1[3]
    x2a = s2(line.add(m, (keep, lo + m), (got, lo + m), (x1a, m)))
    x1b = s1(line.add(lo, (keep, up), (got, up)))
    part2 = attend(4, 6)
    line.mark = part2[3]
    v1 = z1(line.add(m, (keep, m), (got, m), (x1a, 0), (x2a, 0)))
    x2b = s2(line.add(m, (keep, lo), (got, lo), (x1b, m)))
    parts = (part0, part1, part2)
    send3, keep3 = grad_qkv(x, parts, line.hold(core), plain, tuple(p[3] for p in parts) + (vs, bs))
    line.mark = send3
    got3 = swap(send3)
    v2 = z2(line.add_kernel(e, (keep, e), (got, e), (x1b, e), (x2b, e), (v1, e)))
    x1_3 = s1(line.add(up, (keep3, up), (got3, up)))
    t0 = line.add(e, (keep, 0), (got, 0), (x1b, 0), (x2b, 0), (v1, 0), (v2, 0))
    for extra in perms["far"]:
        t0 = line.add(e, (t0, 0), (pperm(t0, extra), 0))
    t1 = z2(t0)
    x2_3 = s2(line.add(lo, (keep3, lo), (got3, lo), (x1_3, lo)))
    t01 = line.join(t0, t1)
    t23 = z1(t01)
    u01 = swap(t01)
    sum3 = line.add(lo, (keep3, 0), (got3, 0), (x1_3, 0), (x2_3, 0))
    y1 = z1(sum3)
    gin = grad_input(dr1, parts, wq_full, line.hold(core))
    line.mark = gin
    count = 1.0 / (seqs * groups * reps)
    mats = ((w_down, moments_down), (w_in, moments_in), (w_out, moments_out))
    done = adam_some(line.hold(spots[0]), t01, u01, mats, count)
    line.mark = done[6]
    sum3 = line.add(lo, (sum3, 0), (y1, 0))
    y2 = z2(sum3)
    t23 = line.hold(t23)
    u23 = swap(t23)
    g_down, n_down, m_down, g_in, n_in, m_in, g_out, n_out, m_out = adam_some(line.hold(spots[1]), t23, u23, mats, count, done)
    line.mark = g_out
    sum3 = line.add(lo, (sum3, 0), (y2, 0))
    for extra in perms["far"]:
        sum3 = line.add(lo, (sum3, 0), (pperm(sum3, extra), 0))
    other3 = swap(sum3)
    g_qkv, n_qkv, m_qkv, g_vec, n_vec, m_vec, g_bias, n_bias, m_bias = adam_qkv(
        line.hold(core), sum3, other3, w_qkv, moments_qkv, vec_params.T, moments_vec.transpose(0, 2, 1), bias_hidden, moments_bias, count)
    g_vec, n_vec, m_vec = g_vec.T, n_vec.T, m_vec.transpose(0, 2, 1)
    return (y.reshape(hidden_in.shape), gin.reshape(hidden_in.shape), g_qkv, g_out, g_in, g_down, g_vec, g_bias,
            n_qkv, n_out, n_in, n_down, n_vec, n_bias, m_qkv, m_out, m_in, m_down, m_vec, m_bias)


def solution(mesh):
    groups, reps = mesh.shape["group"], mesh.shape["rep"]
    tok = P(AX, None, None)
    row, mom = P("group", None), P(None, "group", None)

    def run(*args):
        return local(groups, reps, *args)

    return jax.shard_map(
        run,
        mesh=mesh,
        in_specs=(tok, tok, P(AX, None), tok, row, row, row, row, row, P("group"), mom, mom, mom, mom, mom, P(None, "group")),
        out_specs=(tok, tok, row, row, row, row, row, P("group"), row, row, row, row, row, P("group"), mom, mom, mom, mom, mom, P(None, "group")),
        check_vma=False,
    )
```
